512 devices in a mesh: row: 64 (over y, x, core), col: 8 (over z).
Axes of the slice: x: 4, y: 8, z: 8, core: 2. Of those that a mesh axis runs over, the one named last changes fastest.
Arguments:
- tokens: bfloat16 [8192, 16384], P('row', 'col'), may hold values from -6 to 6
- queries: bfloat16 [8192, 16384], P('row', 'col'), may hold values from -6 to 6
- probes: bfloat16 [8192, 16384], P('row', 'col'), may hold values from -6 to 6
- w_key: bfloat16 [16384, 1024], P('row', 'col'), may hold values from -2 to 2
- w_value: bfloat16 [16384, 1024], P('row', 'col'), may hold values from -0.046875 to 0.046875
- down_proj: bfloat16 [16384, 64], P('col'), may hold values from -0.046875 to 0.046875
- up_key: bfloat16 [64, 1024], P(None, 'col'), may hold values from -0.75 to 0.75
- up_value: bfloat16 [64, 1024], P(None, 'col'), may hold values from -0.75 to 0.75
- lengths: int32 [64, 8], P('row'), may hold values from 1 to 42, 128 in all within a row
Outputs:
- grad_down: float32 [16384, 64], P('col')
- grad_up_key: float32 [64, 1024], P(None, 'col')
- grad_up_value: float32 [64, 1024], P(None, 'col')
The draws below stay inside these ranges and needn't reach their ends.
Inputs may be any that keep to these rules, and one draw needn't show every extreme that they name: Each row holds the lengths of 8 documents that fill one block of 128 tokens exactly; the longest is 42 tokens.
All inputs are finite; a program needn't handle non-finite values.
Results may differ from the reference program's by a relative error of at most 0.019.
Values may be sent and summed in bfloat16 or wider, within the bound.
No kernel may reach another device: no remote copies, remote signals or barrier semaphores. Data moves between devices by JAX's collectives and lax.ppermute only.
A program may use at most 64 MiB of HBM per device.

```python
import math
import jax
import jax.numpy as jnp
import numpy as np
from jax import lax

D = 16384
HD = 128
QPK = 16
RANK = 64
DOCS = 8
TOK_ROW = 128
MOST = 42
KVH = 8
H = 128
KW = 1024
TOKENS = 8192
N_ROW = 64


def draw_tokens(key, part):
    own_key = jax.random.fold_in(key, 1)
    drawn = jnp.clip(jax.random.normal(own_key, (TOKENS, D), jnp.float32), -6.0, 6.0)
    return drawn.astype(jnp.bfloat16)


def draw_queries(key, part):
    own_key = jax.random.fold_in(key, 2)
    drawn = jnp.clip(jax.random.normal(own_key, (TOKENS, H * HD), jnp.float32), -6.0, 6.0)
    return drawn.astype(jnp.bfloat16)


def draw_w_key(key, part):
    own_key = jax.random.fold_in(key, 3)
    drawn = jnp.clip(jax.random.normal(own_key, (D, KW), jnp.float32), -6.0, 6.0) * D ** (-0.5)
    return drawn.astype(jnp.bfloat16)


def level_of(stream_key, extent, pieces, smallest, high):
    gain = 1.0
    for dim, parts in pieces:
        draws = jax.random.uniform(jax.random.fold_in(jax.random.fold_in(stream_key, 6), dim), (parts,), jnp.float32, smallest / len(pieces), high / len(pieces))
        gain = gain * jnp.repeat(jnp.exp(draws), extent[dim] // parts).reshape((-1,) + (1,) * (len(extent) - 1 - dim))
    return gain


def profile(amount, total, most, slope):
    portions = [(1 << 20) // math.isqrt(grade ** slope) + 1 for grade in range(2, amount + 1)]
    rest, holding = total - most - (amount - 1), [1] * (amount - 1)
    while rest > 0:
        free = [i for i in range(amount - 1) if holding[i] < most]
        whole, left = sum([portions[i] for i in free]), rest
        for i in free:
            more = min(most - holding[i], max(1, left * portions[i] // whole), rest)
            holding[i] = holding[i] + more
            rest = rest - more
    return np.array([most] + holding)


def ragged_sizes(key, count, total, reach, lean):
    if count == 2:
        one = jax.random.randint(key, (), max(1, total - reach), min(reach, total - 1) + 1)
        return jnp.stack([one, total - one])
    sizes = jnp.asarray(profile(count, total, reach, lean), jnp.int32)
    couples = (count - 1) // 2
    source_of, sink = sizes[1:1 + 2 * couples:2], sizes[2:2 + 2 * couples:2]
    room = jnp.minimum(source_of - 1, reach - sink)
    shifted = jax.random.randint(jax.random.fold_in(key, 1), (couples,), 0, 1 << 20) % (room + 1)
    sizes = sizes.at[1:1 + 2 * couples:2].set(source_of - shifted).at[2:2 + 2 * couples:2].set(sink + shifted)
    return sizes[jax.random.permutation(jax.random.fold_in(key, 2), count)]


def gaussian(stream_key, extent, scale, most, shards=(), kind=jnp.bfloat16):
    factor_of = level_of(stream_key, extent, shards, -0.22, 0.18) if shards else 1.0
    result = jax.random.normal(stream_key, extent, jnp.float32) * scale * factor_of
    return jnp.minimum(jnp.maximum(result, -most), most).astype(kind)


def setup_inputs(seed: int = 0) -> dict:
    arg_keys = jax.random.split(jax.random.key(seed), 10)
    return {
        "tokens": draw_tokens(jax.random.fold_in(arg_keys[9], 71), 0),
        "queries": draw_queries(jax.random.fold_in(arg_keys[9], 71), 0),
        "probes": gaussian(arg_keys[2], (TOKENS, H * HD), 1.0, 6.0, ((0, 64), (1, 8))),
        "w_key": draw_w_key(jax.random.fold_in(arg_keys[9], 71), 0),
        "w_value": gaussian(arg_keys[4], (D, KW), D ** -0.5, 0.046875, ((0, 64), (1, 8))),
        "down_proj": gaussian(arg_keys[5], (D, RANK), D ** -0.5, 0.046875, ((0, 8),)),
        "up_key": gaussian(arg_keys[6], (RANK, KW), RANK ** -0.5, 0.75, ((1, 8),)),
        "up_value": gaussian(arg_keys[7], (RANK, KW), RANK ** -0.5, 0.75, ((1, 8),)),
        "lengths": jax.vmap(lambda own: ragged_sizes(own, DOCS, TOK_ROW, MOST, 1))(jax.random.split(arg_keys[8], N_ROW)).reshape((N_ROW, DOCS)).astype(jnp.int32),
    }


npo_beta = 0.5


def rounded(values):
    return lax.optimization_barrier(values.astype(jnp.bfloat16)).astype(jnp.float32)


def segment_ids(counts, row_count):
    doc_ends = jnp.cumsum(counts).astype(jnp.int32)
    places = jnp.arange(row_count, dtype=jnp.int32)
    return jnp.sum((places[:, None] >= doc_ends[None, :]).astype(jnp.int32), axis=1)


def attention_probs(query_heads, key_heads, allowed, score_scale):
    scores = jnp.einsum("tgqd,sgd->gqts", query_heads.astype(jnp.float32), key_heads.astype(jnp.float32)) * score_scale
    scores = jnp.where(allowed, scores, -1e30)
    row_peak = jnp.max(scores, axis=-1, keepdims=True)
    row_exp = jnp.exp(scores - row_peak)
    return row_exp / jnp.sum(row_exp, axis=-1, keepdims=True)


def block_grads(block_items):
    query_heads, probe_heads, key_ref, value_ref, key_pol, value_pol, counts = block_items
    row_count = query_heads.shape[0]
    doc_of = segment_ids(counts, row_count)
    places = jnp.arange(row_count, dtype=jnp.int32)
    allowed = (doc_of[:, None] == doc_of[None, :]) & (places[:, None] >= places[None, :])
    score_scale = HD ** -0.5
    probe_scale = (H * HD) ** -0.5
    probs_ref = attention_probs(query_heads, key_ref, allowed, score_scale)
    probs_pol = attention_probs(query_heads, key_pol, allowed, score_scale)
    out_ref = jnp.einsum("gqts,sgd->tgqd", rounded(probs_ref), value_ref.astype(jnp.float32))
    out_pol = jnp.einsum("gqts,sgd->tgqd", rounded(probs_pol), value_pol.astype(jnp.float32))
    gap_part = jnp.sum((out_pol - out_ref) * probe_heads.astype(jnp.float32), axis=(1, 2, 3)) * probe_scale
    member = (doc_of[:, None] == jnp.arange(DOCS, dtype=jnp.int32)[None, :]).astype(jnp.float32)
    doc_gap = jnp.sum(member * gap_part[:, None], axis=0)
    token_gap = jnp.sum(member * doc_gap[None, :], axis=1)
    weight = 2.0 * jax.nn.sigmoid(npo_beta * token_gap)
    grad_out = (weight[:, None, None, None] * probe_scale * probe_heads.astype(jnp.float32)).astype(jnp.bfloat16)
    grad_value = jnp.einsum("gqts,tgqd->sgd", rounded(probs_pol), grad_out.astype(jnp.float32)).astype(jnp.bfloat16)
    grad_probs = jnp.einsum("tgqd,sgd->gqts", grad_out.astype(jnp.float32), value_pol.astype(jnp.float32))
    grad_scores = (probs_pol * (grad_probs - jnp.sum(probs_pol * grad_probs, axis=-1, keepdims=True)) * score_scale).astype(jnp.bfloat16)
    grad_key = jnp.einsum("gqts,tgqd->sgd", grad_scores.astype(jnp.float32), query_heads.astype(jnp.float32)).astype(jnp.bfloat16)
    return grad_key, grad_value


def reference(tokens, queries, probes, w_key, w_value, down_proj, up_key, up_value, lengths):
    key_full = jnp.dot(tokens, w_key, preferred_element_type=jnp.float32)
    value_full = jnp.dot(tokens, w_value, preferred_element_type=jnp.float32)
    low_half = jnp.dot(tokens, down_proj, preferred_element_type=jnp.float32).astype(jnp.bfloat16)
    key_ref = key_full.astype(jnp.bfloat16)
    value_ref = value_full.astype(jnp.bfloat16)
    key_pol = (key_full + jnp.dot(low_half, up_key, preferred_element_type=jnp.float32)).astype(jnp.bfloat16)
    value_pol = (value_full + jnp.dot(low_half, up_value, preferred_element_type=jnp.float32)).astype(jnp.bfloat16)
    block_items = (
        queries.reshape(N_ROW, TOK_ROW, KVH, QPK, HD),
        probes.reshape(N_ROW, TOK_ROW, KVH, QPK, HD),
        key_ref.reshape(N_ROW, TOK_ROW, KVH, HD),
        value_ref.reshape(N_ROW, TOK_ROW, KVH, HD),
        key_pol.reshape(N_ROW, TOK_ROW, KVH, HD),
        value_pol.reshape(N_ROW, TOK_ROW, KVH, HD),
        lengths,
    )
    grad_key, grad_value = lax.map(block_grads, block_items)
    grad_key = grad_key.reshape(TOKENS, KW)
    grad_value = grad_value.reshape(TOKENS, KW)
    grad_up_key = jnp.dot(low_half.T, grad_key, preferred_element_type=jnp.float32)
    grad_up_value = jnp.dot(low_half.T, grad_value, preferred_element_type=jnp.float32)
    back_sum = jnp.dot(grad_key, up_key.T, preferred_element_type=jnp.float32) + jnp.dot(grad_value, up_value.T, preferred_element_type=jnp.float32)
    back_half = back_sum.astype(jnp.bfloat16)
    grad_down = jnp.dot(tokens.T, back_half, preferred_element_type=jnp.float32)
    return grad_down, grad_up_key, grad_up_value
```

```python
import functools
import jax
import jax.numpy as jnp
from jax import lax
from jax.experimental import pallas as pl
from jax.experimental.pallas import tpu as pltpu
from jax.sharding import PartitionSpec as P

HD = 128
QPK = 16
BF = jnp.bfloat16
F32 = jnp.float32
npo_beta = 0.5

VMEM = pl.BlockSpec(memory_space=pltpu.VMEM)
SMEM = pl.BlockSpec(memory_space=pltpu.SMEM)
HBM = pl.BlockSpec(memory_space=pl.ANY)
PARAMS = pltpu.CompilerParams(vmem_limit_bytes=48 * 1024 * 1024)

NT = (((1,), (1,)), ((), ()))
TN = (((0,), (0,)), ((), ()))
NN = (((1,), (0,)), ((), ()))


def mm(a, b, dims):
    return lax.dot_general(a, b, dims, preferred_element_type=F32)


def fold(a):
    half = a.shape[0] // 2
    return jnp.concatenate([a[:half], a[half:]], axis=1)


def unfold(a):
    half = a.shape[1] // 2
    return jnp.concatenate([a[:, :half], a[:, half:]], axis=0)


def doc_ids(lengths_ref, axis, count, docs):
    places = lax.broadcasted_iota(jnp.int32, (count, count), axis)
    ids = jnp.zeros((count, count), jnp.int32)
    end = 0
    for j in range(docs):
        end = end + lengths_ref[0, j]
        ids = ids + jnp.where(places >= end, 1, 0)
    return ids


def split_kernel(pos_ref, t_ref, mine_ref, theirs_ref):
    pieces = t_ref.shape[1] // 512
    for core in range(2):

        @pl.when(pos_ref[0] == core)
        def _():
            for i in range(pieces):
                to = pl.ds(i * 256, 256)
                mine_ref[:, to] = t_ref[:, pl.ds(i * 512 + core * 256, 256)]
                theirs_ref[:, to] = t_ref[:, pl.ds(i * 512 + (1 - core) * 256, 256)]


def low_kernel(t_ref, down_ref, out_ref):
    low = fold(mm(t_ref[...], down_ref[...], NN)).astype(BF)
    for i in range(out_ref.shape[0]):
        out_ref[i] = low


def project_kernel(pos_ref, t_ref, *refs):
    w_refs, (own_ref, other_ref, t_scr, w_scr, t_sem, w_sem) = refs[:9], refs[9:]
    y = pos_ref[1]
    n = t_scr.shape[0]
    half = w_scr.shape[1] // 2
    copies = []
    for e in range(n):
        k = lax.rem(y + e, n)
        mine = [pltpu.make_async_copy(t_ref.at[k], t_scr.at[e], t_sem.at[e])]
        if e == 4:
            for i in range(2):
                mine.append(
                    pltpu.make_async_copy(
                        w_refs[4 + 4 * i], w_scr.at[e, pl.ds(i * half, half)], w_sem.at[e + 4 * i]
                    )
                )
        else:
            mine.append(pltpu.make_async_copy(w_refs[e], w_scr.at[e], w_sem.at[e]))
        for c in mine:
            c.start()
        copies.append(mine)
    total = jnp.zeros((t_scr.shape[1], w_scr.shape[2]), F32)
    for e in range(n):
        for c in copies[e]:
            c.wait()
        total = total + mm(t_scr[e], w_scr[e], NN)
    rows = own_ref.shape[0]
    own_ref[...] = total[:rows]
    other_ref[...] = total[rows:]


def attend_kernel(
    lengths_ref, own_ref, got_ref, low_ref, upk_ref, upv_ref, q_ref, p_ref,
    pack_ref, low_half_ref, gk_ref, gv_ref,
):
    rows = own_ref.shape[0]
    heads = q_ref.shape[1] // HD
    score_scale = HD ** (-0.5)
    probe_scale = (q_ref.shape[1] * pack_ref.shape[0]) ** (-0.5)
    low_sum = low_ref[0].astype(F32)
    for i in range(1, low_ref.shape[0]):
        low_sum = low_sum + low_ref[i].astype(F32)
    low_half = unfold(low_sum).astype(BF)
    low_half_ref[...] = low_half
    full = own_ref[...] + got_ref[...]
    key_full, value_full = full[:, :HD], full[:, HD:]
    key_pol = (key_full + mm(low_half, upk_ref[...], NN)).astype(BF)
    value_pol = (value_full + mm(low_half, upv_ref[...], NN)).astype(BF)
    keys = jnp.concatenate([key_pol, key_full.astype(BF)], axis=0)
    values = jnp.concatenate([value_pol, value_full.astype(BF)], axis=0)
    doc_s = doc_ids(lengths_ref, 0, rows, lengths_ref.shape[1])
    doc_t = doc_ids(lengths_ref, 1, rows, lengths_ref.shape[1])
    s_at = lax.broadcasted_iota(jnp.int32, (rows, rows), 0)
    t_at = lax.broadcasted_iota(jnp.int32, (rows, rows), 1)
    allowed = (doc_s == doc_t) & (t_at >= s_at)

    def probs_of(scores):
        scores = jnp.where(allowed, scores * score_scale, -1e30)
        peak = jnp.max(scores, axis=0, keepdims=True)
        e = jnp.exp(scores - peak)
        return e / jnp.sum(e, axis=0, keepdims=True)

    gk = jnp.zeros((rows, HD), F32)
    gv = jnp.zeros((rows, HD), F32)
    gap = jnp.zeros((1, rows), F32)
    for h in range(heads):
        q = q_ref[:, pl.ds(h * HD, HD)]
        probe = p_ref[:, pl.ds(h * HD, HD)]
        scores = mm(keys, q, NT)
        grads = mm(values, probe, NT)
        pol = probs_of(scores[:rows])
        ref = probs_of(scores[rows:])
        grad_pol = grads[:rows]
        mean_pol = jnp.sum(pol * grad_pol, axis=0, keepdims=True)
        mean_ref = jnp.sum(ref * grads[rows:], axis=0, keepdims=True)
        gap = gap + (mean_pol - mean_ref)
        grad_scores = (pol * (grad_pol - mean_pol)).astype(BF)
        gk = gk + mm(grad_scores, q, NN)
        gv = gv + mm(pol.astype(BF), probe, NN)
    gk = gk * (score_scale * probe_scale)
    gv = gv * probe_scale
    gap = gap * probe_scale
    gk_ref[...] = gk
    gv_ref[...] = gv
    back = mm(gk.astype(BF), upk_ref[...], NT) + mm(gv.astype(BF), upv_ref[...], NT)
    back = fold(back).astype(BF)
    first = gap.astype(BF).astype(F32)
    second = (gap - first).astype(BF).astype(F32)
    third = gap - first - second
    line = lax.broadcasted_iota(jnp.int32, (16, rows), 0)
    tail = jnp.where(line == 0, first, jnp.where(line == 1, second, jnp.where(line == 2, third, 0.0)))
    tail = tail.astype(BF)
    for i in range(pack_ref.shape[0]):
        pack_ref[i, pl.ds(0, 64)] = back
        pack_ref[i, pl.ds(64, 16)] = tail


def weigh_kernel(lengths_ref, pack_ref, low_half_ref, gk_ref, gv_ref, t_ref, out_ref):
    rows = gk_ref.shape[0]
    total = pack_ref[0].astype(F32)
    for i in range(1, pack_ref.shape[0]):
        total = total + pack_ref[i].astype(F32)
    gap = total[64:65] + total[65:66] + total[66:67]
    docs = lengths_ref.shape[1]
    same = doc_ids(lengths_ref, 0, rows, docs) == doc_ids(lengths_ref, 1, rows, docs)
    token_gap = jnp.sum(jnp.where(same, gap, 0.0), axis=1, keepdims=True)
    weight = 2.0 * jax.nn.sigmoid(npo_beta * token_gap)
    back_half = (unfold(total[:64]) * weight).astype(BF)
    down = mm(back_half, t_ref[...], TN).astype(BF)
    both = jnp.concatenate([gk_ref[...] * weight, gv_ref[...] * weight], axis=1).astype(BF)
    up = mm(low_half_ref[...], both, TN).astype(BF)
    groups = 4
    for i in range(16):
        for g in range(groups):
            out_ref[i * groups + g, pl.ds(0, 16)] = down[g * 16:(g + 1) * 16, i * 128:(i + 1) * 128]
    for s in range(64):
        tile, at = s // 8, (s % 8) * 2
        i, g = tile // groups, tile % groups
        piece = up[g * 16 + at:g * 16 + at + 2, i * 128:(i + 1) * 128].astype(F32)
        piece = jnp.concatenate([piece, jnp.zeros((6, 128), F32)], axis=0)
        out_ref[s, pl.ds(16, 8)] = piece.astype(BF)


def sum_kernel(in_ref, out_ref):
    total = in_ref[0].astype(F32)
    for i in range(1, in_ref.shape[0]):
        total = total + in_ref[i].astype(F32)
    total = total.astype(BF)
    for i in range(out_ref.shape[0]):
        out_ref[i] = total


def place_kernel(in_ref, down_ref, upk_ref, upv_ref):
    groups = 4
    for i in range(16):
        tile = jnp.concatenate(
            [in_ref[i * groups + g, pl.ds(0, 16)].astype(F32) for g in range(groups)], axis=0
        )
        down_ref[pl.ds(i * 128, 128)] = tile.T
    for s in range(64):
        tile, at = s // 8, (s % 8) * 2
        i, g = tile // groups, tile % groups
        to = upk_ref if i == 0 else upv_ref
        to[pl.ds(g * 16 + at, 2)] = in_ref[s, pl.ds(16, 8)].astype(F32)[:2]


def call(kernel, outs, in_specs, out_specs, *args, scratch=()):
    return pl.pallas_call(
        kernel,
        out_shape=[jax.ShapeDtypeStruct(s, d) for s, d in outs],
        in_specs=in_specs,
        out_specs=out_specs,
        scratch_shapes=list(scratch),
        compiler_params=PARAMS,
    )(*args)


def on_device(tokens, queries, probes, w_key, w_value, down_proj, up_key, up_value, lengths):
    rows, feats = tokens.shape
    row_at = lax.axis_index("row")
    pos = jnp.stack([row_at % 2, row_at // 8]).astype(jnp.int32)

    def place(y, x, core):
        return ((y % 8) * 4 + x % 4) * 2 + core % 2

    sites = [(y, x, core) for y in range(8) for x in range(4) for core in range(2)]
    swap = [(place(y, x, c), place(y, x, 1 - c)) for y, x, c in sites]
    fore = [(place(y, x, c), place(y + 1, x, c)) for y, x, c in sites]
    aft = [(place(y, x, c), place(y - 1, x, c)) for y, x, c in sites]
    x_lines = [[place(y, x, c) for x in range(4)] for y in range(8) for c in range(2)]

    half = (rows, feats // 2)
    mine, theirs = call(
        split_kernel, [(half, BF), (half, BF)], [SMEM, VMEM], [VMEM, VMEM], pos, tokens
    )
    swapped = lax.ppermute(theirs, "row", swap)
    pair = jnp.concatenate([mine, swapped], axis=0)
    all_tokens = lax.all_gather(pair, "col", axis=0)

    w_both = jnp.concatenate([w_key, w_value], axis=1)
    w_line = lax.all_to_all(
        jnp.broadcast_to(w_both, (4,) + w_both.shape), "row", 0, 0, axis_index_groups=x_lines
    )
    w_own = w_line.reshape(4 * w_both.shape[0], w_both.shape[1])
    up_going, down_going = [w_own], [w_own]
    for _ in range(3):
        up_going.append(lax.ppermute(up_going[-1], "row", fore))
        down_going.append(lax.ppermute(down_going[-1], "row", aft))
    middle = w_own.shape[0] // 2
    last_up = lax.ppermute(up_going[3][:middle], "row", fore)
    last_down = lax.ppermute(down_going[3][middle:], "row", aft)
    w_parts = [
        w_own, down_going[1], down_going[2], down_going[3], last_up,
        up_going[3], up_going[2], up_going[1], last_down,
    ]

    (low_pack,) = call(
        low_kernel, [((8, rows // 2, 128), BF)], [VMEM, VMEM], [VMEM], tokens, down_proj
    )
    low_parts = lax.all_to_all(low_pack, "col", 0, 0)

    wide = w_both.shape[1]
    own, other = call(
        project_kernel,
        [((rows, wide), F32)] * 2,
        [SMEM] + [HBM] * 10,
        [VMEM, VMEM],
        pos, all_tokens, *w_parts,
        scratch=[
            pltpu.VMEM((8, 2 * rows, feats // 2), BF),
            pltpu.VMEM((8, feats // 2, wide), BF),
            pltpu.SemaphoreType.DMA((8,)),
            pltpu.SemaphoreType.DMA((9,)),
        ],
    )
    got = lax.ppermute(other, "row", swap)
    pack, low_half, gk, gv = call(
        attend_kernel,
        [((8, 80, 128), BF), ((rows, 64), BF), ((rows, HD), F32), ((rows, HD), F32)],
        [SMEM] + [VMEM] * 7,
        [VMEM] * 4,
        lengths, own, got, low_parts, up_key, up_value, queries, probes,
    )
    packs = lax.all_to_all(pack, "col", 0, 0)
    (terms,) = call(
        weigh_kernel, [((64, 24, 128), BF)], [SMEM] + [VMEM] * 5, [VMEM],
        lengths, packs, low_half, gk, gv, tokens,
    )
    term_parts = lax.all_to_all(terms, "row", 0, 0)
    (summed,) = call(sum_kernel, [((64, 24, 128), BF)], [VMEM], [VMEM], term_parts)
    pieces = lax.all_to_all(summed, "row", 0, 0)
    return tuple(
        call(
            place_kernel,
            [((feats, 64), F32), ((64, HD), F32), ((64, HD), F32)],
            [VMEM], [VMEM] * 3, pieces,
        )
    )


def solution(mesh):
    in_specs = (
        P("row", "col"),
        P("row", "col"),
        P("row", "col"),
        P("row", "col"),
        P("row", "col"),
        P("col", None),
        P(None, "col"),
        P(None, "col"),
        P("row", None),
    )
    out_specs = (P("col", None), P(None, "col"), P(None, "col"))
    return jax.shard_map(
        on_device, mesh=mesh, in_specs=in_specs, out_specs=out_specs, check_vma=False
    )
```

```python
import functools
import jax
import jax.numpy as jnp
from jax import lax
from jax.experimental import pallas as pl
from jax.experimental.pallas import tpu as pltpu
from jax.sharding import PartitionSpec as P

HD = 128
QPK = 16
BF = jnp.bfloat16
F32 = jnp.float32
npo_beta = 0.5

VMEM = pl.BlockSpec(memory_space=pltpu.VMEM)
SMEM = pl.BlockSpec(memory_space=pltpu.SMEM)
HBM = pl.BlockSpec(memory_space=pltpu.HBM)

NT = (((1,), (1,)), ((), ()))
TN = (((0,), (0,)), ((), ()))
NN = (((1,), (0,)), ((), ()))


def mm(a, b, dims):
    return lax.dot_general(a, b, dims, preferred_element_type=F32)


def fold(a):
    half = a.shape[0] // 2
    return jnp.concatenate([a[:half], a[half:]], axis=1)


def unfold(a):
    half = a.shape[1] // 2
    return jnp.concatenate([a[:, :half], a[:, half:]], axis=0)


def doc_ids(lengths_ref, axis, count, docs):
    places = lax.broadcasted_iota(jnp.int32, (count, count), axis)
    ids = jnp.zeros((count, count), jnp.int32)
    end = 0
    for j in range(docs):
        end = end + lengths_ref[0, j]
        ids = ids + jnp.where(places >= end, 1, 0)
    return ids


def split_kernel(pos_ref, t_ref, mine_ref, theirs_ref, sem):
    copies = []
    for i in range(t_ref.shape[1] // 512):
        to = pl.ds(i * 256, 256)
        for k, ref in enumerate((mine_ref, theirs_ref)):
            core = lax.rem(pos_ref[0] + k, 2)
            at = pl.ds(pl.multiple_of(i * 512 + core * 256, 256), 256)
            copies.append(pltpu.make_async_copy(t_ref.at[:, at], ref.at[:, to], sem.at[2 * i + k]))
    for c in copies:
        c.start()
    for c in copies:
        c.wait()


def low_kernel(t_ref, down_ref, out_ref):
    low = fold(mm(t_ref[...], down_ref[...], NT)).astype(BF)
    for i in range(out_ref.shape[0]):
        out_ref[i] = low


def project_kernel(pos_ref, t_ref, *refs):
    w_refs, (own_ref, other_ref, t_scr, w_scr, sem) = refs[:16], refs[16:]
    n = t_scr.shape[0]
    half = w_refs[0].shape[0]
    copies = []
    for j in range(n):
        k = lax.rem(pos_ref[1] + j * (2 * pos_ref[0] - 1) + n, n)
        copies.append(
            [pltpu.make_async_copy(t_ref.at[k], t_scr.at[j], sem.at[3 * j])]
            + [
                pltpu.make_async_copy(
                    w_refs[8 * i + j], w_scr.at[j, pl.ds(i * half, half)], sem.at[3 * j + 1 + i]
                )
                for i in range(2)
            ]
        )
        for c in copies[j]:
            c.start()
    total = jnp.zeros((t_scr.shape[1], w_scr.shape[2]), F32)
    for j in range(n):
        for c in copies[j]:
            c.wait()
        total = total + mm(t_scr[j], w_scr[j], NN)
    rows = own_ref.shape[0]
    own_ref[...] = total[:rows]
    other_ref[...] = total[rows:]


def attend_kernel(
    lengths_ref, own_ref, got_ref, low_ref, upk_ref, upv_ref, q_ref, p_ref,
    pack_ref, low_half_ref, gk_ref, gv_ref, q_scr, p_scr, sem,
):
    rows = own_ref.shape[0]
    heads = q_ref.shape[1] // HD
    batch = 4
    copies = []
    for i in range(heads // batch):
        at = pl.ds(i * batch * HD, batch * HD)
        for k, (ref, scr) in enumerate(((q_ref, q_scr), (p_ref, p_scr))):
            copies.append(pltpu.make_async_copy(ref.at[:, at], scr.at[:, at], sem.at[2 * i + k]))
    for c in copies:
        c.start()
    score_scale = HD ** (-0.5)
    probe_scale = (q_ref.shape[1] * pack_ref.shape[0]) ** (-0.5)
    low_sum = low_ref[0].astype(F32)
    for i in range(1, low_ref.shape[0]):
        low_sum = low_sum + low_ref[i].astype(F32)
    low_half = unfold(low_sum).astype(BF)
    low_half_ref[...] = low_half
    full = own_ref[...] + got_ref[...]
    key_full, value_full = full[:, :HD], full[:, HD:]
    key_pol = (key_full + mm(low_half, upk_ref[...], NN)).astype(BF)
    value_pol = (value_full + mm(low_half, upv_ref[...], NN)).astype(BF)
    keys = jnp.concatenate([key_pol, key_full.astype(BF)], axis=0)
    values = jnp.concatenate([value_pol, value_full.astype(BF)], axis=0)
    doc_s = doc_ids(lengths_ref, 0, rows, lengths_ref.shape[1])
    doc_t = doc_ids(lengths_ref, 1, rows, lengths_ref.shape[1])
    s_at = lax.broadcasted_iota(jnp.int32, (rows, rows), 0)
    t_at = lax.broadcasted_iota(jnp.int32, (rows, rows), 1)
    allowed = (doc_s == doc_t) & (t_at >= s_at)

    def probs_of(scores):
        scores = jnp.where(allowed, scores * score_scale, -1e30)
        peak = jnp.max(scores, axis=0, keepdims=True)
        e = jnp.exp(scores - peak)
        return e / jnp.sum(e, axis=0, keepdims=True)

    gk = jnp.zeros((rows, HD), F32)
    gv = jnp.zeros((rows, HD), F32)
    gap = jnp.zeros((1, rows), F32)
    for h in range(heads):
        if h % batch == 0:
            for c in copies[2 * h // batch:2 * h // batch + 2]:
                c.wait()
        q = q_scr[:, pl.ds(h * HD, HD)]
        probe = p_scr[:, pl.ds(h * HD, HD)]
        scores = mm(keys, q, NT)
        grads = mm(values, probe, NT)
        pol = probs_of(scores[:rows])
        ref = probs_of(scores[rows:])
        grad_pol = grads[:rows]
        mean_pol = jnp.sum(pol * grad_pol, axis=0, keepdims=True)
        mean_ref = jnp.sum(ref * grads[rows:], axis=0, keepdims=True)
        gap = gap + (mean_pol - mean_ref)
        grad_scores = (pol * (grad_pol - mean_pol)).astype(BF)
        gk = gk + mm(grad_scores, q, NN)
        gv = gv + mm(pol.astype(BF), probe, NN)
    gk = gk * (score_scale * probe_scale)
    gv = gv * probe_scale
    gap = gap * probe_scale
    gk_ref[...] = gk
    gv_ref[...] = gv
    back = mm(gk.astype(BF), upk_ref[...], NT) + mm(gv.astype(BF), upv_ref[...], NT)
    back = fold(back).astype(BF)
    first = gap.astype(BF).astype(F32)
    second = (gap - first).astype(BF).astype(F32)
    third = gap - first - second
    line = lax.broadcasted_iota(jnp.int32, (16, rows), 0)
    tail = jnp.where(line == 0, first, jnp.where(line == 1, second, jnp.where(line == 2, third, 0.0)))
    tail = tail.astype(BF)
    for i in range(pack_ref.shape[0]):
        pack_ref[i, pl.ds(0, 64)] = back
        pack_ref[i, pl.ds(64, 16)] = tail


def weigh_kernel(lengths_ref, pack_ref, low_half_ref, gk_ref, gv_ref, t_ref, out_ref):
    rows = gk_ref.shape[0]
    total = pack_ref[0].astype(F32)
    for i in range(1, pack_ref.shape[0]):
        total = total + pack_ref[i].astype(F32)
    gap = total[64:65] + total[65:66] + total[66:67]
    docs = lengths_ref.shape[1]
    same = doc_ids(lengths_ref, 0, rows, docs) == doc_ids(lengths_ref, 1, rows, docs)
    token_gap = jnp.sum(jnp.where(same, gap, 0.0), axis=1, keepdims=True)
    weight = 2.0 * jax.nn.sigmoid(npo_beta * token_gap)
    back_half = (unfold(total[:64]) * weight).astype(BF)
    down = mm(back_half, t_ref[...], TN).astype(BF)
    both = jnp.concatenate([gk_ref[...] * weight, gv_ref[...] * weight], axis=1).astype(BF)
    up = mm(low_half_ref[...], both, TN).astype(BF)
    slots = out_ref.shape[0]
    wide, deep = t_ref.shape[1] // slots, up.shape[0] // slots
    for j in range(slots):
        out_ref[j, pl.ds(0, 64)] = down[:, j * wide:(j + 1) * wide]
        out_ref[j, pl.ds(64, deep)] = up[j * deep:(j + 1) * deep]


def sum_kernel(in_ref, out_ref):
    total = in_ref[0].astype(F32)
    for i in range(1, in_ref.shape[0]):
        total = total + in_ref[i].astype(F32)
    total = total.astype(BF)
    for i in range(out_ref.shape[0]):
        out_ref[i] = total


def place_kernel(in_ref, down_ref, upk_ref, upv_ref):
    slots, _, wide = in_ref.shape
    deep = upk_ref.shape[0] // slots
    for j in range(slots):
        down_ref[:, pl.ds(j * wide, wide)] = in_ref[j, pl.ds(0, 64)].astype(F32)
        up = in_ref[j, pl.ds(64, deep)].astype(F32)
        upk_ref[pl.ds(j * deep, deep)] = up[:, :HD]
        upv_ref[pl.ds(j * deep, deep)] = up[:, HD:]


def call(kernel, outs, in_specs, out_specs, *args, scratch=(), mib=8):
    return pl.pallas_call(
        kernel,
        out_shape=[jax.ShapeDtypeStruct(s, d) for s, d in outs],
        in_specs=in_specs,
        out_specs=out_specs,
        scratch_shapes=list(scratch),
        compiler_params=pltpu.CompilerParams(vmem_limit_bytes=mib * 1024 * 1024),
    )(*args)


def on_device(tokens, queries, probes, w_key, w_value, down_proj, up_key, up_value, lengths):
    rows, feats = tokens.shape
    row_at = lax.axis_index("row")
    pos = jnp.stack([row_at % 2, row_at // 8]).astype(jnp.int32)

    def place(y, x, core):
        return ((y % 8) * 4 + x % 4) * 2 + core % 2

    sites = [(y, x, core) for y in range(8) for x in range(4) for core in range(2)]
    swap = [(place(y, x, c), place(y, x, 1 - c)) for y, x, c in sites]
    orbit = [(place(y, x, c), place(y + 1 - 2 * c, x, c)) for y, x, c in sites]
    y_lines = [[place(y, x, c) for y in range(8)] for x in range(4) for c in range(2)]
    squares = [[place(y, x, c) for x in range(4) for c in range(2)] for y in range(8)]
    x_lines = [[place(y, x, c) for x in range(4)] for y in range(8) for c in range(2)]

    half = (rows, feats // 2)
    mine, theirs = call(
        split_kernel, [(half, BF), (half, BF)], [SMEM, HBM], [VMEM, VMEM], pos, tokens,
        scratch=[pltpu.SemaphoreType.DMA((feats // 256,))],
    )
    swapped = lax.ppermute(theirs, "row", swap)
    pair = jnp.concatenate([mine, swapped], axis=0)
    all_tokens = lax.all_gather(pair, "col", axis=0)

    w_both = jnp.concatenate([w_key, w_value], axis=1)
    wide = w_both.shape[1]
    w_line = lax.all_to_all(
        jnp.broadcast_to(w_both, (4,) + w_both.shape), "row", 0, 0, axis_index_groups=x_lines
    )
    w_parts = []
    for i in range(2):
        w_chain = w_line[2 * i:2 * i + 2].reshape(feats // 4, wide)
        w_parts.append(w_chain)
        for _ in range(7):
            w_chain = lax.ppermute(w_chain, "row", orbit)
            w_parts.append(w_chain)

    (low_pack,) = call(
        low_kernel, [((8, rows // 2, 128), BF)], [VMEM, VMEM], [VMEM], tokens, down_proj.T
    )
    low_parts = lax.all_to_all(low_pack, "col", 0, 0)

    own, other = call(
        project_kernel,
        [((rows, wide), F32)] * 2,
        [SMEM] + [HBM] * 17,
        [VMEM, VMEM],
        pos, all_tokens, *w_parts,
        scratch=[
            pltpu.VMEM((8, 2 * rows, feats // 2), BF),
            pltpu.VMEM((8, feats // 2, wide), BF),
            pltpu.SemaphoreType.DMA((24,)),
        ],
        mib=56,
    )
    got = lax.ppermute(other, "row", swap)
    pack, low_half, gk, gv = call(
        attend_kernel,
        [((8, 80, 128), BF), ((rows, 64), BF), ((rows, HD), F32), ((rows, HD), F32)],
        [SMEM] + [VMEM] * 5 + [HBM] * 2,
        [VMEM] * 4,
        lengths, own, got, low_parts, up_key, up_value, queries, probes,
        scratch=[
            pltpu.VMEM((rows, feats), BF),
            pltpu.VMEM((rows, feats), BF),
            pltpu.SemaphoreType.DMA((8,)),
        ],
    )
    packs = lax.all_to_all(pack, "col", 0, 0)
    slot = (8, 64 + 8, 2 * HD)
    (terms,) = call(
        weigh_kernel, [(slot, BF)], [SMEM] + [VMEM] * 5, [VMEM],
        lengths, packs, low_half, gk, gv, tokens,
    )
    term_parts = lax.all_to_all(terms, "row", 0, 0, axis_index_groups=squares)
    (square,) = call(sum_kernel, [(slot, BF)], [VMEM], [VMEM], term_parts)
    square_parts = lax.all_to_all(square, "row", 0, 0, axis_index_groups=y_lines)
    (summed,) = call(sum_kernel, [(slot, BF)], [VMEM], [VMEM], square_parts)
    pieces = lax.all_to_all(summed, "row", 0, 0, axis_index_groups=squares)
    grad_down, grad_up_key, grad_up_value = call(
        place_kernel,
        [((64, feats), F32), ((64, HD), F32), ((64, HD), F32)],
        [VMEM], [VMEM] * 3, pieces,
    )
    return grad_down.T, grad_up_key, grad_up_value


def solution(mesh):
    in_specs = (
        P("row", "col"),
        P("row", "col"),
        P("row", "col"),
        P("row", "col"),
        P("row", "col"),
        P("col", None),
        P(None, "col"),
        P(None, "col"),
        P("row", None),
    )
    out_specs = (P("col", None), P(None, "col"), P(None, "col"))
    return jax.shard_map(
        on_device, mesh=mesh, in_specs=in_specs, out_specs=out_specs, check_vma=False
    )
```

```python
import functools
import jax
import jax.numpy as jnp
from jax import lax
from jax.experimental import pallas as pl
from jax.experimental.pallas import tpu as pltpu
from jax.sharding import PartitionSpec as P

HD = 128
QPK = 16
BF = jnp.bfloat16
F32 = jnp.float32
npo_beta = 0.5

VMEM = pl.BlockSpec(memory_space=pltpu.VMEM)
SMEM = pl.BlockSpec(memory_space=pltpu.SMEM)
HBM = pl.BlockSpec(memory_space=pltpu.HBM)

NT = (((1,), (1,)), ((), ()))
TN = (((0,), (0,)), ((), ()))
NN = (((1,), (0,)), ((), ()))


def mm(a, b, dims):
    return lax.dot_general(a, b, dims, preferred_element_type=F32)


def fold(a, rows):
    return jnp.concatenate([a[i:i + rows] for i in range(0, a.shape[0], rows)], axis=1)


def unfold(a, wide):
    return jnp.concatenate([a[:, i:i + wide] for i in range(0, a.shape[1], wide)], axis=0)


def doc_ids(lengths_ref, axis, count, docs):
    places = lax.broadcasted_iota(jnp.int32, (count, count), axis)
    ids = jnp.zeros((count, count), jnp.int32)
    end = 0
    for j in range(docs):
        end = end + lengths_ref[0, j]
        ids = ids + jnp.where(places >= end, 1, 0)
    return ids


def split_kernel(pos_ref, t_ref, mine_ref, theirs_ref, sem):
    copies = []
    for i in range(t_ref.shape[1] // 512):
        to = pl.ds(i * 256, 256)
        for k, ref in enumerate((mine_ref, theirs_ref)):
            core = lax.rem(pos_ref[0] + k, 2)
            at = pl.ds(pl.multiple_of(i * 512 + core * 256, 256), 256)
            copies.append(pltpu.make_async_copy(t_ref.at[:, at], ref.at[:, to], sem.at[2 * i + k]))
    for c in copies:
        c.start()
    for c in copies:
        c.wait()


def low_kernel(t_ref, down_ref, out_ref):
    low = mm(t_ref[...], down_ref[...], NT)
    rows, wide = out_ref.shape
    low = fold(low, rows // 2)
    high = low.astype(BF).astype(F32)
    out_ref[...] = jnp.concatenate([high, low - high], axis=0).astype(BF)


def project_kernel(pos_ref, t_ref, *refs):
    w_refs, (own_ref, other_ref, low_ref, t_scr, w_scr, sem) = refs[:9], refs[9:]
    n = t_scr.shape[0]
    half = w_scr.shape[1] // 2
    way = 2 * pos_ref[0] - 1
    copies = []
    for j, step in enumerate((0, 1, 2, 3, -1, -2, -3, 4)):
        k = lax.rem(pos_ref[1] + step * way + n, n)
        parts = [(t_ref.at[k], t_scr.at[j])]
        if step == 4:
            parts.append((w_refs[7], w_scr.at[j, pl.ds(0, half)]))
            parts.append((w_refs[8], w_scr.at[j, pl.ds(half, half)]))
        else:
            parts.append((w_refs[j], w_scr.at[j]))
        copies.append(
            [pltpu.make_async_copy(a, b, sem.at[3 * j + i]) for i, (a, b) in enumerate(parts)]
        )
        for c in copies[j]:
            c.start()
    rows = own_ref.shape[0]
    total = jnp.zeros((2 * rows, w_scr.shape[2]), F32)
    low = jnp.zeros((t_scr.shape[1] - 2 * rows, t_scr.shape[2]), F32)
    for j in range(n):
        for c in copies[j]:
            c.wait()
        total = total + mm(t_scr[j, pl.ds(0, 2 * rows)], w_scr[j], NN)
        low = low + t_scr[j, pl.ds(2 * rows, low.shape[0])].astype(F32)
    own_ref[...] = total[:rows]
    other_ref[...] = total[rows:]
    low = low[:low.shape[0] // 2] + low[low.shape[0] // 2:]
    low_ref[...] = unfold(low, low_ref.shape[1]).astype(BF)


def attend_kernel(
    lengths_ref, own_ref, got_ref, low_ref, upk_ref, upv_ref, q_ref, p_ref,
    pack_ref, gk_ref, gv_ref, q_scr, p_scr, sem,
):
    rows = own_ref.shape[0]
    heads = q_ref.shape[1] // HD
    batch = 4
    copies = []
    for i in range(heads // batch):
        at = pl.ds(i * batch * HD, batch * HD)
        for k, (ref, scr) in enumerate(((q_ref, q_scr), (p_ref, p_scr))):
            copies.append(pltpu.make_async_copy(ref.at[:, at], scr.at[:, at], sem.at[2 * i + k]))
    for c in copies:
        c.start()
    score_scale = HD ** (-0.5)
    probe_scale = (q_ref.shape[1] * pack_ref.shape[0]) ** (-0.5)
    low_half = low_ref[...]
    full = own_ref[...] + got_ref[...]
    key_full, value_full = full[:, :HD], full[:, HD:]
    key_pol = (key_full + mm(low_half, upk_ref[...], NN)).astype(BF)
    value_pol = (value_full + mm(low_half, upv_ref[...], NN)).astype(BF)
    keys = jnp.concatenate([key_pol, key_full.astype(BF)], axis=0)
    values = jnp.concatenate([value_pol, value_full.astype(BF)], axis=0)
    doc_s = doc_ids(lengths_ref, 0, rows, lengths_ref.shape[1])
    doc_t = doc_ids(lengths_ref, 1, rows, lengths_ref.shape[1])
    s_at = lax.broadcasted_iota(jnp.int32, (rows, rows), 0)
    t_at = lax.broadcasted_iota(jnp.int32, (rows, rows), 1)
    allowed = (doc_s == doc_t) & (t_at >= s_at)

    def probs_of(scores):
        scores = jnp.where(allowed, scores * score_scale, -1e30)
        peak = jnp.max(scores, axis=0, keepdims=True)
        e = jnp.exp(scores - peak)
        return e / jnp.sum(e, axis=0, keepdims=True)

    gk = jnp.zeros((rows, HD), F32)
    gv = jnp.zeros((rows, HD), F32)
    gap = jnp.zeros((1, rows), F32)
    for h in range(heads):
        if h % batch == 0:
            for c in copies[2 * h // batch:2 * h // batch + 2]:
                c.wait()
        q = q_scr[:, pl.ds(h * HD, HD)]
        probe = p_scr[:, pl.ds(h * HD, HD)]
        scores = mm(keys, q, NT)
        grads = mm(values, probe, NT)
        pol = probs_of(scores[:rows])
        ref = probs_of(scores[rows:])
        grad_pol = grads[:rows]
        mean_pol = jnp.sum(pol * grad_pol, axis=0, keepdims=True)
        mean_ref = jnp.sum(ref * grads[rows:], axis=0, keepdims=True)
        gap = gap + (mean_pol - mean_ref)
        grad_scores = (pol * (grad_pol - mean_pol)).astype(BF)
        gk = gk + mm(grad_scores, q, NN)
        gv = gv + mm(pol.astype(BF), probe, NN)
    gk = gk * (score_scale * probe_scale)
    gv = gv * probe_scale
    gap = gap * probe_scale
    gk_ref[...] = gk
    gv_ref[...] = gv
    back = mm(gk.astype(BF), upk_ref[...], NT) + mm(gv.astype(BF), upv_ref[...], NT)
    back = fold(back, 64).astype(BF)
    first = gap.astype(BF).astype(F32)
    second = (gap - first).astype(BF).astype(F32)
    third = gap - first - second
    line = lax.broadcasted_iota(jnp.int32, (16, rows), 0)
    tail = jnp.where(line == 0, first, jnp.where(line == 1, second, jnp.where(line == 2, third, 0.0)))
    tail = tail.astype(BF)
    for i in range(pack_ref.shape[0]):
        pack_ref[i, pl.ds(0, 64)] = back
        pack_ref[i, pl.ds(64, 16)] = tail


def weigh_kernel(lengths_ref, pack_ref, low_half_ref, gk_ref, gv_ref, t_ref, out_ref):
    rows = gk_ref.shape[0]
    total = pack_ref[0].astype(F32)
    for i in range(1, pack_ref.shape[0]):
        total = total + pack_ref[i].astype(F32)
    gap = total[64:65] + total[65:66] + total[66:67]
    docs = lengths_ref.shape[1]
    same = doc_ids(lengths_ref, 0, rows, docs) == doc_ids(lengths_ref, 1, rows, docs)
    token_gap = jnp.sum(jnp.where(same, gap, 0.0), axis=1, keepdims=True)
    weight = 2.0 * jax.nn.sigmoid(npo_beta * token_gap)
    back_half = (unfold(total[:64], 64) * weight).astype(BF)
    down = mm(back_half, t_ref[...], TN).astype(BF)
    both = jnp.concatenate([gk_ref[...] * weight, gv_ref[...] * weight], axis=1).astype(BF)
    up = mm(low_half_ref[...], both, TN).astype(BF)
    slots = out_ref.shape[0]
    wide, deep = t_ref.shape[1] // slots, up.shape[0] // slots
    for j in range(slots):
        out_ref[j, pl.ds(0, 64)] = down[:, j * wide:(j + 1) * wide]
        out_ref[j, pl.ds(64, deep)] = up[j * deep:(j + 1) * deep]


def sum_kernel(in_ref, out_ref):
    total = in_ref[0].astype(F32)
    for i in range(1, in_ref.shape[0]):
        total = total + in_ref[i].astype(F32)
    total = total.astype(BF)
    for i in range(out_ref.shape[0]):
        out_ref[i] = total


def place_kernel(in_ref, down_ref, upk_ref, upv_ref):
    slots, _, wide = in_ref.shape
    deep = upk_ref.shape[0] // slots
    for j in range(slots):
        down_ref[:, pl.ds(j * wide, wide)] = in_ref[j, pl.ds(0, 64)].astype(F32)
        up = in_ref[j, pl.ds(64, deep)].astype(F32)
        upk_ref[pl.ds(j * deep, deep)] = up[:, :HD]
        upv_ref[pl.ds(j * deep, deep)] = up[:, HD:]


def call(kernel, outs, in_specs, out_specs, *args, scratch=(), mib=8):
    return pl.pallas_call(
        kernel,
        out_shape=[jax.ShapeDtypeStruct(s, d) for s, d in outs],
        in_specs=in_specs,
        out_specs=out_specs,
        scratch_shapes=list(scratch),
        compiler_params=pltpu.CompilerParams(vmem_limit_bytes=mib * 1024 * 1024),
    )(*args)


def on_device(tokens, queries, probes, w_key, w_value, down_proj, up_key, up_value, lengths):
    rows, feats = tokens.shape
    row_at = lax.axis_index("row")
    pos = jnp.stack([row_at % 2, row_at // 8]).astype(jnp.int32)

    def place(y, x, core):
        return ((y % 8) * 4 + x % 4) * 2 + core % 2

    sites = [(y, x, core) for y in range(8) for x in range(4) for core in range(2)]
    swap = [(place(y, x, c), place(y, x, 1 - c)) for y, x, c in sites]
    fore = [(place(y, x, c), place(y + 1 - 2 * c, x, c)) for y, x, c in sites]
    aft = [(b, a) for a, b in fore]
    y_lines = [[place(y, x, c) for y in range(8)] for x in range(4) for c in range(2)]
    squares = [[place(y, x, c) for x in range(4) for c in range(2)] for y in range(8)]
    x_lines = [[place(y, x, c) for x in range(4)] for y in range(8) for c in range(2)]

    half = (rows, feats // 2)
    mine, theirs = call(
        split_kernel, [(half, BF), (half, BF)], [SMEM, HBM], [VMEM, VMEM], pos, tokens,
        scratch=[pltpu.SemaphoreType.DMA((feats // 256,))],
    )
    swapped = lax.ppermute(theirs, "row", swap)
    (low_part,) = call(
        low_kernel, [((16, feats // 2), BF)], [VMEM, VMEM], [VMEM], tokens, down_proj.T
    )
    pair = jnp.concatenate([mine, swapped, low_part], axis=0)
    all_tokens = lax.all_gather(pair, "col", axis=0)

    w_both = jnp.concatenate([w_key, w_value], axis=1)
    wide = w_both.shape[1]
    w_line = lax.all_to_all(
        jnp.broadcast_to(w_both, (4,) + w_both.shape), "row", 0, 0, axis_index_groups=x_lines
    )
    w_own = w_line.reshape(feats // 2, wide)
    fore_going, aft_going = [w_own], [w_own]
    for _ in range(3):
        fore_going.append(lax.ppermute(fore_going[-1], "row", fore))
        aft_going.append(lax.ppermute(aft_going[-1], "row", aft))
    middle = feats // 4
    w_parts = fore_going + aft_going[1:] + [
        lax.ppermute(fore_going[3][:middle], "row", fore),
        lax.ppermute(aft_going[3][middle:], "row", aft),
    ]

    own, other, low_half = call(
        project_kernel,
        [((rows, wide), F32), ((rows, wide), F32), ((rows, 64), BF)],
        [SMEM] + [HBM] * 10,
        [VMEM] * 3,
        pos, all_tokens, *w_parts,
        scratch=[
            pltpu.VMEM((8, 2 * rows + 16, feats // 2), BF),
            pltpu.VMEM((8, feats // 2, wide), BF),
            pltpu.SemaphoreType.DMA((24,)),
        ],
        mib=56,
    )
    got = lax.ppermute(other, "row", swap)
    pack, gk, gv = call(
        attend_kernel,
        [((8, 80, 128), BF), ((rows, HD), F32), ((rows, HD), F32)],
        [SMEM] + [VMEM] * 5 + [HBM] * 2,
        [VMEM] * 3,
        lengths, own, got, low_half, up_key, up_value, queries, probes,
        scratch=[
            pltpu.VMEM((rows, feats), BF),
            pltpu.VMEM((rows, feats), BF),
            pltpu.SemaphoreType.DMA((8,)),
        ],
    )
    packs = lax.all_to_all(pack, "col", 0, 0)
    slot = (8, 64 + 8, 2 * HD)
    (terms,) = call(
        weigh_kernel, [(slot, BF)], [SMEM] + [VMEM] * 5, [VMEM],
        lengths, packs, low_half, gk, gv, tokens,
    )
    term_parts = lax.all_to_all(terms, "row", 0, 0, axis_index_groups=squares)
    (square,) = call(sum_kernel, [(slot, BF)], [VMEM], [VMEM], term_parts)
    square_parts = lax.all_to_all(square, "row", 0, 0, axis_index_groups=y_lines)
    (summed,) = call(sum_kernel, [(slot, BF)], [VMEM], [VMEM], square_parts)
    pieces = lax.all_to_all(summed, "row", 0, 0, axis_index_groups=squares)
    grad_down, grad_up_key, grad_up_value = call(
        place_kernel,
        [((64, feats), F32), ((64, HD), F32), ((64, HD), F32)],
        [VMEM], [VMEM] * 3, pieces,
    )
    return grad_down.T, grad_up_key, grad_up_value


def solution(mesh):
    in_specs = (
        P("row", "col"),
        P("row", "col"),
        P("row", "col"),
        P("row", "col"),
        P("row", "col"),
        P("col", None),
        P(None, "col"),
        P(None, "col"),
        P("row", None),
    )
    out_specs = (P("col", None), P(None, "col"), P(None, "col"))
    return jax.shard_map(
        on_device, mesh=mesh, in_specs=in_specs, out_specs=out_specs, check_vma=False
    )
```

```python
import functools
import jax
import jax.numpy as jnp
from jax import lax
from jax.experimental import pallas as pl
from jax.experimental.pallas import tpu as pltpu
from jax.sharding import PartitionSpec as P

HD = 128
QPK = 16
BF = jnp.bfloat16
F32 = jnp.float32
npo_beta = 0.5

VMEM = pl.BlockSpec(memory_space=pltpu.VMEM)
SMEM = pl.BlockSpec(memory_space=pltpu.SMEM)
HBM = pl.BlockSpec(memory_space=pltpu.HBM)

NT = (((1,), (1,)), ((), ()))
TN = (((0,), (0,)), ((), ()))
NN = (((1,), (0,)), ((), ()))


def mm(a, b, dims):
    return lax.dot_general(a, b, dims, preferred_element_type=F32)


def fold(a, rows):
    return jnp.concatenate([a[i:i + rows] for i in range(0, a.shape[0], rows)], axis=1)


def unfold(a, wide):
    return jnp.concatenate([a[:, i:i + wide] for i in range(0, a.shape[1], wide)], axis=0)


def doc_ids(lengths_ref, axis, count, docs):
    places = lax.broadcasted_iota(jnp.int32, (count, count), axis)
    ids = jnp.zeros((count, count), jnp.int32)
    end = 0
    for j in range(docs):
        end = end + lengths_ref[0, j]
        ids = ids + jnp.where(places >= end, 1, 0)
    return ids


def split_kernel(pos_ref, t_ref, mine_ref, theirs_ref, sem):
    copies = []
    for i in range(t_ref.shape[1] // 512):
        to = pl.ds(i * 256, 256)
        for k, ref in enumerate((mine_ref, theirs_ref)):
            core = lax.rem(pos_ref[0] + k, 2)
            at = pl.ds(pl.multiple_of(i * 512 + core * 256, 256), 256)
            copies.append(pltpu.make_async_copy(t_ref.at[:, at], ref.at[:, to], sem.at[2 * i + k]))
    for c in copies:
        c.start()
    for c in copies:
        c.wait()


def low_kernel(t_ref, down_ref, out_ref):
    low = mm(t_ref[...], down_ref[...], NT)
    rows, wide = out_ref.shape
    low = fold(low, rows // 2)
    high = low.astype(BF).astype(F32)
    out_ref[...] = jnp.concatenate([high, low - high], axis=0).astype(BF)


STEPS = (0, 1, 2, 3, -1, -2, -3, 4)


def ring_of(own, axis, fore, aft, cut):
    fore_going, aft_going = [own], [own]
    for _ in range(3):
        fore_going.append(lax.ppermute(fore_going[-1], axis, fore))
        aft_going.append(lax.ppermute(aft_going[-1], axis, aft))
    return fore_going + aft_going[1:] + [
        lax.ppermute(fore_going[3][:cut], axis, fore),
        lax.ppermute(aft_going[3][cut:], axis, aft),
    ]


def project_kernel(pos_ref, *refs):
    t_refs, w_refs, refs = refs[:9], refs[9:18], refs[18:]
    own_ref, other_ref, low_ref, t_scr, w_scr, sem = refs
    n = t_scr.shape[0]
    way = 2 * pos_ref[0] - 1
    copies = []
    for at, (parts, scr) in enumerate(((t_refs, t_scr), (w_refs, w_scr))):
        cut = parts[7].shape[0]
        for j, step in enumerate(STEPS):
            k = lax.rem(pos_ref[1 + at] + step * way + n, n)
            if step == 4:
                pairs = [
                    (parts[7], scr.at[k, pl.ds(0, cut)]),
                    (parts[8], scr.at[k, pl.ds(cut, scr.shape[1] - cut)]),
                ]
            else:
                pairs = [(parts[j], scr.at[k])]
            for i, (a, b) in enumerate(pairs):
                copies.append(pltpu.make_async_copy(a, b, sem.at[at, j + i]))
    for c in copies:
        c.start()
    for c in copies:
        c.wait()
    rows = own_ref.shape[0]
    total = jnp.zeros((2 * rows, w_scr.shape[2]), F32)
    low = jnp.zeros((t_scr.shape[1] - 2 * rows, t_scr.shape[2]), F32)
    for k in range(n):
        total = total + mm(t_scr[k, pl.ds(0, 2 * rows)], w_scr[k], NN)
        low = low + t_scr[k, pl.ds(2 * rows, low.shape[0])].astype(F32)
    own_ref[...] = total[:rows]
    other_ref[...] = total[rows:]
    low = low[:low.shape[0] // 2] + low[low.shape[0] // 2:]
    low_ref[...] = unfold(low, low_ref.shape[1]).astype(BF)


def attend_kernel(
    lengths_ref, own_ref, got_ref, low_ref, upk_ref, upv_ref, q_ref, p_ref,
    pack_ref, gk_ref, gv_ref, q_scr, p_scr, sem,
):
    rows = own_ref.shape[0]
    heads = q_ref.shape[1] // HD
    batch = 4
    copies = []
    for i in range(heads // batch):
        at = pl.ds(i * batch * HD, batch * HD)
        for k, (ref, scr) in enumerate(((q_ref, q_scr), (p_ref, p_scr))):
            copies.append(pltpu.make_async_copy(ref.at[:, at], scr.at[:, at], sem.at[2 * i + k]))
    for c in copies:
        c.start()
    score_scale = HD ** (-0.5)
    probe_scale = (q_ref.shape[1] * pack_ref.shape[0]) ** (-0.5)
    low_half = low_ref[...]
    full = own_ref[...] + got_ref[...]
    key_full, value_full = full[:, :HD], full[:, HD:]
    key_pol = (key_full + mm(low_half, upk_ref[...], NN)).astype(BF)
    value_pol = (value_full + mm(low_half, upv_ref[...], NN)).astype(BF)
    keys = jnp.concatenate([key_pol, key_full.astype(BF)], axis=0)
    values = jnp.concatenate([value_pol, value_full.astype(BF)], axis=0)
    doc_s = doc_ids(lengths_ref, 0, rows, lengths_ref.shape[1])
    doc_t = doc_ids(lengths_ref, 1, rows, lengths_ref.shape[1])
    s_at = lax.broadcasted_iota(jnp.int32, (rows, rows), 0)
    t_at = lax.broadcasted_iota(jnp.int32, (rows, rows), 1)
    allowed = (doc_s == doc_t) & (t_at >= s_at)

    def probs_of(scores):
        scores = jnp.where(allowed, scores * score_scale, -1e30)
        peak = jnp.max(scores, axis=0, keepdims=True)
        e = jnp.exp(scores - peak)
        return e / jnp.sum(e, axis=0, keepdims=True)

    gk = jnp.zeros((rows, HD), F32)
    gv = jnp.zeros((rows, HD), F32)
    gap = jnp.zeros((1, rows), F32)
    for h in range(heads):
        if h % batch == 0:
            for c in copies[2 * h // batch:2 * h // batch + 2]:
                c.wait()
        q = q_scr[:, pl.ds(h * HD, HD)]
        probe = p_scr[:, pl.ds(h * HD, HD)]
        scores = mm(keys, q, NT)
        grads = mm(values, probe, NT)
        pol = probs_of(scores[:rows])
        ref = probs_of(scores[rows:])
        grad_pol = grads[:rows]
        mean_pol = jnp.sum(pol * grad_pol, axis=0, keepdims=True)
        mean_ref = jnp.sum(ref * grads[rows:], axis=0, keepdims=True)
        gap = gap + (mean_pol - mean_ref)
        grad_scores = (pol * (grad_pol - mean_pol)).astype(BF)
        gk = gk + mm(grad_scores, q, NN)
        gv = gv + mm(pol.astype(BF), probe, NN)
    gk = gk * (score_scale * probe_scale)
    gv = gv * probe_scale
    gap = gap * probe_scale
    gk_ref[...] = gk
    gv_ref[...] = gv
    back = mm(gk.astype(BF), upk_ref[...], NT) + mm(gv.astype(BF), upv_ref[...], NT)
    back = fold(back, 64).astype(BF)
    first = gap.astype(BF).astype(F32)
    second = (gap - first).astype(BF).astype(F32)
    third = gap - first - second
    line = lax.broadcasted_iota(jnp.int32, (16, rows), 0)
    tail = jnp.where(line == 0, first, jnp.where(line == 1, second, jnp.where(line == 2, third, 0.0)))
    tail = tail.astype(BF)
    for i in range(pack_ref.shape[0]):
        pack_ref[i, pl.ds(0, 64)] = back
        pack_ref[i, pl.ds(64, 16)] = tail


def weigh_kernel(lengths_ref, pack_ref, low_half_ref, gk_ref, gv_ref, t_ref, out_ref):
    rows = gk_ref.shape[0]
    total = pack_ref[0].astype(F32)
    for i in range(1, pack_ref.shape[0]):
        total = total + pack_ref[i].astype(F32)
    gap = total[64:65] + total[65:66] + total[66:67]
    docs = lengths_ref.shape[1]
    same = doc_ids(lengths_ref, 0, rows, docs) == doc_ids(lengths_ref, 1, rows, docs)
    token_gap = jnp.sum(jnp.where(same, gap, 0.0), axis=1, keepdims=True)
    weight = 2.0 * jax.nn.sigmoid(npo_beta * token_gap)
    back_half = (unfold(total[:64], 64) * weight).astype(BF)
    down = mm(back_half, t_ref[...], TN).astype(BF)
    both = jnp.concatenate([gk_ref[...] * weight, gv_ref[...] * weight], axis=1).astype(BF)
    up = mm(low_half_ref[...], both, TN).astype(BF)
    slots = out_ref.shape[0]
    wide, deep = t_ref.shape[1] // slots, up.shape[0] // slots
    for j in range(slots):
        out_ref[j, pl.ds(0, 64)] = down[:, j * wide:(j + 1) * wide]
        out_ref[j, pl.ds(64, deep)] = up[j * deep:(j + 1) * deep]


def sum_kernel(in_ref, out_ref):
    total = in_ref[0].astype(F32)
    for i in range(1, in_ref.shape[0]):
        total = total + in_ref[i].astype(F32)
    total = total.astype(BF)
    for i in range(out_ref.shape[0]):
        out_ref[i] = total


def place_kernel(in_ref, down_ref, upk_ref, upv_ref):
    slots, _, wide = in_ref.shape
    deep = upk_ref.shape[0] // slots
    for j in range(slots):
        down_ref[:, pl.ds(j * wide, wide)] = in_ref[j, pl.ds(0, 64)].astype(F32)
        up = in_ref[j, pl.ds(64, deep)].astype(F32)
        upk_ref[pl.ds(j * deep, deep)] = up[:, :HD]
        upv_ref[pl.ds(j * deep, deep)] = up[:, HD:]


def call(kernel, outs, in_specs, out_specs, *args, scratch=(), mib=8):
    return pl.pallas_call(
        kernel,
        out_shape=[jax.ShapeDtypeStruct(s, d) for s, d in outs],
        in_specs=in_specs,
        out_specs=out_specs,
        scratch_shapes=list(scratch),
        compiler_params=pltpu.CompilerParams(vmem_limit_bytes=mib * 1024 * 1024),
    )(*args)


def on_device(tokens, queries, probes, w_key, w_value, down_proj, up_key, up_value, lengths):
    rows, feats = tokens.shape
    row_at = lax.axis_index("row")
    pos = jnp.stack([row_at % 2, lax.axis_index("col"), row_at // 8]).astype(jnp.int32)

    def place(y, x, core):
        return ((y % 8) * 4 + x % 4) * 2 + core % 2

    sites = [(y, x, core) for y in range(8) for x in range(4) for core in range(2)]
    swap = [(place(y, x, c), place(y, x, 1 - c)) for y, x, c in sites]
    y_fore = [(place(y, x, c), place(y + 1 - 2 * c, x, c)) for y, x, c in sites]
    y_aft = [(b, a) for a, b in y_fore]
    z_fore = [
        (place(y, x, c) * 8 + z, place(y, x, c) * 8 + (z + 1 - 2 * c) % 8)
        for y, x, c in sites
        for z in range(8)
    ]
    z_aft = [(b, a) for a, b in z_fore]
    y_lines = [[place(y, x, c) for y in range(8)] for x in range(4) for c in range(2)]
    squares = [[place(y, x, c) for x in range(4) for c in range(2)] for y in range(8)]
    x_lines = [[place(y, x, c) for x in range(4)] for y in range(8) for c in range(2)]

    half = (rows, feats // 2)
    mine, theirs = call(
        split_kernel, [(half, BF), (half, BF)], [SMEM, HBM], [VMEM, VMEM], pos, tokens,
        scratch=[pltpu.SemaphoreType.DMA((feats // 256,))],
    )
    swapped = lax.ppermute(theirs, "row", swap)
    (low_part,) = call(
        low_kernel, [((16, feats // 2), BF)], [VMEM, VMEM], [VMEM], tokens, down_proj.T
    )
    pair = jnp.concatenate([mine, swapped, low_part], axis=0)
    t_parts = ring_of(pair, ("row", "col"), z_fore, z_aft, rows)

    w_both = jnp.concatenate([w_key, w_value], axis=1)
    wide = w_both.shape[1]
    w_line = lax.all_to_all(
        jnp.broadcast_to(w_both, (4,) + w_both.shape), "row", 0, 0, axis_index_groups=x_lines
    )
    w_own = w_line.reshape(feats // 2, wide)
    w_parts = ring_of(w_own, "row", y_fore, y_aft, feats // 4)

    own, other, low_half = call(
        project_kernel,
        [((rows, wide), F32), ((rows, wide), F32), ((rows, 64), BF)],
        [SMEM] + [HBM] * 18,
        [VMEM] * 3,
        pos, *t_parts, *w_parts,
        scratch=[
            pltpu.VMEM((8, 2 * rows + 16, feats // 2), BF),
            pltpu.VMEM((8, feats // 2, wide), BF),
            pltpu.SemaphoreType.DMA((2, 9)),
        ],
        mib=56,
    )
    got = lax.ppermute(other, "row", swap)
    pack, gk, gv = call(
        attend_kernel,
        [((8, 80, 128), BF), ((rows, HD), F32), ((rows, HD), F32)],
        [SMEM] + [VMEM] * 5 + [HBM] * 2,
        [VMEM] * 3,
        lengths, own, got, low_half, up_key, up_value, queries, probes,
        scratch=[
            pltpu.VMEM((rows, feats), BF),
            pltpu.VMEM((rows, feats), BF),
            pltpu.SemaphoreType.DMA((8,)),
        ],
    )
    packs = lax.all_to_all(pack, "col", 0, 0)
    slot = (8, 64 + 8, 2 * HD)
    (terms,) = call(
        weigh_kernel, [(slot, BF)], [SMEM] + [VMEM] * 5, [VMEM],
        lengths, packs, low_half, gk, gv, tokens,
    )
    term_parts = lax.all_to_all(terms, "row", 0, 0, axis_index_groups=squares)
    (square,) = call(sum_kernel, [(slot, BF)], [VMEM], [VMEM], term_parts)
    square_parts = lax.all_to_all(square, "row", 0, 0, axis_index_groups=y_lines)
    (summed,) = call(sum_kernel, [(slot, BF)], [VMEM], [VMEM], square_parts)
    pieces = lax.all_to_all(summed, "row", 0, 0, axis_index_groups=squares)
    grad_down, grad_up_key, grad_up_value = call(
        place_kernel,
        [((64, feats), F32), ((64, HD), F32), ((64, HD), F32)],
        [VMEM], [VMEM] * 3, pieces,
    )
    return grad_down.T, grad_up_key, grad_up_value


def solution(mesh):
    in_specs = (
        P("row", "col"),
        P("row", "col"),
        P("row", "col"),
        P("row", "col"),
        P("row", "col"),
        P("col", None),
        P(None, "col"),
        P(None, "col"),
        P("row", None),
    )
    out_specs = (P("col", None), P(None, "col"), P(None, "col"))
    return jax.shard_map(
        on_device, mesh=mesh, in_specs=in_specs, out_specs=out_specs, check_vma=False
    )
```

```python
import functools
import jax
import jax.numpy as jnp
from jax import lax
from jax.experimental import pallas as pl
from jax.experimental.pallas import tpu as pltpu
from jax.sharding import PartitionSpec as P

HD = 128
QPK = 16
BF = jnp.bfloat16
F32 = jnp.float32
npo_beta = 0.5

VMEM = pl.BlockSpec(memory_space=pltpu.VMEM)
SMEM = pl.BlockSpec(memory_space=pltpu.SMEM)
HBM = pl.BlockSpec(memory_space=pltpu.HBM)

NT = (((1,), (1,)), ((), ()))
TN = (((0,), (0,)), ((), ()))
NN = (((1,), (0,)), ((), ()))


def mm(a, b, dims):
    return lax.dot_general(a, b, dims, preferred_element_type=F32)


def fold(a, rows):
    return jnp.concatenate([a[i:i + rows] for i in range(0, a.shape[0], rows)], axis=1)


def unfold(a, wide):
    return jnp.concatenate([a[:, i:i + wide] for i in range(0, a.shape[1], wide)], axis=0)


def doc_ids(lengths_ref, axis, count, docs):
    places = lax.broadcasted_iota(jnp.int32, (count, count), axis)
    ids = jnp.zeros((count, count), jnp.int32)
    end = 0
    for j in range(docs):
        end = end + lengths_ref[0, j]
        ids = ids + jnp.where(places >= end, 1, 0)
    return ids


def split_kernel(pos_ref, t_ref, mine_ref, theirs_ref, sem):
    copies = []
    for i in range(t_ref.shape[1] // 512):
        to = pl.ds(i * 256, 256)
        for k, ref in enumerate((mine_ref, theirs_ref)):
            core = lax.rem(pos_ref[0] + k, 2)
            at = pl.ds(pl.multiple_of(i * 512 + core * 256, 256), 256)
            copies.append(pltpu.make_async_copy(t_ref.at[:, at], ref.at[:, to], sem.at[2 * i + k]))
    for c in copies:
        c.start()
    for c in copies:
        c.wait()


def low_kernel(t_ref, down_ref, out_ref):
    low = mm(t_ref[...], down_ref[...], NT)
    rows, wide = out_ref.shape
    low = fold(low, rows // 2)
    high = low.astype(BF).astype(F32)
    out_ref[...] = jnp.concatenate([high, low - high], axis=0).astype(BF)


STEPS = (0, 1, 2, 3, -1, -2, -3, 4)


def ring_of(own, axis, fore, swap):
    near, far, crossed = [own], lax.ppermute(own, "row", swap), []
    for _ in range(3):
        near.append(lax.ppermute(near[-1], axis, fore))
        far = lax.ppermute(far, axis, fore)
        crossed.append(lax.ppermute(far, "row", swap))
    return near + crossed + [lax.ppermute(near[3], axis, fore)]


def project_kernel(pos_ref, *refs):
    t_refs, w_refs, refs = refs[:8], refs[8:16], refs[16:]
    own_ref, other_ref, low_ref, t_scr, w_scr, sem = refs
    n = t_scr.shape[0]
    way = 2 * pos_ref[0] - 1
    copies = []
    for at, (parts, scr) in enumerate(((t_refs, t_scr), (w_refs, w_scr))):
        for j, step in enumerate(STEPS):
            k = lax.rem(pos_ref[1 + at] + step * way + n, n)
            copies.append(pltpu.make_async_copy(parts[j], scr.at[k], sem.at[at, j]))
    for c in copies:
        c.start()
    for c in copies:
        c.wait()
    rows = own_ref.shape[0]
    total = jnp.zeros((2 * rows, w_scr.shape[2]), F32)
    low = jnp.zeros((t_scr.shape[1] - 2 * rows, t_scr.shape[2]), F32)
    for k in range(n):
        total = total + mm(t_scr[k, pl.ds(0, 2 * rows)], w_scr[k], NN)
        low = low + t_scr[k, pl.ds(2 * rows, low.shape[0])].astype(F32)
    own_ref[...] = total[:rows]
    other_ref[...] = total[rows:]
    low = low[:low.shape[0] // 2] + low[low.shape[0] // 2:]
    low_ref[...] = unfold(low, low_ref.shape[1]).astype(BF)


def attend_kernel(
    lengths_ref, own_ref, got_ref, low_ref, upk_ref, upv_ref, q_ref, p_ref,
    pack_ref, gk_ref, gv_ref, q_scr, p_scr, sem,
):
    rows = own_ref.shape[0]
    heads = q_ref.shape[1] // HD
    batch = 4
    copies = []
    for i in range(heads // batch):
        at = pl.ds(i * batch * HD, batch * HD)
        for k, (ref, scr) in enumerate(((q_ref, q_scr), (p_ref, p_scr))):
            copies.append(pltpu.make_async_copy(ref.at[:, at], scr.at[:, at], sem.at[2 * i + k]))
    for c in copies:
        c.start()
    score_scale = HD ** (-0.5)
    probe_scale = (q_ref.shape[1] * pack_ref.shape[0]) ** (-0.5)
    low_half = low_ref[...]
    full = own_ref[...] + got_ref[...]
    key_full, value_full = full[:, :HD], full[:, HD:]
    key_pol = (key_full + mm(low_half, upk_ref[...], NN)).astype(BF)
    value_pol = (value_full + mm(low_half, upv_ref[...], NN)).astype(BF)
    keys = jnp.concatenate([key_pol, key_full.astype(BF)], axis=0)
    values = jnp.concatenate([value_pol, value_full.astype(BF)], axis=0)
    doc_s = doc_ids(lengths_ref, 0, rows, lengths_ref.shape[1])
    doc_t = doc_ids(lengths_ref, 1, rows, lengths_ref.shape[1])
    s_at = lax.broadcasted_iota(jnp.int32, (rows, rows), 0)
    t_at = lax.broadcasted_iota(jnp.int32, (rows, rows), 1)
    allowed = (doc_s == doc_t) & (t_at >= s_at)

    def probs_of(scores):
        scores = jnp.where(allowed, scores * score_scale, -1e30)
        peak = jnp.max(scores, axis=0, keepdims=True)
        e = jnp.exp(scores - peak)
        return e / jnp.sum(e, axis=0, keepdims=True)

    gk = jnp.zeros((rows, HD), F32)
    gv = jnp.zeros((rows, HD), F32)
    gap = jnp.zeros((1, rows), F32)
    for h in range(heads):
        if h % batch == 0:
            for c in copies[2 * h // batch:2 * h // batch + 2]:
                c.wait()
        q = q_scr[:, pl.ds(h * HD, HD)]
        probe = p_scr[:, pl.ds(h * HD, HD)]
        scores = mm(keys, q, NT)
        grads = mm(values, probe, NT)
        pol = probs_of(scores[:rows])
        ref = probs_of(scores[rows:])
        grad_pol = grads[:rows]
        mean_pol = jnp.sum(pol * grad_pol, axis=0, keepdims=True)
        mean_ref = jnp.sum(ref * grads[rows:], axis=0, keepdims=True)
        gap = gap + (mean_pol - mean_ref)
        grad_scores = (pol * (grad_pol - mean_pol)).astype(BF)
        gk = gk + mm(grad_scores, q, NN)
        gv = gv + mm(pol.astype(BF), probe, NN)
    gk = gk * (score_scale * probe_scale)
    gv = gv * probe_scale
    gap = gap * probe_scale
    gk_ref[...] = gk
    gv_ref[...] = gv
    back = mm(gk.astype(BF), upk_ref[...], NT) + mm(gv.astype(BF), upv_ref[...], NT)
    back = fold(back, 64).astype(BF)
    first = gap.astype(BF).astype(F32)
    second = (gap - first).astype(BF).astype(F32)
    third = gap - first - second
    line = lax.broadcasted_iota(jnp.int32, (16, rows), 0)
    tail = jnp.where(line == 0, first, jnp.where(line == 1, second, jnp.where(line == 2, third, 0.0)))
    tail = tail.astype(BF)
    for i in range(pack_ref.shape[0]):
        pack_ref[i, pl.ds(0, 64)] = back
        pack_ref[i, pl.ds(64, 16)] = tail


def weigh_kernel(lengths_ref, pack_ref, low_half_ref, gk_ref, gv_ref, t_ref, out_ref):
    rows = gk_ref.shape[0]
    total = pack_ref[0].astype(F32)
    for i in range(1, pack_ref.shape[0]):
        total = total + pack_ref[i].astype(F32)
    gap = total[64:65] + total[65:66] + total[66:67]
    docs = lengths_ref.shape[1]
    same = doc_ids(lengths_ref, 0, rows, docs) == doc_ids(lengths_ref, 1, rows, docs)
    token_gap = jnp.sum(jnp.where(same, gap, 0.0), axis=1, keepdims=True)
    weight = 2.0 * jax.nn.sigmoid(npo_beta * token_gap)
    back_half = (unfold(total[:64], 64) * weight).astype(BF)
    down = mm(back_half, t_ref[...], TN).astype(BF)
    both = jnp.concatenate([gk_ref[...] * weight, gv_ref[...] * weight], axis=1).astype(BF)
    up = mm(low_half_ref[...], both, TN).astype(BF)
    slots = out_ref.shape[0]
    wide, deep = t_ref.shape[1] // slots, up.shape[0] // slots
    for j in range(slots):
        out_ref[j, pl.ds(0, 64)] = down[:, j * wide:(j + 1) * wide]
        out_ref[j, pl.ds(64, deep)] = up[j * deep:(j + 1) * deep]


def sum_kernel(in_ref, out_ref):
    total = in_ref[0].astype(F32)
    for i in range(1, in_ref.shape[0]):
        total = total + in_ref[i].astype(F32)
    total = total.astype(BF)
    for i in range(out_ref.shape[0]):
        out_ref[i] = total


def place_kernel(in_ref, down_ref, upk_ref, upv_ref):
    slots, _, wide = in_ref.shape
    deep = upk_ref.shape[0] // slots
    for j in range(slots):
        down_ref[:, pl.ds(j * wide, wide)] = in_ref[j, pl.ds(0, 64)].astype(F32)
        up = in_ref[j, pl.ds(64, deep)].astype(F32)
        upk_ref[pl.ds(j * deep, deep)] = up[:, :HD]
        upv_ref[pl.ds(j * deep, deep)] = up[:, HD:]


def call(kernel, outs, in_specs, out_specs, *args, scratch=(), mib=8):
    return pl.pallas_call(
        kernel,
        out_shape=[jax.ShapeDtypeStruct(s, d) for s, d in outs],
        in_specs=in_specs,
        out_specs=out_specs,
        scratch_shapes=list(scratch),
        compiler_params=pltpu.CompilerParams(vmem_limit_bytes=mib * 1024 * 1024),
    )(*args)


def on_device(tokens, queries, probes, w_key, w_value, down_proj, up_key, up_value, lengths):
    rows, feats = tokens.shape
    row_at = lax.axis_index("row")
    pos = jnp.stack([row_at % 2, lax.axis_index("col"), row_at // 8]).astype(jnp.int32)

    def place(y, x, core):
        return ((y % 8) * 4 + x % 4) * 2 + core % 2

    sites = [(y, x, core) for y in range(8) for x in range(4) for core in range(2)]
    swap = [(place(y, x, c), place(y, x, 1 - c)) for y, x, c in sites]
    y_fore = [(place(y, x, c), place(y + 1 - 2 * c, x, c)) for y, x, c in sites]
    z_fore = [
        (place(y, x, c) * 8 + z, place(y, x, c) * 8 + (z + 1 - 2 * c) % 8)
        for y, x, c in sites
        for z in range(8)
    ]
    y_lines = [[place(y, x, c) for y in range(8)] for x in range(4) for c in range(2)]
    squares = [[place(y, x, c) for x in range(4) for c in range(2)] for y in range(8)]
    x_lines = [[place(y, x, c) for x in range(4)] for y in range(8) for c in range(2)]

    half = (rows, feats // 2)
    mine, theirs = call(
        split_kernel, [(half, BF), (half, BF)], [SMEM, HBM], [VMEM, VMEM], pos, tokens,
        scratch=[pltpu.SemaphoreType.DMA((feats // 256,))],
    )
    swapped = lax.ppermute(theirs, "row", swap)
    (low_part,) = call(
        low_kernel, [((16, feats // 2), BF)], [VMEM, VMEM], [VMEM], tokens, down_proj.T
    )
    pair = jnp.concatenate([mine, swapped, low_part], axis=0)
    t_parts = ring_of(pair, ("row", "col"), z_fore, swap)

    w_both = jnp.concatenate([w_key, w_value], axis=1)
    wide = w_both.shape[1]
    w_line = lax.all_to_all(
        jnp.broadcast_to(w_both, (4,) + w_both.shape), "row", 0, 0, axis_index_groups=x_lines
    )
    w_own = w_line.reshape(feats // 2, wide)
    w_parts = ring_of(w_own, "row", y_fore, swap)

    own, other, low_half = call(
        project_kernel,
        [((rows, wide), F32), ((rows, wide), F32), ((rows, 64), BF)],
        [SMEM] + [HBM] * 16,
        [VMEM] * 3,
        pos, *t_parts, *w_parts,
        scratch=[
            pltpu.VMEM((8, 2 * rows + 16, feats // 2), BF),
            pltpu.VMEM((8, feats // 2, wide), BF),
            pltpu.SemaphoreType.DMA((2, 8)),
        ],
        mib=56,
    )
    got = lax.ppermute(other, "row", swap)
    pack, gk, gv = call(
        attend_kernel,
        [((8, 80, 128), BF), ((rows, HD), F32), ((rows, HD), F32)],
        [SMEM] + [VMEM] * 5 + [HBM] * 2,
        [VMEM] * 3,
        lengths, own, got, low_half, up_key, up_value, queries, probes,
        scratch=[
            pltpu.VMEM((rows, feats), BF),
            pltpu.VMEM((rows, feats), BF),
            pltpu.SemaphoreType.DMA((8,)),
        ],
    )
    packs = lax.all_to_all(pack, "col", 0, 0)
    slot = (8, 64 + 8, 2 * HD)
    (terms,) = call(
        weigh_kernel, [(slot, BF)], [SMEM] + [VMEM] * 5, [VMEM],
        lengths, packs, low_half, gk, gv, tokens,
    )
    term_parts = lax.all_to_all(terms, "row", 0, 0, axis_index_groups=squares)
    (square,) = call(sum_kernel, [(slot, BF)], [VMEM], [VMEM], term_parts)
    square_parts = lax.all_to_all(square, "row", 0, 0, axis_index_groups=y_lines)
    (summed,) = call(sum_kernel, [(slot, BF)], [VMEM], [VMEM], square_parts)
    pieces = lax.all_to_all(summed, "row", 0, 0, axis_index_groups=squares)
    grad_down, grad_up_key, grad_up_value = call(
        place_kernel,
        [((64, feats), F32), ((64, HD), F32), ((64, HD), F32)],
        [VMEM], [VMEM] * 3, pieces,
    )
    return grad_down.T, grad_up_key, grad_up_value


def solution(mesh):
    in_specs = (
        P("row", "col"),
        P("row", "col"),
        P("row", "col"),
        P("row", "col"),
        P("row", "col"),
        P("col", None),
        P(None, "col"),
        P(None, "col"),
        P("row", None),
    )
    out_specs = (P("col", None), P(None, "col"), P(None, "col"))
    return jax.shard_map(
        on_device, mesh=mesh, in_specs=in_specs, out_specs=out_specs, check_vma=False
    )
```

```python
import functools
import jax
import jax.numpy as jnp
from jax import lax
from jax.experimental import pallas as pl
from jax.experimental.pallas import tpu as pltpu
from jax.sharding import PartitionSpec as P

HD = 128
QPK = 16
BF = jnp.bfloat16
F32 = jnp.float32
npo_beta = 0.5

VMEM = pl.BlockSpec(memory_space=pltpu.VMEM)
SMEM = pl.BlockSpec(memory_space=pltpu.SMEM)
HBM = pl.BlockSpec(memory_space=pltpu.HBM)

NT = (((1,), (1,)), ((), ()))
TN = (((0,), (0,)), ((), ()))
NN = (((1,), (0,)), ((), ()))


def mm(a, b, dims):
    return lax.dot_general(a, b, dims, preferred_element_type=F32)


def fold(a, rows):
    return jnp.concatenate([a[i:i + rows] for i in range(0, a.shape[0], rows)], axis=1)


def unfold(a, wide):
    return jnp.concatenate([a[:, i:i + wide] for i in range(0, a.shape[1], wide)], axis=0)


def doc_ids(lengths_ref, axis, count, docs):
    places = lax.broadcasted_iota(jnp.int32, (count, count), axis)
    ids = jnp.zeros((count, count), jnp.int32)
    end = 0
    for j in range(docs):
        end = end + lengths_ref[0, j]
        ids = ids + jnp.where(places >= end, 1, 0)
    return ids


def spread_kernel(pos_ref, t_ref, out_ref, sem):
    copies = []
    for slot in range(4):
        for i in range(2):
            x = slot // 2 + 2 * lax.rem(pos_ref[3] + i, 2)
            at = pl.ds(pl.multiple_of(x * 512 + slot % 2 * 256, 256), 256)
            copies.append(
                pltpu.make_async_copy(
                    t_ref.at[:, at], out_ref.at[slot, :, pl.ds(i * 256, 256)], sem.at[2 * slot + i]
                )
            )
    for c in copies:
        c.start()
    for c in copies:
        c.wait()


def low_kernel(t_ref, down_ref, out_ref):
    low = mm(t_ref[...], down_ref[...], NT)
    rows, wide = out_ref.shape
    low = fold(low, rows // 2)
    high = low.astype(BF).astype(F32)
    out_ref[...] = jnp.concatenate([high, low - high], axis=0).astype(BF)


STEPS = (0, 1, 2, 3, -1, -2, -3, 4)


def ring_of(own, axis, fore, swap):
    near, far, crossed = [own], lax.ppermute(own, "row", swap), []
    for _ in range(3):
        near.append(lax.ppermute(near[-1], axis, fore))
        far = lax.ppermute(far, axis, fore)
        crossed.append(lax.ppermute(far, "row", swap))
    return near + crossed + [lax.ppermute(near[3], axis, fore)]


def project_kernel(pos_ref, *refs):
    t_refs, (w_ref, out_ref, low_ref, t_scr, w_scr, t_sem, w_sem) = refs[:8], refs[8:]
    n = t_scr.shape[0]
    slots, rows, wide = out_ref.shape
    way = 2 * pos_ref[0] - 1
    copies = [pltpu.make_async_copy(w_ref, w_scr, w_sem)]
    for j, step in enumerate(STEPS):
        k = lax.rem(pos_ref[1] + step * way + n, n)
        copies.append(pltpu.make_async_copy(t_refs[j], t_scr.at[k], t_sem.at[j]))
    for c in copies:
        c.start()
    for c in copies:
        c.wait()
    total = jnp.zeros((slots * rows, wide), F32)
    low = jnp.zeros((t_scr.shape[1] - slots * rows, t_scr.shape[2]), F32)
    for k in range(n):
        total = total + mm(t_scr[k, pl.ds(0, slots * rows)], w_scr[k], NN)
        low = low + t_scr[k, pl.ds(slots * rows, low.shape[0])].astype(F32)
    for i in range(slots):
        out_ref[i] = total[i * rows:(i + 1) * rows].astype(BF)
    low = low[:low.shape[0] // 2] + low[low.shape[0] // 2:]
    low_ref[...] = unfold(low, low_ref.shape[1]).astype(BF)


def attend_kernel(
    lengths_ref, full_ref, low_ref, upk_ref, upv_ref, q_ref, p_ref,
    pack_ref, gk_ref, gv_ref, q_scr, p_scr, sem,
):
    rows = q_ref.shape[0]
    heads = q_ref.shape[1] // HD
    batch = 4
    copies = []
    for i in range(heads // batch):
        at = pl.ds(i * batch * HD, batch * HD)
        for k, (ref, scr) in enumerate(((q_ref, q_scr), (p_ref, p_scr))):
            copies.append(pltpu.make_async_copy(ref.at[:, at], scr.at[:, at], sem.at[2 * i + k]))
    for c in copies:
        c.start()
    score_scale = HD ** (-0.5)
    probe_scale = (q_ref.shape[1] * pack_ref.shape[0]) ** (-0.5)
    low_half = low_ref[...]
    full = full_ref[0].astype(F32)
    for i in range(1, full_ref.shape[0]):
        full = full + full_ref[i].astype(F32)
    key_full, value_full = full[:, :HD], full[:, HD:]
    key_pol = (key_full + mm(low_half, upk_ref[...], NN)).astype(BF)
    value_pol = (value_full + mm(low_half, upv_ref[...], NN)).astype(BF)
    keys = jnp.concatenate([key_pol, key_full.astype(BF)], axis=0)
    values = jnp.concatenate([value_pol, value_full.astype(BF)], axis=0)
    doc_s = doc_ids(lengths_ref, 0, rows, lengths_ref.shape[1])
    doc_t = doc_ids(lengths_ref, 1, rows, lengths_ref.shape[1])
    s_at = lax.broadcasted_iota(jnp.int32, (rows, rows), 0)
    t_at = lax.broadcasted_iota(jnp.int32, (rows, rows), 1)
    allowed = (doc_s == doc_t) & (t_at >= s_at)

    def probs_of(scores):
        scores = jnp.where(allowed, scores * score_scale, -1e30)
        peak = jnp.max(scores, axis=0, keepdims=True)
        e = jnp.exp(scores - peak)
        return e / jnp.sum(e, axis=0, keepdims=True)

    gk = jnp.zeros((rows, HD), F32)
    gv = jnp.zeros((rows, HD), F32)
    gap = jnp.zeros((1, rows), F32)
    for h in range(heads):
        if h % batch == 0:
            for c in copies[2 * h // batch:2 * h // batch + 2]:
                c.wait()
        q = q_scr[:, pl.ds(h * HD, HD)]
        probe = p_scr[:, pl.ds(h * HD, HD)]
        scores = mm(keys, q, NT)
        grads = mm(values, probe, NT)
        pol = probs_of(scores[:rows])
        ref = probs_of(scores[rows:])
        grad_pol = grads[:rows]
        mean_pol = jnp.sum(pol * grad_pol, axis=0, keepdims=True)
        mean_ref = jnp.sum(ref * grads[rows:], axis=0, keepdims=True)
        gap = gap + (mean_pol - mean_ref)
        grad_scores = (pol * (grad_pol - mean_pol)).astype(BF)
        gk = gk + mm(grad_scores, q, NN)
        gv = gv + mm(pol.astype(BF), probe, NN)
    gk = gk * (score_scale * probe_scale)
    gv = gv * probe_scale
    gap = gap * probe_scale
    gk_ref[...] = gk
    gv_ref[...] = gv
    back = mm(gk.astype(BF), upk_ref[...], NT) + mm(gv.astype(BF), upv_ref[...], NT)
    back = fold(back, 64).astype(BF)
    first = gap.astype(BF).astype(F32)
    second = (gap - first).astype(BF).astype(F32)
    third = gap - first - second
    line = lax.broadcasted_iota(jnp.int32, (16, rows), 0)
    tail = jnp.where(line == 0, first, jnp.where(line == 1, second, jnp.where(line == 2, third, 0.0)))
    tail = tail.astype(BF)
    for i in range(pack_ref.shape[0]):
        pack_ref[i, pl.ds(0, 64)] = back
        pack_ref[i, pl.ds(64, 16)] = tail


def weigh_kernel(lengths_ref, pack_ref, low_half_ref, gk_ref, gv_ref, t_ref, out_ref):
    rows = gk_ref.shape[0]
    total = pack_ref[0].astype(F32)
    for i in range(1, pack_ref.shape[0]):
        total = total + pack_ref[i].astype(F32)
    gap = total[64:65] + total[65:66] + total[66:67]
    docs = lengths_ref.shape[1]
    same = doc_ids(lengths_ref, 0, rows, docs) == doc_ids(lengths_ref, 1, rows, docs)
    token_gap = jnp.sum(jnp.where(same, gap, 0.0), axis=1, keepdims=True)
    weight = 2.0 * jax.nn.sigmoid(npo_beta * token_gap)
    back_half = (unfold(total[:64], 64) * weight).astype(BF)
    down = mm(back_half, t_ref[...], TN).astype(BF)
    both = jnp.concatenate([gk_ref[...] * weight, gv_ref[...] * weight], axis=1).astype(BF)
    up = mm(low_half_ref[...], both, TN).astype(BF)
    slots = out_ref.shape[0]
    wide, deep = t_ref.shape[1] // slots, up.shape[0] // slots
    for j in range(slots):
        out_ref[j, pl.ds(0, 64)] = down[:, j * wide:(j + 1) * wide]
        out_ref[j, pl.ds(64, deep)] = up[j * deep:(j + 1) * deep]


def sum_kernel(in_ref, out_ref):
    total = in_ref[0].astype(F32)
    for i in range(1, in_ref.shape[0]):
        total = total + in_ref[i].astype(F32)
    total = total.astype(BF)
    for i in range(out_ref.shape[0]):
        out_ref[i] = total


def place_kernel(in_ref, down_ref, upk_ref, upv_ref):
    slots, _, wide = in_ref.shape
    deep = upk_ref.shape[0] // slots
    for j in range(slots):
        down_ref[:, pl.ds(j * wide, wide)] = in_ref[j, pl.ds(0, 64)].astype(F32)
        up = in_ref[j, pl.ds(64, deep)].astype(F32)
        upk_ref[pl.ds(j * deep, deep)] = up[:, :HD]
        upv_ref[pl.ds(j * deep, deep)] = up[:, HD:]


def call(kernel, outs, in_specs, out_specs, *args, scratch=(), mib=8):
    return pl.pallas_call(
        kernel,
        out_shape=[jax.ShapeDtypeStruct(s, d) for s, d in outs],
        in_specs=in_specs,
        out_specs=out_specs,
        scratch_shapes=list(scratch),
        compiler_params=pltpu.CompilerParams(vmem_limit_bytes=mib * 1024 * 1024),
    )(*args)


def on_device(tokens, queries, probes, w_key, w_value, down_proj, up_key, up_value, lengths):
    rows, feats = tokens.shape
    row_at = lax.axis_index("row")
    pos = jnp.stack([row_at % 2, lax.axis_index("col"), row_at // 8, row_at // 4 % 2]).astype(jnp.int32)

    def place(y, x, core):
        return ((y % 8) * 4 + x % 4) * 2 + core % 2

    sites = [(y, x, core) for y in range(8) for x in range(4) for core in range(2)]
    swap = [(place(y, x, c), place(y, x, 1 - c)) for y, x, c in sites]
    z_fore = [
        (place(y, x, c) * 8 + z, place(y, x, c) * 8 + (z + 1 - 2 * c) % 8)
        for y, x, c in sites
        for z in range(8)
    ]
    y_lines = [[place(y, x, c) for y in range(8)] for x in range(4) for c in range(2)]
    squares = [[place(y, x, c) for x in range(4) for c in range(2)] for y in range(8)]
    pairs = [
        [place(y, 2 * h + x, c) for x in range(2) for c in range(2)]
        for y in range(8)
        for h in range(2)
    ]
    across = [(place(y, x, c), place(y, x + 2, c)) for y, x, c in sites]

    quarter = feats // 4
    (spread,) = call(
        spread_kernel, [((4, rows, quarter), BF)], [SMEM, HBM], [VMEM], pos, tokens,
        scratch=[pltpu.SemaphoreType.DMA((8,))],
    )
    paired = lax.all_to_all(spread, "row", 0, 0, axis_index_groups=pairs)
    (low_part,) = call(
        low_kernel, [((32, quarter), BF)], [VMEM, VMEM], [VMEM], tokens, down_proj.T
    )
    block = jnp.concatenate([paired.reshape(4 * rows, quarter), low_part], axis=0)
    t_parts = ring_of(block, ("row", "col"), z_fore, swap)

    w_both = jnp.concatenate([w_key, w_value], axis=1)
    wide = w_both.shape[1]
    w_own = jnp.concatenate([w_both, lax.ppermute(w_both, "row", across)], axis=0)
    w_all = lax.all_to_all(
        jnp.broadcast_to(w_own, (8,) + w_own.shape), "row", 0, 0, axis_index_groups=y_lines
    )

    shares, low_half = call(
        project_kernel,
        [((4, rows, wide), BF), ((rows, 64), BF)],
        [SMEM] + [HBM] * 9,
        [VMEM] * 2,
        pos, *t_parts, w_all,
        scratch=[
            pltpu.VMEM((8,) + block.shape, BF),
            pltpu.VMEM(w_all.shape, BF),
            pltpu.SemaphoreType.DMA((8,)),
            pltpu.SemaphoreType.DMA,
        ],
        mib=56,
    )
    full_parts = lax.all_to_all(shares, "row", 0, 0, axis_index_groups=pairs)
    pack, gk, gv = call(
        attend_kernel,
        [((8, 80, 128), BF), ((rows, HD), F32), ((rows, HD), F32)],
        [SMEM] + [VMEM] * 4 + [HBM] * 2,
        [VMEM] * 3,
        lengths, full_parts, low_half, up_key, up_value, queries, probes,
        scratch=[
            pltpu.VMEM((rows, feats), BF),
            pltpu.VMEM((rows, feats), BF),
            pltpu.SemaphoreType.DMA((8,)),
        ],
    )
    packs = lax.all_to_all(pack, "col", 0, 0)
    slot = (8, 64 + 8, 2 * HD)
    (terms,) = call(
        weigh_kernel, [(slot, BF)], [SMEM] + [VMEM] * 5, [VMEM],
        lengths, packs, low_half, gk, gv, tokens,
    )
    term_parts = lax.all_to_all(terms, "row", 0, 0, axis_index_groups=squares)
    (square,) = call(sum_kernel, [(slot, BF)], [VMEM], [VMEM], term_parts)
    square_parts = lax.all_to_all(square, "row", 0, 0, axis_index_groups=y_lines)
    (summed,) = call(sum_kernel, [(slot, BF)], [VMEM], [VMEM], square_parts)
    pieces = lax.all_to_all(summed, "row", 0, 0, axis_index_groups=squares)
    grad_down, grad_up_key, grad_up_value = call(
        place_kernel,
        [((64, feats), F32), ((64, HD), F32), ((64, HD), F32)],
        [VMEM], [VMEM] * 3, pieces,
    )
    return grad_down.T, grad_up_key, grad_up_value


def solution(mesh):
    in_specs = (
        P("row", "col"),
        P("row", "col"),
        P("row", "col"),
        P("row", "col"),
        P("row", "col"),
        P("col", None),
        P(None, "col"),
        P(None, "col"),
        P("row", None),
    )
    out_specs = (P("col", None), P(None, "col"), P(None, "col"))
    return jax.shard_map(
        on_device, mesh=mesh, in_specs=in_specs, out_specs=out_specs, check_vma=False
    )
```

```python
import functools
import jax
import jax.numpy as jnp
from jax import lax
from jax.experimental import pallas as pl
from jax.experimental.pallas import tpu as pltpu
from jax.sharding import PartitionSpec as P

HD = 128
QPK = 16
BF = jnp.bfloat16
F32 = jnp.float32
npo_beta = 0.5

VMEM = pl.BlockSpec(memory_space=pltpu.VMEM)
SMEM = pl.BlockSpec(memory_space=pltpu.SMEM)
HBM = pl.BlockSpec(memory_space=pltpu.HBM)

NT = (((1,), (1,)), ((), ()))
TN = (((0,), (0,)), ((), ()))
NN = (((1,), (0,)), ((), ()))


def mm(a, b, dims):
    return lax.dot_general(a, b, dims, preferred_element_type=F32)


def fold(a, rows):
    return jnp.concatenate([a[i:i + rows] for i in range(0, a.shape[0], rows)], axis=1)


def unfold(a, wide):
    return jnp.concatenate([a[:, i:i + wide] for i in range(0, a.shape[1], wide)], axis=0)


def doc_ids(lengths_ref, axis, count, docs):
    places = lax.broadcasted_iota(jnp.int32, (count, count), axis)
    ids = jnp.zeros((count, count), jnp.int32)
    end = 0
    for j in range(docs):
        end = end + lengths_ref[0, j]
        ids = ids + jnp.where(places >= end, 1, 0)
    return ids


def spread_kernel(t_ref, out_ref, sem):
    copies = []
    for slot in range(4):
        for i in range(2):
            at = pl.ds((slot // 2 + 2 * i) * 512 + slot % 2 * 256, 256)
            copies.append(
                pltpu.make_async_copy(
                    t_ref.at[:, at], out_ref.at[slot, :, pl.ds(i * 256, 256)], sem.at[2 * slot + i]
                )
            )
    for c in copies:
        c.start()
    for c in copies:
        c.wait()


def low_kernel(t_ref, down_ref, out_ref):
    out_ref[...] = fold(mm(t_ref[...], down_ref[...], NT), out_ref.shape[0]).astype(BF)


STEPS = (0, 1, 2, 3, -1, -2, -3, 4)


def ring_of(own, axis, fore, swap):
    near, far, crossed = [own], lax.ppermute(own, "row", swap), []
    for _ in range(3):
        near.append(lax.ppermute(near[-1], axis, fore))
        far = lax.ppermute(far, axis, fore)
        crossed.append(lax.ppermute(far, "row", swap))
    return near + crossed + [lax.ppermute(near[3], axis, fore)]


def block_at(pos_ref, step, n):
    return lax.rem(pos_ref[1] + step * (2 * pos_ref[0] - 1) + n, n)


def project_kernel(pos_ref, *refs):
    t_refs, (w_ref, total_ref, low_ref, t_scr, w_scr, t_sem, w_sem) = refs[:7], refs[7:]
    rows = total_ref.shape[0]
    copies = [pltpu.make_async_copy(w_ref, w_scr, w_sem)]
    for j, t_ref in enumerate(t_refs):
        copies.append(pltpu.make_async_copy(t_ref, t_scr.at[j], t_sem.at[j]))
    for c in copies:
        c.start()
    copies[0].wait()
    total = jnp.zeros(total_ref.shape, F32)
    low = jnp.zeros(low_ref.shape, F32)
    for j, step in enumerate(STEPS[:7]):
        copies[1 + j].wait()
        w = w_scr[block_at(pos_ref, step, w_scr.shape[0])]
        total = total + mm(t_scr[j, pl.ds(0, rows)], w, NN)
        low = low + t_scr[j, pl.ds(rows, low.shape[0])].astype(F32)
    total_ref[...] = total
    low_ref[...] = low


def finish_kernel(
    pos_ref, total_ref, low_ref, t_ref, w_ref, out_ref, low_half_ref,
    total_scr, low_scr, t_scr, w_scr, sem,
):
    k = block_at(pos_ref, STEPS[7], w_ref.shape[0])
    pairs = ((t_ref, t_scr), (w_ref.at[k], w_scr), (total_ref, total_scr), (low_ref, low_scr))
    copies = [pltpu.make_async_copy(a, b, sem.at[i]) for i, (a, b) in enumerate(pairs)]
    for c in copies:
        c.start()
    for c in copies:
        c.wait()
    slots, rows, _ = out_ref.shape
    total = total_scr[...] + mm(t_scr[pl.ds(0, slots * rows)], w_scr[...], NN)
    for i in range(slots):
        out_ref[i] = total[i * rows:(i + 1) * rows].astype(BF)
    low = low_scr[...] + t_scr[pl.ds(slots * rows, low_scr.shape[0])].astype(F32)
    low_half_ref[...] = unfold(low, low_half_ref.shape[1]).astype(BF)


def attend_kernel(
    lengths_ref, full_ref, low_ref, upk_ref, upv_ref, q_ref, p_ref,
    pack_ref, gk_ref, gv_ref, q_scr, p_scr, sem,
):
    rows = q_ref.shape[0]
    heads = q_ref.shape[1] // HD
    batch = 4
    copies = []
    for i in range(heads // batch):
        at = pl.ds(i * batch * HD, batch * HD)
        for k, (ref, scr) in enumerate(((q_ref, q_scr), (p_ref, p_scr))):
            copies.append(pltpu.make_async_copy(ref.at[:, at], scr.at[:, at], sem.at[2 * i + k]))
    for c in copies:
        c.start()
    score_scale = HD ** (-0.5)
    probe_scale = (q_ref.shape[1] * pack_ref.shape[0]) ** (-0.5)
    low_half = low_ref[...]
    full = full_ref[0].astype(F32)
    for i in range(1, full_ref.shape[0]):
        full = full + full_ref[i].astype(F32)
    key_full, value_full = full[:, :HD], full[:, HD:]
    key_pol = (key_full + mm(low_half, upk_ref[...], NN)).astype(BF)
    value_pol = (value_full + mm(low_half, upv_ref[...], NN)).astype(BF)
    keys = jnp.concatenate([key_pol, key_full.astype(BF)], axis=0)
    values = jnp.concatenate([value_pol, value_full.astype(BF)], axis=0)
    doc_s = doc_ids(lengths_ref, 0, rows, lengths_ref.shape[1])
    doc_t = doc_ids(lengths_ref, 1, rows, lengths_ref.shape[1])
    s_at = lax.broadcasted_iota(jnp.int32, (rows, rows), 0)
    t_at = lax.broadcasted_iota(jnp.int32, (rows, rows), 1)
    allowed = (doc_s == doc_t) & (t_at >= s_at)

    def probs_of(scores):
        scores = jnp.where(allowed, scores * score_scale, -1e30)
        peak = jnp.max(scores, axis=0, keepdims=True)
        e = jnp.exp(scores - peak)
        return e / jnp.sum(e, axis=0, keepdims=True)

    gk = jnp.zeros((rows, HD), F32)
    gv = jnp.zeros((rows, HD), F32)
    gap = jnp.zeros((1, rows), F32)
    for h in range(heads):
        if h % batch == 0:
            for c in copies[2 * h // batch:2 * h // batch + 2]:
                c.wait()
        q = q_scr[:, pl.ds(h * HD, HD)]
        probe = p_scr[:, pl.ds(h * HD, HD)]
        scores = mm(keys, q, NT)
        grads = mm(values, probe, NT)
        pol = probs_of(scores[:rows])
        ref = probs_of(scores[rows:])
        grad_pol = grads[:rows]
        mean_pol = jnp.sum(pol * grad_pol, axis=0, keepdims=True)
        mean_ref = jnp.sum(ref * grads[rows:], axis=0, keepdims=True)
        gap = gap + (mean_pol - mean_ref)
        grad_scores = (pol * (grad_pol - mean_pol)).astype(BF)
        gk = gk + mm(grad_scores, q, NN)
        gv = gv + mm(pol.astype(BF), probe, NN)
    gk = gk * (score_scale * probe_scale)
    gv = gv * probe_scale
    gap = gap * probe_scale
    gk_ref[...] = gk
    gv_ref[...] = gv
    back = mm(gk.astype(BF), upk_ref[...], NT) + mm(gv.astype(BF), upv_ref[...], NT)
    back = fold(back, 64).astype(BF)
    first = gap.astype(BF).astype(F32)
    second = (gap - first).astype(BF).astype(F32)
    third = gap - first - second
    line = lax.broadcasted_iota(jnp.int32, (16, rows), 0)
    tail = jnp.where(line == 0, first, jnp.where(line == 1, second, jnp.where(line == 2, third, 0.0)))
    tail = tail.astype(BF)
    for i in range(pack_ref.shape[0]):
        pack_ref[i, pl.ds(0, 64)] = back
        pack_ref[i, pl.ds(64, 16)] = tail


def weigh_kernel(lengths_ref, pack_ref, low_half_ref, gk_ref, gv_ref, t_ref, out_ref):
    rows = gk_ref.shape[0]
    total = pack_ref[0].astype(F32)
    for i in range(1, pack_ref.shape[0]):
        total = total + pack_ref[i].astype(F32)
    gap = total[64:65] + total[65:66] + total[66:67]
    docs = lengths_ref.shape[1]
    same = doc_ids(lengths_ref, 0, rows, docs) == doc_ids(lengths_ref, 1, rows, docs)
    token_gap = jnp.sum(jnp.where(same, gap, 0.0), axis=1, keepdims=True)
    weight = 2.0 * jax.nn.sigmoid(npo_beta * token_gap)
    back_half = (unfold(total[:64], 64) * weight).astype(BF)
    down = mm(back_half, t_ref[...], TN).astype(BF)
    both = jnp.concatenate([gk_ref[...] * weight, gv_ref[...] * weight], axis=1).astype(BF)
    up = mm(low_half_ref[...], both, TN).astype(BF)
    slots = out_ref.shape[0]
    wide, deep = t_ref.shape[1] // slots, up.shape[0] // slots
    for j in range(slots):
        out_ref[j, pl.ds(0, 64)] = down[:, j * wide:(j + 1) * wide]
        out_ref[j, pl.ds(64, deep)] = up[j * deep:(j + 1) * deep]


def sum_kernel(in_ref, out_ref):
    total = in_ref[0].astype(F32)
    for i in range(1, in_ref.shape[0]):
        total = total + in_ref[i].astype(F32)
    total = total.astype(BF)
    for i in range(out_ref.shape[0]):
        out_ref[i] = total


def place_kernel(in_ref, down_ref, upk_ref, upv_ref):
    slots, _, wide = in_ref.shape
    deep = upk_ref.shape[0] // slots
    for j in range(slots):
        down_ref[:, pl.ds(j * wide, wide)] = in_ref[j, pl.ds(0, 64)].astype(F32)
        up = in_ref[j, pl.ds(64, deep)].astype(F32)
        upk_ref[pl.ds(j * deep, deep)] = up[:, :HD]
        upv_ref[pl.ds(j * deep, deep)] = up[:, HD:]


def call(kernel, outs, in_specs, out_specs, *args, scratch=(), mib=8, cost=None):
    return pl.pallas_call(
        kernel,
        out_shape=[jax.ShapeDtypeStruct(s, d) for s, d in outs],
        in_specs=in_specs,
        out_specs=out_specs,
        scratch_shapes=list(scratch),
        cost_estimate=cost and pl.CostEstimate(
            flops=cost[0], bytes_accessed=cost[1], transcendentals=0
        ),
        compiler_params=pltpu.CompilerParams(vmem_limit_bytes=mib * 1024 * 1024),
    )(*args)


def on_device(tokens, queries, probes, w_key, w_value, down_proj, up_key, up_value, lengths):
    rows, feats = tokens.shape
    row_at = lax.axis_index("row")
    pos = jnp.stack([row_at % 2, lax.axis_index("col"), row_at // 8]).astype(jnp.int32)

    def place(y, x, core):
        return ((y % 8) * 4 + x % 4) * 2 + core % 2

    sites = [(y, x, core) for y in range(8) for x in range(4) for core in range(2)]
    swap = [(place(y, x, c), place(y, x, 1 - c)) for y, x, c in sites]
    z_fore = [
        (place(y, x, c) * 8 + z, place(y, x, c) * 8 + (z + 1 - 2 * c) % 8)
        for y, x, c in sites
        for z in range(8)
    ]
    y_lines = [[place(y, x, c) for y in range(8)] for x in range(4) for c in range(2)]
    squares = [[place(y, x, c) for x in range(4) for c in range(2)] for y in range(8)]
    pairs = [
        [place(y, 2 * h + x, c) for x in range(2) for c in range(2)]
        for y in range(8)
        for h in range(2)
    ]
    sixteens = [
        [place(y, x + 2 * i, c) for y in range(8) for i in range(2)]
        for x in range(2)
        for c in range(2)
    ]

    quarter = feats // 4
    (spread,) = call(
        spread_kernel, [((4, rows, quarter), BF)], [HBM], [VMEM], tokens,
        scratch=[pltpu.SemaphoreType.DMA((8,))], mib=56,
    )
    paired = lax.all_to_all(spread, "row", 0, 0, axis_index_groups=pairs)
    (low_part,) = call(
        low_kernel, [((16, quarter), BF)], [VMEM, VMEM], [VMEM], tokens, down_proj.T
    )
    block = jnp.concatenate([paired.reshape(4 * rows, quarter), low_part], axis=0)
    t_parts = ring_of(block, ("row", "col"), z_fore, swap)

    w_both = jnp.concatenate([w_key, w_value], axis=1)
    wide = w_both.shape[1]
    w_all = lax.all_to_all(
        jnp.broadcast_to(w_both, (16,) + w_both.shape), "row", 0, 0, axis_index_groups=sixteens
    )
    w_all = w_all.reshape(8, quarter, wide)

    total, low_sum = call(
        project_kernel,
        [((4 * rows, wide), F32), ((16, quarter), F32)],
        [SMEM] + [HBM] * 8,
        [VMEM] * 2,
        pos, *t_parts[:7], w_all,
        scratch=[
            pltpu.VMEM((7,) + block.shape, BF),
            pltpu.VMEM(w_all.shape, BF),
            pltpu.SemaphoreType.DMA((7,)),
            pltpu.SemaphoreType.DMA,
        ],
        mib=52,
        cost=(2 * 28 * rows * quarter * wide, 7 * 2 * block.size + 2 * w_all.size),
    )
    shares, low_half = call(
        finish_kernel,
        [((4, rows, wide), BF), ((rows, 64), BF)],
        [SMEM] + [HBM] * 4,
        [VMEM] * 2,
        pos, total, low_sum, t_parts[7], w_all,
        scratch=[
            pltpu.VMEM(total.shape, F32),
            pltpu.VMEM(low_sum.shape, F32),
            pltpu.VMEM(block.shape, BF),
            pltpu.VMEM((quarter, wide), BF),
            pltpu.SemaphoreType.DMA((4,)),
        ],
        mib=52,
    )
    full_parts = lax.all_to_all(shares, "row", 0, 0, axis_index_groups=pairs)
    pack, gk, gv = call(
        attend_kernel,
        [((8, 80, 128), BF), ((rows, HD), F32), ((rows, HD), F32)],
        [SMEM] + [VMEM] * 4 + [HBM] * 2,
        [VMEM] * 3,
        lengths, full_parts, low_half, up_key, up_value, queries, probes,
        scratch=[
            pltpu.VMEM((rows, feats), BF),
            pltpu.VMEM((rows, feats), BF),
            pltpu.SemaphoreType.DMA((8,)),
        ],
    )
    packs = lax.all_to_all(pack, "col", 0, 0)
    slot = (8, 64 + 8, 2 * HD)
    (terms,) = call(
        weigh_kernel, [(slot, BF)], [SMEM] + [VMEM] * 5, [VMEM],
        lengths, packs, low_half, gk, gv, tokens,
    )
    term_parts = lax.all_to_all(terms, "row", 0, 0, axis_index_groups=squares)
    (square,) = call(sum_kernel, [(slot, BF)], [VMEM], [VMEM], term_parts)
    square_parts = lax.all_to_all(square, "row", 0, 0, axis_index_groups=y_lines)
    (summed,) = call(sum_kernel, [(slot, BF)], [VMEM], [VMEM], square_parts)
    pieces = lax.all_to_all(summed, "row", 0, 0, axis_index_groups=squares)
    grad_down, grad_up_key, grad_up_value = call(
        place_kernel,
        [((64, feats), F32), ((64, HD), F32), ((64, HD), F32)],
        [VMEM], [VMEM] * 3, pieces,
    )
    return grad_down.T, grad_up_key, grad_up_value


def solution(mesh):
    in_specs = (
        P("row", "col"),
        P("row", "col"),
        P("row", "col"),
        P("row", "col"),
        P("row", "col"),
        P("col", None),
        P(None, "col"),
        P(None, "col"),
        P("row", None),
    )
    out_specs = (P("col", None), P(None, "col"), P(None, "col"))
    return jax.shard_map(
        on_device, mesh=mesh, in_specs=in_specs, out_specs=out_specs, check_vma=False
    )
```

```python
import functools
import jax
import jax.numpy as jnp
from jax import lax
from jax.experimental import pallas as pl
from jax.experimental.pallas import tpu as pltpu
from jax.sharding import PartitionSpec as P

HD = 128
QPK = 16
BF = jnp.bfloat16
F32 = jnp.float32
npo_beta = 0.5

VMEM = pl.BlockSpec(memory_space=pltpu.VMEM)
SMEM = pl.BlockSpec(memory_space=pltpu.SMEM)
HBM = pl.BlockSpec(memory_space=pltpu.HBM)

NT = (((1,), (1,)), ((), ()))
TN = (((0,), (0,)), ((), ()))
NN = (((1,), (0,)), ((), ()))


def mm(a, b, dims):
    return lax.dot_general(a, b, dims, preferred_element_type=F32)


def fold(a, rows):
    return jnp.concatenate([a[i:i + rows] for i in range(0, a.shape[0], rows)], axis=1)


def unfold(a, wide):
    return jnp.concatenate([a[:, i:i + wide] for i in range(0, a.shape[1], wide)], axis=0)


def doc_ids(lengths_ref, axis, count, docs):
    places = lax.broadcasted_iota(jnp.int32, (count, count), axis)
    ids = jnp.zeros((count, count), jnp.int32)
    end = 0
    for j in range(docs):
        end = end + lengths_ref[0, j]
        ids = ids + jnp.where(places >= end, 1, 0)
    return ids


def spread_kernel(pos_ref, t_ref, *refs):
    out_refs, sem = refs[:4], refs[4]
    copies = []
    for slot in range(4):
        x = lax.rem(pos_ref[3] + slot // 2, 2)
        core = lax.rem(pos_ref[0] + slot % 2, 2)
        for i in range(2):
            far = lax.rem(pos_ref[4] + i, 2)
            at = pl.ds(pl.multiple_of((x + 2 * far) * 512 + core * 256, 256), 256)
            copies.append(
                pltpu.make_async_copy(
                    t_ref.at[:, at], out_refs[slot].at[:, pl.ds(i * 256, 256)], sem.at[2 * slot + i]
                )
            )
    for c in copies:
        c.start()
    for c in copies:
        c.wait()


def low_kernel(t_ref, down_ref, out_ref):
    out_ref[...] = fold(mm(t_ref[...], down_ref[...], NT), out_ref.shape[0]).astype(BF)


def join_kernel(*refs):
    parts, out_ref = refs[:-1], refs[-1]
    at = 0
    for part in parts:
        out_ref[pl.ds(at, part.shape[0])] = part[...]
        at += part.shape[0]


STEPS = (0, 1, 2, 3, -1, -2, -3, 4)


def ring_of(own, axis, fore, swap):
    near, far, crossed = [own], lax.ppermute(own, "row", swap), []
    for _ in range(3):
        near.append(lax.ppermute(near[-1], axis, fore))
        far = lax.ppermute(far, axis, fore)
        crossed.append(lax.ppermute(far, "row", swap))
    return near + crossed + [lax.ppermute(near[3], axis, fore)]


def block_at(pos_ref, step, n):
    return lax.rem(pos_ref[1] + step * (2 * pos_ref[0] - 1) + n, n)


def project_kernel(pos_ref, *refs):
    t_refs, (w_ref, total_ref, low_ref, t_scr, w_scr, t_sem, w_sem) = refs[:7], refs[7:]
    rows = total_ref.shape[0]
    copies = [pltpu.make_async_copy(w_ref, w_scr, w_sem)]
    for j, t_ref in enumerate(t_refs):
        copies.append(pltpu.make_async_copy(t_ref, t_scr.at[j], t_sem.at[j]))
    for c in copies:
        c.start()
    copies[0].wait()
    total = jnp.zeros(total_ref.shape, F32)
    low = jnp.zeros(low_ref.shape, F32)
    for j, step in enumerate(STEPS[:7]):
        copies[1 + j].wait()
        w = w_scr[block_at(pos_ref, step, w_scr.shape[0])]
        total = total + mm(t_scr[j, pl.ds(0, rows)], w, NN)
        low = low + t_scr[j, pl.ds(rows, low.shape[0])].astype(F32)
    total_ref[...] = total
    low_ref[...] = low


def finish_kernel(
    pos_ref, total_ref, low_ref, t_ref, w_ref, out_ref, low_half_ref,
    total_scr, low_scr, t_scr, w_scr, sem,
):
    k = block_at(pos_ref, STEPS[7], w_ref.shape[0])
    pairs = ((t_ref, t_scr), (w_ref.at[k], w_scr), (total_ref, total_scr), (low_ref, low_scr))
    copies = [pltpu.make_async_copy(a, b, sem.at[i]) for i, (a, b) in enumerate(pairs)]
    for c in copies:
        c.start()
    for c in copies:
        c.wait()
    slots, rows, _ = out_ref.shape
    total = total_scr[...] + mm(t_scr[pl.ds(0, slots * rows)], w_scr[...], NN)
    for i in range(slots):
        x = lax.rem(pos_ref[3] + i // 2, 2)
        core = lax.rem(pos_ref[0] + i % 2, 2)
        out_ref[2 * x + core] = total[i * rows:(i + 1) * rows].astype(BF)
    low = low_scr[...] + t_scr[pl.ds(slots * rows, low_scr.shape[0])].astype(F32)
    low_half_ref[...] = unfold(low, low_half_ref.shape[1]).astype(BF)


def attend_kernel(
    lengths_ref, full_ref, low_ref, upk_ref, upv_ref, q_ref, p_ref,
    pack_ref, gk_ref, gv_ref, q_scr, p_scr, sem,
):
    rows = q_ref.shape[0]
    heads = q_ref.shape[1] // HD
    batch = 4
    copies = []
    for i in range(heads // batch):
        at = pl.ds(i * batch * HD, batch * HD)
        for k, (ref, scr) in enumerate(((q_ref, q_scr), (p_ref, p_scr))):
            copies.append(pltpu.make_async_copy(ref.at[:, at], scr.at[:, at], sem.at[2 * i + k]))
    for c in copies:
        c.start()
    score_scale = HD ** (-0.5)
    probe_scale = (q_ref.shape[1] * pack_ref.shape[0]) ** (-0.5)
    low_half = low_ref[...]
    full = full_ref[0].astype(F32)
    for i in range(1, full_ref.shape[0]):
        full = full + full_ref[i].astype(F32)
    key_full, value_full = full[:, :HD], full[:, HD:]
    key_pol = (key_full + mm(low_half, upk_ref[...], NN)).astype(BF)
    value_pol = (value_full + mm(low_half, upv_ref[...], NN)).astype(BF)
    keys = jnp.concatenate([key_pol, key_full.astype(BF)], axis=0)
    values = jnp.concatenate([value_pol, value_full.astype(BF)], axis=0)
    doc_s = doc_ids(lengths_ref, 0, rows, lengths_ref.shape[1])
    doc_t = doc_ids(lengths_ref, 1, rows, lengths_ref.shape[1])
    s_at = lax.broadcasted_iota(jnp.int32, (rows, rows), 0)
    t_at = lax.broadcasted_iota(jnp.int32, (rows, rows), 1)
    allowed = (doc_s == doc_t) & (t_at >= s_at)

    def probs_of(scores):
        scores = jnp.where(allowed, scores * score_scale, -1e30)
        peak = jnp.max(scores, axis=0, keepdims=True)
        e = jnp.exp(scores - peak)
        return e / jnp.sum(e, axis=0, keepdims=True)

    gk = jnp.zeros((rows, HD), F32)
    gv = jnp.zeros((rows, HD), F32)
    gap = jnp.zeros((1, rows), F32)
    for h in range(heads):
        if h % batch == 0:
            for c in copies[2 * h // batch:2 * h // batch + 2]:
                c.wait()
        q = q_scr[:, pl.ds(h * HD, HD)]
        probe = p_scr[:, pl.ds(h * HD, HD)]
        scores = mm(keys, q, NT)
        grads = mm(values, probe, NT)
        pol = probs_of(scores[:rows])
        ref = probs_of(scores[rows:])
        grad_pol = grads[:rows]
        mean_pol = jnp.sum(pol * grad_pol, axis=0, keepdims=True)
        mean_ref = jnp.sum(ref * grads[rows:], axis=0, keepdims=True)
        gap = gap + (mean_pol - mean_ref)
        grad_scores = (pol * (grad_pol - mean_pol)).astype(BF)
        gk = gk + mm(grad_scores, q, NN)
        gv = gv + mm(pol.astype(BF), probe, NN)
    gk = gk * (score_scale * probe_scale)
    gv = gv * probe_scale
    gap = gap * probe_scale
    gk_ref[...] = gk
    gv_ref[...] = gv
    back = mm(gk.astype(BF), upk_ref[...], NT) + mm(gv.astype(BF), upv_ref[...], NT)
    back = fold(back, 64).astype(BF)
    first = gap.astype(BF).astype(F32)
    second = (gap - first).astype(BF).astype(F32)
    third = gap - first - second
    line = lax.broadcasted_iota(jnp.int32, (16, rows), 0)
    tail = jnp.where(line == 0, first, jnp.where(line == 1, second, jnp.where(line == 2, third, 0.0)))
    tail = tail.astype(BF)
    for i in range(pack_ref.shape[0]):
        pack_ref[i, pl.ds(0, 64)] = back
        pack_ref[i, pl.ds(64, 16)] = tail


def weigh_kernel(lengths_ref, pack_ref, low_half_ref, gk_ref, gv_ref, t_ref, out_ref):
    rows = gk_ref.shape[0]
    total = pack_ref[0].astype(F32)
    for i in range(1, pack_ref.shape[0]):
        total = total + pack_ref[i].astype(F32)
    gap = total[64:65] + total[65:66] + total[66:67]
    docs = lengths_ref.shape[1]
    same = doc_ids(lengths_ref, 0, rows, docs) == doc_ids(lengths_ref, 1, rows, docs)
    token_gap = jnp.sum(jnp.where(same, gap, 0.0), axis=1, keepdims=True)
    weight = 2.0 * jax.nn.sigmoid(npo_beta * token_gap)
    back_half = (unfold(total[:64], 64) * weight).astype(BF)
    down = mm(back_half, t_ref[...], TN).astype(BF)
    both = jnp.concatenate([gk_ref[...] * weight, gv_ref[...] * weight], axis=1).astype(BF)
    up = mm(low_half_ref[...], both, TN).astype(BF)
    slots = out_ref.shape[0]
    wide, deep = t_ref.shape[1] // slots, up.shape[0] // slots
    for j in range(slots):
        out_ref[j, pl.ds(0, 64)] = down[:, j * wide:(j + 1) * wide]
        out_ref[j, pl.ds(64, deep)] = up[j * deep:(j + 1) * deep]


def sum_kernel(in_ref, out_ref):
    total = in_ref[0].astype(F32)
    for i in range(1, in_ref.shape[0]):
        total = total + in_ref[i].astype(F32)
    total = total.astype(BF)
    for i in range(out_ref.shape[0]):
        out_ref[i] = total


def place_kernel(in_ref, down_ref, upk_ref, upv_ref):
    slots, _, wide = in_ref.shape
    deep = upk_ref.shape[0] // slots
    for j in range(slots):
        down_ref[:, pl.ds(j * wide, wide)] = in_ref[j, pl.ds(0, 64)].astype(F32)
        up = in_ref[j, pl.ds(64, deep)].astype(F32)
        upk_ref[pl.ds(j * deep, deep)] = up[:, :HD]
        upv_ref[pl.ds(j * deep, deep)] = up[:, HD:]


def call(kernel, outs, in_specs, out_specs, *args, scratch=(), mib=8, cost=None):
    return pl.pallas_call(
        kernel,
        out_shape=[jax.ShapeDtypeStruct(s, d) for s, d in outs],
        in_specs=in_specs,
        out_specs=out_specs,
        scratch_shapes=list(scratch),
        cost_estimate=cost and pl.CostEstimate(
            flops=cost[0], bytes_accessed=cost[1], transcendentals=0
        ),
        compiler_params=pltpu.CompilerParams(vmem_limit_bytes=mib * 1024 * 1024),
    )(*args)


def on_device(tokens, queries, probes, w_key, w_value, down_proj, up_key, up_value, lengths):
    rows, feats = tokens.shape
    row_at = lax.axis_index("row")
    pos = jnp.stack([row_at % 2, lax.axis_index("col"), row_at // 8, row_at // 2 % 2, row_at // 4 % 2])
    pos = pos.astype(jnp.int32)

    def place(y, x, core):
        return ((y % 8) * 4 + x % 4) * 2 + core % 2

    sites = [(y, x, core) for y in range(8) for x in range(4) for core in range(2)]
    swap = [(place(y, x, c), place(y, x, 1 - c)) for y, x, c in sites]
    z_fore = [
        (place(y, x, c) * 8 + z, place(y, x, c) * 8 + (z + 1 - 2 * c) % 8)
        for y, x, c in sites
        for z in range(8)
    ]
    y_lines = [[place(y, x, c) for y in range(8)] for x in range(4) for c in range(2)]
    squares = [[place(y, x, c) for x in range(4) for c in range(2)] for y in range(8)]
    pairs = [
        [place(y, 2 * h + x, c) for x in range(2) for c in range(2)]
        for y in range(8)
        for h in range(2)
    ]
    beside = [(place(y, x, c), place(y, x ^ 1, c)) for y, x, c in sites]
    across = [(place(y, x, c), place(y, x ^ 1, 1 - c)) for y, x, c in sites]
    opposite = [(place(y, x, c), place(y, x + 2, c)) for y, x, c in sites]
    z_fore = [
        (place(y, x, c) * 8 + z, place(y, x, c) * 8 + (z + 1 - 2 * c) % 8)
        for y, x, c in sites
        for z in range(8)
    ]
    y_lines = [[place(y, x, c) for y in range(8)] for x in range(4) for c in range(2)]
    squares = [[place(y, x, c) for x in range(4) for c in range(2)] for y in range(8)]
    pairs = [
        [place(y, 2 * h + x, c) for x in range(2) for c in range(2)]
        for y in range(8)
        for h in range(2)
    ]
    beside = [(place(y, x, c), place(y, x ^ 1, c)) for y, x, c in sites]
    across = [(place(y, x, c), place(y, x ^ 1, 1 - c)) for y, x, c in sites]
    sixteens = [
        [place(y, x + 2 * i, c) for y in range(8) for i in range(2)]
        for x in range(2)
        for c in range(2)
    ]

    quarter = feats // 4
    mine, *others = call(
        spread_kernel, [((rows, quarter), BF)] * 4, [SMEM, HBM], [VMEM] * 4, pos, tokens,
        scratch=[pltpu.SemaphoreType.DMA((8,))], mib=56,
    )
    paired = [
        lax.ppermute(part, "row", way) for part, way in zip(others, (swap, beside, across))
    ]
    (low_part,) = call(
        low_kernel, [((16, quarter), BF)], [VMEM, VMEM], [VMEM], tokens, down_proj.T
    )

    w_both = jnp.concatenate([w_key, w_value], axis=1)
    wide = w_both.shape[1]
    w_far = lax.ppermute(w_both, "row", opposite)
    paired, w_far = lax.optimization_barrier((paired, w_far))
    (block,) = call(
        join_kernel, [((4 * rows + 16, quarter), BF)], [VMEM] * 5, [VMEM],
        mine, *paired, low_part,
    )
    t_parts = ring_of(block, ("row", "col"), z_fore, swap)
    w_own = jnp.concatenate([w_both, w_far], axis=0)
    w_all = lax.all_to_all(
        jnp.broadcast_to(w_own, (8,) + w_own.shape), "row", 0, 0, axis_index_groups=y_lines
    )

    total, low_sum = call(
        project_kernel,
        [((4 * rows, wide), F32), ((16, quarter), F32)],
        [SMEM] + [HBM] * 8,
        [VMEM] * 2,
        pos, *t_parts[:7], w_all,
        scratch=[
            pltpu.VMEM((7,) + block.shape, BF),
            pltpu.VMEM(w_all.shape, BF),
            pltpu.SemaphoreType.DMA((7,)),
            pltpu.SemaphoreType.DMA,
        ],
        mib=52,
        cost=(2 * 28 * rows * quarter * wide, 7 * 2 * block.size + 2 * w_all.size),
    )
    shares, low_half = call(
        finish_kernel,
        [((4, rows, wide), BF), ((rows, 64), BF)],
        [SMEM] + [HBM] * 4,
        [VMEM] * 2,
        pos, total, low_sum, t_parts[7], w_all,
        scratch=[
            pltpu.VMEM(total.shape, F32),
            pltpu.VMEM(low_sum.shape, F32),
            pltpu.VMEM(block.shape, BF),
            pltpu.VMEM((quarter, wide), BF),
            pltpu.SemaphoreType.DMA((4,)),
        ],
        mib=52,
    )
    full_parts = lax.all_to_all(shares, "row", 0, 0, axis_index_groups=pairs)
    pack, gk, gv = call(
        attend_kernel,
        [((8, 80, 128), BF), ((rows, HD), F32), ((rows, HD), F32)],
        [SMEM] + [VMEM] * 4 + [HBM] * 2,
        [VMEM] * 3,
        lengths, full_parts, low_half, up_key, up_value, queries, probes,
        scratch=[
            pltpu.VMEM((rows, feats), BF),
            pltpu.VMEM((rows, feats), BF),
            pltpu.SemaphoreType.DMA((8,)),
        ],
    )
    packs = lax.all_to_all(pack, "col", 0, 0)
    slot = (8, 64 + 8, 2 * HD)
    (terms,) = call(
        weigh_kernel, [(slot, BF)], [SMEM] + [VMEM] * 5, [VMEM],
        lengths, packs, low_half, gk, gv, tokens,
    )
    term_parts = lax.all_to_all(terms, "row", 0, 0, axis_index_groups=squares)
    (square,) = call(sum_kernel, [(slot, BF)], [VMEM], [VMEM], term_parts)
    square_parts = lax.all_to_all(square, "row", 0, 0, axis_index_groups=y_lines)
    (summed,) = call(sum_kernel, [(slot, BF)], [VMEM], [VMEM], square_parts)
    pieces = lax.all_to_all(summed, "row", 0, 0, axis_index_groups=squares)
    grad_down, grad_up_key, grad_up_value = call(
        place_kernel,
        [((64, feats), F32), ((64, HD), F32), ((64, HD), F32)],
        [VMEM], [VMEM] * 3, pieces,
    )
    return grad_down.T, grad_up_key, grad_up_value


def solution(mesh):
    in_specs = (
        P("row", "col"),
        P("row", "col"),
        P("row", "col"),
        P("row", "col"),
        P("row", "col"),
        P("col", None),
        P(None, "col"),
        P(None, "col"),
        P("row", None),
    )
    out_specs = (P("col", None), P(None, "col"), P(None, "col"))
    return jax.shard_map(
        on_device, mesh=mesh, in_specs=in_specs, out_specs=out_specs, check_vma=False
    )
```

```python
import functools
import jax
import jax.numpy as jnp
from jax import lax
from jax.experimental import pallas as pl
from jax.experimental.pallas import tpu as pltpu
from jax.sharding import PartitionSpec as P

HD = 128
QPK = 16
BF = jnp.bfloat16
F32 = jnp.float32
npo_beta = 0.5
LOG2E = 1.4426950408889634

VMEM = pl.BlockSpec(memory_space=pltpu.VMEM)
SMEM = pl.BlockSpec(memory_space=pltpu.SMEM)
HBM = pl.BlockSpec(memory_space=pltpu.HBM)

NT = (((1,), (1,)), ((), ()))
TN = (((0,), (0,)), ((), ()))
NN = (((1,), (0,)), ((), ()))


def mm(a, b, dims):
    return lax.dot_general(a, b, dims, preferred_element_type=F32)


def fold(a, rows):
    return jnp.concatenate([a[i:i + rows] for i in range(0, a.shape[0], rows)], axis=1)


def unfold(a, wide):
    return jnp.concatenate([a[:, i:i + wide] for i in range(0, a.shape[1], wide)], axis=0)


def doc_ids(lengths_ref, axis, count, docs):
    places = lax.broadcasted_iota(jnp.int32, (count, count), axis)
    ids = jnp.zeros((count, count), jnp.int32)
    end = 0
    for j in range(docs):
        end = end + lengths_ref[0, j]
        ids = ids + jnp.where(places >= end, 1, 0)
    return ids


def split_kernel(pos_ref, t_ref, mine_ref, theirs_ref, sem):
    copies = []
    for i in range(t_ref.shape[1] // 512):
        to = pl.ds(i * 256, 256)
        for k, ref in enumerate((mine_ref, theirs_ref)):
            core = lax.rem(pos_ref[0] + k, 2)
            at = pl.ds(pl.multiple_of(i * 512 + core * 256, 256), 256)
            copies.append(pltpu.make_async_copy(t_ref.at[:, at], ref.at[:, to], sem.at[2 * i + k]))
    for c in copies:
        c.start()
    for c in copies:
        c.wait()


def low_kernel(t_ref, down_ref, out_ref):
    low = mm(t_ref[...], down_ref[...], NT)
    rows, wide = out_ref.shape
    low = fold(low, rows // 2)
    high = low.astype(BF).astype(F32)
    out_ref[...] = jnp.concatenate([high, low - high], axis=0).astype(BF)


STEPS = (0, 1, 2, 3, -1, -2, -3, 4)


def ring_of(own, axis, fore, aft, cut):
    fore_going, aft_going = [own], [own]
    for _ in range(3):
        fore_going.append(lax.ppermute(fore_going[-1], axis, fore))
        aft_going.append(lax.ppermute(aft_going[-1], axis, aft))
    return fore_going + aft_going[1:] + [
        lax.ppermute(fore_going[3][:cut], axis, fore),
        lax.ppermute(aft_going[3][cut:], axis, aft),
    ]


def block_at(pos_ref, axis, step, n):
    return lax.rem(pos_ref[1 + axis] + step * (2 * pos_ref[0] - 1) + n, n)


def project_kernel(pos_ref, *refs):
    t_refs, w_refs, refs = refs[:7], refs[7:14], refs[14:]
    total_ref, low_ref, t_left_ref, w_left_ref, t_scr, w_scr, sem = refs
    n = t_scr.shape[0]
    copies = []
    for axis, (parts, scr) in enumerate(((t_refs, t_scr), (w_refs, w_scr))):
        for j, part in enumerate(parts):
            k = block_at(pos_ref, axis, STEPS[j], n)
            copies.append(pltpu.make_async_copy(part, scr.at[k], sem.at[axis, j]))
    for c in copies:
        c.start()
    t_far, w_far = (block_at(pos_ref, axis, STEPS[7], n) for axis in range(2))
    t_scr[t_far] = jnp.zeros(t_scr.shape[1:], BF)
    w_scr[w_far] = jnp.zeros(w_scr.shape[1:], BF)
    for c in copies:
        c.wait()
    rows = total_ref.shape[0]
    total = jnp.zeros(total_ref.shape, F32)
    low = jnp.zeros(low_ref.shape, F32)
    for k in range(n):
        total = total + mm(t_scr[k, pl.ds(0, rows)], w_scr[k], NN)
        low = low + t_scr[k, pl.ds(rows, low.shape[0])].astype(F32)
    total_ref[...] = total
    low_ref[...] = low
    t_left_ref[...] = t_scr[w_far, pl.ds(0, rows)]
    w_left_ref[...] = w_scr[t_far]


def finish_kernel(
    pos_ref, t1_ref, t2_ref, w1_ref, w2_ref, total_ref, low_ref, t_left_ref, w_left_ref,
    own_ref, other_ref, low_half_ref,
    t_scr, w_scr, total_scr, low_scr, t_left_scr, w_left_scr, sem,
):
    pairs = [
        (t1_ref, t_scr.at[pl.ds(0, t1_ref.shape[0])]),
        (t2_ref, t_scr.at[pl.ds(t1_ref.shape[0], t2_ref.shape[0])]),
        (w1_ref, w_scr.at[pl.ds(0, w1_ref.shape[0])]),
        (w2_ref, w_scr.at[pl.ds(w1_ref.shape[0], w2_ref.shape[0])]),
        (total_ref, total_scr),
        (low_ref, low_scr),
        (t_left_ref, t_left_scr),
        (w_left_ref, w_left_scr),
    ]
    copies = [pltpu.make_async_copy(a, b, sem.at[i]) for i, (a, b) in enumerate(pairs)]
    for c in copies:
        c.start()
    for c in copies:
        c.wait()
    rows = own_ref.shape[0]
    same = pos_ref[1] == pos_ref[2]
    w_late = w_scr[...]
    w_match = jnp.where(same, w_late, w_left_scr[...])
    total = total_scr[...] + mm(t_scr[pl.ds(0, 2 * rows)], w_match, NN)
    total = total + mm(t_left_scr[...], w_late, NN)
    own_ref[...] = total[:rows]
    other_ref[...] = total[rows:]
    low = low_scr[...] + t_scr[pl.ds(2 * rows, low_scr.shape[0])].astype(F32)
    low = low[:low.shape[0] // 2] + low[low.shape[0] // 2:]
    low_half_ref[...] = unfold(low, low_half_ref.shape[1]).astype(BF)


def attend_kernel(
    lengths_ref, own_ref, got_ref, low_ref, upk_ref, upv_ref, q_ref, p_ref,
    pack_ref, gk_ref, gv_ref, q_scr, p_scr, sem,
):
    rows = own_ref.shape[0]
    heads = q_ref.shape[1] // HD
    batch = 4
    copies = []
    for i in range(heads // batch):
        at = pl.ds(i * batch * HD, batch * HD)
        for k, (ref, scr) in enumerate(((q_ref, q_scr), (p_ref, p_scr))):
            copies.append(pltpu.make_async_copy(ref.at[:, at], scr.at[:, at], sem.at[2 * i + k]))
    for c in copies:
        c.start()
    score_scale = HD ** (-0.5)
    probe_scale = (q_ref.shape[1] * pack_ref.shape[0]) ** (-0.5)
    low_half = low_ref[...]
    full = own_ref[...] + got_ref[...]
    key_full, value_full = full[:, :HD], full[:, HD:]
    key_pol = (key_full + mm(low_half, upk_ref[...], NN)).astype(BF)
    value_pol = (value_full + mm(low_half, upv_ref[...], NN)).astype(BF)
    keys = jnp.concatenate([key_pol, key_full.astype(BF)], axis=0)
    values = jnp.concatenate([value_pol, value_full.astype(BF)], axis=0)
    doc_s = doc_ids(lengths_ref, 0, rows, lengths_ref.shape[1])
    doc_t = doc_ids(lengths_ref, 1, rows, lengths_ref.shape[1])
    s_at = lax.broadcasted_iota(jnp.int32, (rows, rows), 0)
    t_at = lax.broadcasted_iota(jnp.int32, (rows, rows), 1)
    allowed = (doc_s == doc_t) & (t_at >= s_at)

    def raised(scores):
        scores = jnp.where(allowed, scores, -1e30)
        peak = jnp.max(scores, axis=0, keepdims=True)
        e = jnp.exp2((scores - peak) * (score_scale * LOG2E))
        return e, 1.0 / jnp.sum(e, axis=0, keepdims=True)

    gk = jnp.zeros((rows, HD), F32)
    gv = jnp.zeros((rows, HD), F32)
    gap = jnp.zeros((1, rows), F32)
    for h in range(heads):
        if h % batch == 0:
            for c in copies[2 * h // batch:2 * h // batch + 2]:
                c.wait()
        q = q_scr[:, pl.ds(h * HD, HD)]
        probe = p_scr[:, pl.ds(h * HD, HD)]
        scores = mm(keys, q, NT)
        grads = mm(values, probe, NT)
        pol, share = raised(scores[:rows])
        pol = pol * share
        ref, share = raised(scores[rows:])
        grad_pol = grads[:rows]
        mean_pol = jnp.sum(pol * grad_pol, axis=0, keepdims=True)
        mean_ref = jnp.sum(ref * grads[rows:], axis=0, keepdims=True) * share
        gap = gap + (mean_pol - mean_ref)
        grad_scores = (pol * (grad_pol - mean_pol)).astype(BF)
        gk = gk + mm(grad_scores, q, NN)
        gv = gv + mm(pol.astype(BF), probe, NN)
    gk = gk * (score_scale * probe_scale)
    gv = gv * probe_scale
    gap = gap * probe_scale
    gk_ref[...] = gk
    gv_ref[...] = gv
    back = mm(gk.astype(BF), upk_ref[...], NT) + mm(gv.astype(BF), upv_ref[...], NT)
    back = fold(back, 64).astype(BF)
    first = gap.astype(BF).astype(F32)
    second = (gap - first).astype(BF).astype(F32)
    third = gap - first - second
    line = lax.broadcasted_iota(jnp.int32, (16, rows), 0)
    tail = jnp.where(line == 0, first, jnp.where(line == 1, second, jnp.where(line == 2, third, 0.0)))
    tail = tail.astype(BF)
    for i in range(pack_ref.shape[0]):
        pack_ref[i, pl.ds(0, 64)] = back
        pack_ref[i, pl.ds(64, 16)] = tail


def weigh_kernel(lengths_ref, pack_ref, low_half_ref, gk_ref, gv_ref, t_ref, out_ref):
    rows = gk_ref.shape[0]
    total = pack_ref[0].astype(F32)
    for i in range(1, pack_ref.shape[0]):
        total = total + pack_ref[i].astype(F32)
    gap = total[64:65] + total[65:66] + total[66:67]
    docs = lengths_ref.shape[1]
    same = doc_ids(lengths_ref, 0, rows, docs) == doc_ids(lengths_ref, 1, rows, docs)
    token_gap = jnp.sum(jnp.where(same, gap, 0.0), axis=1, keepdims=True)
    weight = 2.0 * jax.nn.sigmoid(npo_beta * token_gap)
    back_half = (unfold(total[:64], 64) * weight).astype(BF)
    down = mm(back_half, t_ref[...], TN).astype(BF)
    both = jnp.concatenate([gk_ref[...] * weight, gv_ref[...] * weight], axis=1).astype(BF)
    up = mm(low_half_ref[...], both, TN).astype(BF)
    slots = out_ref.shape[0]
    wide, deep = t_ref.shape[1] // slots, up.shape[0] // slots
    for j in range(slots):
        out_ref[j, pl.ds(0, 64)] = down[:, j * wide:(j + 1) * wide]
        out_ref[j, pl.ds(64, deep)] = up[j * deep:(j + 1) * deep]


def sum_kernel(in_ref, out_ref):
    total = in_ref[0].astype(F32)
    for i in range(1, in_ref.shape[0]):
        total = total + in_ref[i].astype(F32)
    total = total.astype(BF)
    for i in range(out_ref.shape[0]):
        out_ref[i] = total


def place_kernel(in_ref, down_ref, upk_ref, upv_ref):
    slots, _, wide = in_ref.shape
    deep = upk_ref.shape[0] // slots
    for j in range(slots):
        down_ref[:, pl.ds(j * wide, wide)] = in_ref[j, pl.ds(0, 64)].astype(F32)
        up = in_ref[j, pl.ds(64, deep)].astype(F32)
        upk_ref[pl.ds(j * deep, deep)] = up[:, :HD]
        upv_ref[pl.ds(j * deep, deep)] = up[:, HD:]


def call(kernel, outs, in_specs, out_specs, *args, scratch=(), mib=8, cost=None):
    return pl.pallas_call(
        kernel,
        out_shape=[jax.ShapeDtypeStruct(s, d) for s, d in outs],
        in_specs=in_specs,
        out_specs=out_specs,
        scratch_shapes=list(scratch),
        cost_estimate=cost and pl.CostEstimate(
            flops=cost[0], bytes_accessed=cost[1], transcendentals=0
        ),
        compiler_params=pltpu.CompilerParams(vmem_limit_bytes=mib * 1024 * 1024),
    )(*args)


def on_device(tokens, queries, probes, w_key, w_value, down_proj, up_key, up_value, lengths):
    rows, feats = tokens.shape
    row_at = lax.axis_index("row")
    pos = jnp.stack([row_at % 2, lax.axis_index("col"), row_at // 8]).astype(jnp.int32)

    def place(y, x, core):
        return ((y % 8) * 4 + x % 4) * 2 + core % 2

    sites = [(y, x, core) for y in range(8) for x in range(4) for core in range(2)]
    swap = [(place(y, x, c), place(y, x, 1 - c)) for y, x, c in sites]
    y_fore = [(place(y, x, c), place(y + 1 - 2 * c, x, c)) for y, x, c in sites]
    y_aft = [(b, a) for a, b in y_fore]
    z_fore = [
        (place(y, x, c) * 8 + z, place(y, x, c) * 8 + (z + 1 - 2 * c) % 8)
        for y, x, c in sites
        for z in range(8)
    ]
    z_aft = [(b, a) for a, b in z_fore]
    y_lines = [[place(y, x, c) for y in range(8)] for x in range(4) for c in range(2)]
    squares = [[place(y, x, c) for x in range(4) for c in range(2)] for y in range(8)]
    x_lines = [[place(y, x, c) for x in range(4)] for y in range(8) for c in range(2)]

    half = (rows, feats // 2)
    mine, theirs = call(
        split_kernel, [(half, BF), (half, BF)], [SMEM, HBM], [VMEM, VMEM], pos, tokens,
        scratch=[pltpu.SemaphoreType.DMA((feats // 256,))],
    )
    swapped = lax.ppermute(theirs, "row", swap)
    (low_part,) = call(
        low_kernel, [((16, feats // 2), BF)], [VMEM, VMEM], [VMEM], tokens, down_proj.T
    )
    pair = jnp.concatenate([mine, swapped, low_part], axis=0)

    w_both = jnp.concatenate([w_key, w_value], axis=1)
    wide = w_both.shape[1]
    w_line = lax.all_to_all(
        jnp.broadcast_to(w_both, (4,) + w_both.shape), "row", 0, 0, axis_index_groups=x_lines
    )
    w_own = w_line.reshape(feats // 2, wide)
    t_parts = ring_of(pair, ("row", "col"), z_fore, z_aft, rows)
    w_parts = ring_of(w_own, "row", y_fore, y_aft, feats // 4)

    deep = feats // 2
    total, low_sum, t_left, w_left = call(
        project_kernel,
        [((2 * rows, wide), F32), ((16, deep), F32), ((2 * rows, deep), BF), (w_own.shape, BF)],
        [SMEM] + [HBM] * 14,
        [VMEM] * 4,
        pos, *t_parts[:7], *w_parts[:7],
        scratch=[
            pltpu.VMEM((8,) + pair.shape, BF),
            pltpu.VMEM((8,) + w_own.shape, BF),
            pltpu.SemaphoreType.DMA((2, 7)),
        ],
        mib=52,
        cost=(2 * 16 * rows * deep * wide, 14 * (pair.size + w_own.size)),
    )
    own, other, low_half = call(
        finish_kernel,
        [((rows, wide), F32), ((rows, wide), F32), ((rows, 64), BF)],
        [SMEM] + [HBM] * 8,
        [VMEM] * 3,
        pos, *t_parts[7:], *w_parts[7:], total, low_sum, t_left, w_left,
        scratch=[
            pltpu.VMEM(pair.shape, BF),
            pltpu.VMEM(w_own.shape, BF),
            pltpu.VMEM(total.shape, F32),
            pltpu.VMEM(low_sum.shape, F32),
            pltpu.VMEM(t_left.shape, BF),
            pltpu.VMEM(w_left.shape, BF),
            pltpu.SemaphoreType.DMA((8,)),
        ],
        mib=52,
    )
    got = lax.ppermute(other, "row", swap)
    pack, gk, gv = call(
        attend_kernel,
        [((8, 80, 128), BF), ((rows, HD), F32), ((rows, HD), F32)],
        [SMEM] + [VMEM] * 5 + [HBM] * 2,
        [VMEM] * 3,
        lengths, own, got, low_half, up_key, up_value, queries, probes,
        scratch=[
            pltpu.VMEM((rows, feats), BF),
            pltpu.VMEM((rows, feats), BF),
            pltpu.SemaphoreType.DMA((8,)),
        ],
    )
    packs = lax.all_to_all(pack, "col", 0, 0)
    slot = (8, 64 + 8, 2 * HD)
    (terms,) = call(
        weigh_kernel, [(slot, BF)], [SMEM] + [VMEM] * 5, [VMEM],
        lengths, packs, low_half, gk, gv, tokens,
    )
    term_parts = lax.all_to_all(terms, "row", 0, 0, axis_index_groups=squares)
    (square,) = call(sum_kernel, [(slot, BF)], [VMEM], [VMEM], term_parts)
    square_parts = lax.all_to_all(square, "row", 0, 0, axis_index_groups=y_lines)
    (summed,) = call(sum_kernel, [(slot, BF)], [VMEM], [VMEM], square_parts)
    pieces = lax.all_to_all(summed, "row", 0, 0, axis_index_groups=squares)
    grad_down, grad_up_key, grad_up_value = call(
        place_kernel,
        [((64, feats), F32), ((64, HD), F32), ((64, HD), F32)],
        [VMEM], [VMEM] * 3, pieces,
    )
    return grad_down.T, grad_up_key, grad_up_value


def solution(mesh):
    in_specs = (
        P("row", "col"),
        P("row", "col"),
        P("row", "col"),
        P("row", "col"),
        P("row", "col"),
        P("col", None),
        P(None, "col"),
        P(None, "col"),
        P("row", None),
    )
    out_specs = (P("col", None), P(None, "col"), P(None, "col"))
    return jax.shard_map(
        on_device, mesh=mesh, in_specs=in_specs, out_specs=out_specs, check_vma=False
    )
```

```python
import functools
import jax
import jax.numpy as jnp
from jax import lax
from jax.experimental import pallas as pl
from jax.experimental.pallas import tpu as pltpu
from jax.sharding import PartitionSpec as P

HD = 128
QPK = 16
BF = jnp.bfloat16
F32 = jnp.float32
npo_beta = 0.5
LOG2E = 1.4426950408889634

VMEM = pl.BlockSpec(memory_space=pltpu.VMEM)
SMEM = pl.BlockSpec(memory_space=pltpu.SMEM)
HBM = pl.BlockSpec(memory_space=pltpu.HBM)

NT = (((1,), (1,)), ((), ()))
TN = (((0,), (0,)), ((), ()))
NN = (((1,), (0,)), ((), ()))


def mm(a, b, dims):
    return lax.dot_general(a, b, dims, preferred_element_type=F32)


def fold(a, rows):
    return jnp.concatenate([a[i:i + rows] for i in range(0, a.shape[0], rows)], axis=1)


def unfold(a, wide):
    return jnp.concatenate([a[:, i:i + wide] for i in range(0, a.shape[1], wide)], axis=0)


def doc_ids(lengths_ref, axis, count, docs):
    places = lax.broadcasted_iota(jnp.int32, (count, count), axis)
    ids = jnp.zeros((count, count), jnp.int32)
    end = 0
    for j in range(docs):
        end = end + lengths_ref[0, j]
        ids = ids + jnp.where(places >= end, 1, 0)
    return ids


def split_kernel(pos_ref, t_ref, mine_ref, theirs_ref, sem):
    copies = []
    for i in range(t_ref.shape[1] // 512):
        to = pl.ds(i * 256, 256)
        for k, ref in enumerate((mine_ref, theirs_ref)):
            core = lax.rem(pos_ref[0] + k, 2)
            at = pl.ds(pl.multiple_of(i * 512 + core * 256, 256), 256)
            copies.append(pltpu.make_async_copy(t_ref.at[:, at], ref.at[:, to], sem.at[2 * i + k]))
    for c in copies:
        c.start()
    for c in copies:
        c.wait()


def low_kernel(t_ref, down_ref, out_ref):
    low = mm(t_ref[...], down_ref[...], NT)
    rows, wide = out_ref.shape
    low = fold(low, rows // 2)
    high = low.astype(BF).astype(F32)
    out_ref[...] = jnp.concatenate([high, low - high], axis=0).astype(BF)


STEPS = (0, 1, 2, 3, -1, -2, -3, 4)


def rings_of(owns, axes, fores, afts, cuts):
    both = range(2)
    going = [list(owns), list(owns)]
    blocks = [[[own] for own in owns] for _ in going]
    for step in range(4):
        for side, ways in enumerate((fores, afts)):
            now = going[side]
            if step == 0 and side == 1:
                now = lax.optimization_barrier(tuple(now))
            if step == 3:
                now = [now[i][:cuts[i]] if side == 0 else now[i][cuts[i]:] for i in both]
            going[side] = [lax.ppermute(now[i], axes[i], ways[i]) for i in both]
            for i in both:
                blocks[side][i].append(going[side][i])
    return [blocks[0][i][:4] + blocks[1][i][1:4] + [blocks[0][i][4], blocks[1][i][4]] for i in both]


def block_at(pos_ref, axis, step, n):
    return lax.rem(pos_ref[1 + axis] + step * (2 * pos_ref[0] - 1) + n, n)


def project_kernel(pos_ref, *refs):
    t_refs, w_refs, refs = refs[:7], refs[7:14], refs[14:]
    total_ref, low_ref, t_left_ref, w_left_ref, t_scr, w_scr, sem = refs
    n = t_scr.shape[0]
    copies = []
    for axis, (parts, scr) in enumerate(((t_refs, t_scr), (w_refs, w_scr))):
        for j, part in enumerate(parts):
            k = block_at(pos_ref, axis, STEPS[j], n)
            copies.append(pltpu.make_async_copy(part, scr.at[k], sem.at[axis, j]))
    for c in copies:
        c.start()
    t_far, w_far = (block_at(pos_ref, axis, STEPS[7], n) for axis in range(2))
    t_scr[t_far] = jnp.zeros(t_scr.shape[1:], BF)
    w_scr[w_far] = jnp.zeros(w_scr.shape[1:], BF)
    for c in copies:
        c.wait()
    rows = total_ref.shape[0]
    left = [
        pltpu.make_async_copy(t_scr.at[w_far, pl.ds(0, rows)], t_left_ref, sem.at[0, 7]),
        pltpu.make_async_copy(w_scr.at[t_far], w_left_ref, sem.at[1, 7]),
    ]
    for c in left:
        c.start()
    total = jnp.zeros(total_ref.shape, F32)
    low = jnp.zeros(low_ref.shape, F32)
    for k in range(n):
        total = total + mm(t_scr[k, pl.ds(0, rows)], w_scr[k, pl.ds(0, t_scr.shape[2])], NN)
        low = low + t_scr[k, pl.ds(rows, low.shape[0])].astype(F32)
    total_ref[...] = total
    low_ref[...] = low
    for c in left:
        c.wait()


def finish_kernel(
    pos_ref, t1_ref, t2_ref, w1_ref, w2_ref, total_ref, low_ref, t_left_ref, w_left_ref,
    own_ref, other_ref, low_half_ref,
    t_scr, w_scr, total_scr, low_scr, t_left_scr, w_left_scr, sem,
):
    pairs = [
        (t1_ref, t_scr.at[pl.ds(0, t1_ref.shape[0])]),
        (t2_ref, t_scr.at[pl.ds(t1_ref.shape[0], t2_ref.shape[0])]),
        (w1_ref, w_scr.at[pl.ds(0, w1_ref.shape[0])]),
        (w2_ref, w_scr.at[pl.ds(w1_ref.shape[0], w2_ref.shape[0])]),
        (total_ref, total_scr),
        (low_ref, low_scr),
        (t_left_ref, t_left_scr),
        (w_left_ref, w_left_scr),
    ]
    copies = [pltpu.make_async_copy(a, b, sem.at[i]) for i, (a, b) in enumerate(pairs)]
    for c in copies:
        c.start()
    for c in copies:
        c.wait()
    rows = own_ref.shape[0]
    same = pos_ref[1] == pos_ref[2]
    w_late = w_scr[pl.ds(0, t_left_scr.shape[1])]
    w_match = jnp.where(same, w_late, w_left_scr[pl.ds(0, t_left_scr.shape[1])])
    total = total_scr[...] + mm(t_scr[pl.ds(0, 2 * rows)], w_match, NN)
    total = total + mm(t_left_scr[...], w_late, NN)
    own_ref[...] = total[:rows]
    other_ref[...] = total[rows:]
    low = low_scr[...] + t_scr[pl.ds(2 * rows, low_scr.shape[0])].astype(F32)
    low = low[:low.shape[0] // 2] + low[low.shape[0] // 2:]
    low_half_ref[...] = unfold(low, low_half_ref.shape[1]).astype(BF)


def attend_kernel(
    lengths_ref, own_ref, got_ref, low_ref, upk_ref, upv_ref, q_ref, p_ref,
    pack_ref, gk_ref, gv_ref, q_scr, p_scr, sem,
):
    rows = own_ref.shape[0]
    heads = q_ref.shape[1] // HD
    batch = 4
    copies = []
    for i in range(heads // batch):
        at = pl.ds(i * batch * HD, batch * HD)
        for k, (ref, scr) in enumerate(((q_ref, q_scr), (p_ref, p_scr))):
            copies.append(pltpu.make_async_copy(ref.at[:, at], scr.at[:, at], sem.at[2 * i + k]))
    for c in copies:
        c.start()
    score_scale = HD ** (-0.5)
    probe_scale = (q_ref.shape[1] * pack_ref.shape[0]) ** (-0.5)
    low_half = low_ref[...]
    full = own_ref[...] + got_ref[...]
    key_full, value_full = full[:, :HD], full[:, HD:]
    key_pol = (key_full + mm(low_half, upk_ref[...], NN)).astype(BF)
    value_pol = (value_full + mm(low_half, upv_ref[...], NN)).astype(BF)
    keys = jnp.concatenate([key_pol, key_full.astype(BF)], axis=0)
    values = jnp.concatenate([value_pol, value_full.astype(BF)], axis=0)
    doc_s = doc_ids(lengths_ref, 0, rows, lengths_ref.shape[1])
    doc_t = doc_ids(lengths_ref, 1, rows, lengths_ref.shape[1])
    s_at = lax.broadcasted_iota(jnp.int32, (rows, rows), 0)
    t_at = lax.broadcasted_iota(jnp.int32, (rows, rows), 1)
    allowed = (doc_s == doc_t) & (t_at >= s_at)

    def raised(scores):
        scores = jnp.where(allowed, scores, -1e30)
        peak = jnp.max(scores, axis=0, keepdims=True)
        e = jnp.exp2((scores - peak) * (score_scale * LOG2E))
        return e, 1.0 / jnp.sum(e, axis=0, keepdims=True)

    gk = jnp.zeros((rows, HD), F32)
    gv = jnp.zeros((rows, HD), F32)
    gap = jnp.zeros((1, rows), F32)
    for h in range(heads):
        if h % batch == 0:
            for c in copies[2 * h // batch:2 * h // batch + 2]:
                c.wait()
        q = q_scr[:, pl.ds(h * HD, HD)]
        probe = p_scr[:, pl.ds(h * HD, HD)]
        scores = mm(keys, q, NT)
        grads = mm(values, probe, NT)
        pol, share = raised(scores[:rows])
        pol = pol * share
        ref, share = raised(scores[rows:])
        grad_pol = grads[:rows]
        mean_pol = jnp.sum(pol * grad_pol, axis=0, keepdims=True)
        mean_ref = jnp.sum(ref * grads[rows:], axis=0, keepdims=True) * share
        gap = gap + (mean_pol - mean_ref)
        grad_scores = (pol * (grad_pol - mean_pol)).astype(BF)
        gk = gk + mm(grad_scores, q, NN)
        gv = gv + mm(pol.astype(BF), probe, NN)
    gk = gk * (score_scale * probe_scale)
    gv = gv * probe_scale
    gap = gap * probe_scale
    gk_ref[...] = gk
    gv_ref[...] = gv
    back = mm(gk.astype(BF), upk_ref[...], NT) + mm(gv.astype(BF), upv_ref[...], NT)
    back = fold(back, 64).astype(BF)
    first = gap.astype(BF).astype(F32)
    second = (gap - first).astype(BF).astype(F32)
    third = gap - first - second
    line = lax.broadcasted_iota(jnp.int32, (16, rows), 0)
    tail = jnp.where(line == 0, first, jnp.where(line == 1, second, jnp.where(line == 2, third, 0.0)))
    tail = tail.astype(BF)
    for i in range(pack_ref.shape[0]):
        pack_ref[i, pl.ds(0, 64)] = back
        pack_ref[i, pl.ds(64, 16)] = tail


def weigh_kernel(lengths_ref, pack_ref, low_half_ref, gk_ref, gv_ref, t_ref, out_ref):
    rows = gk_ref.shape[0]
    total = pack_ref[0].astype(F32)
    for i in range(1, pack_ref.shape[0]):
        total = total + pack_ref[i].astype(F32)
    gap = total[64:65] + total[65:66] + total[66:67]
    docs = lengths_ref.shape[1]
    same = doc_ids(lengths_ref, 0, rows, docs) == doc_ids(lengths_ref, 1, rows, docs)
    token_gap = jnp.sum(jnp.where(same, gap, 0.0), axis=1, keepdims=True)
    weight = 2.0 * jax.nn.sigmoid(npo_beta * token_gap)
    back_half = (unfold(total[:64], 64) * weight).astype(BF)
    down = mm(back_half, t_ref[...], TN).astype(BF)
    both = jnp.concatenate([gk_ref[...] * weight, gv_ref[...] * weight], axis=1).astype(BF)
    up = mm(low_half_ref[...], both, TN).astype(BF)
    slots = out_ref.shape[0]
    wide, deep = t_ref.shape[1] // slots, up.shape[0] // slots
    for j in range(slots):
        out_ref[j, pl.ds(0, 64)] = down[:, j * wide:(j + 1) * wide]
        out_ref[j, pl.ds(64, deep)] = up[j * deep:(j + 1) * deep]


def sum_kernel(in_ref, out_ref):
    total = in_ref[0].astype(F32)
    for i in range(1, in_ref.shape[0]):
        total = total + in_ref[i].astype(F32)
    total = total.astype(BF)
    for i in range(out_ref.shape[0]):
        out_ref[i] = total


def place_kernel(in_ref, down_ref, upk_ref, upv_ref):
    slots, _, wide = in_ref.shape
    deep = upk_ref.shape[0] // slots
    for j in range(slots):
        down_ref[:, pl.ds(j * wide, wide)] = in_ref[j, pl.ds(0, 64)].astype(F32)
        up = in_ref[j, pl.ds(64, deep)].astype(F32)
        upk_ref[pl.ds(j * deep, deep)] = up[:, :HD]
        upv_ref[pl.ds(j * deep, deep)] = up[:, HD:]


def call(kernel, outs, in_specs, out_specs, *args, scratch=(), mib=8, cost=None):
    return pl.pallas_call(
        kernel,
        out_shape=[jax.ShapeDtypeStruct(s, d) for s, d in outs],
        in_specs=in_specs,
        out_specs=out_specs,
        scratch_shapes=list(scratch),
        cost_estimate=cost and pl.CostEstimate(
            flops=cost[0], bytes_accessed=cost[1], transcendentals=0
        ),
        compiler_params=pltpu.CompilerParams(vmem_limit_bytes=mib * 1024 * 1024),
    )(*args)


def on_device(tokens, queries, probes, w_key, w_value, down_proj, up_key, up_value, lengths):
    rows, feats = tokens.shape
    row_at = lax.axis_index("row")
    pos = jnp.stack([row_at % 2, lax.axis_index("col"), row_at // 8]).astype(jnp.int32)

    def place(y, x, core):
        return ((y % 8) * 4 + x % 4) * 2 + core % 2

    sites = [(y, x, core) for y in range(8) for x in range(4) for core in range(2)]
    swap = [(place(y, x, c), place(y, x, 1 - c)) for y, x, c in sites]
    y_fore = [(place(y, x, c), place(y + 1 - 2 * c, x, c)) for y, x, c in sites]
    y_aft = [(b, a) for a, b in y_fore]
    z_fore = [
        (place(y, x, c) * 8 + z, place(y, x, c) * 8 + (z + 1 - 2 * c) % 8)
        for y, x, c in sites
        for z in range(8)
    ]
    z_aft = [(b, a) for a, b in z_fore]
    y_lines = [[place(y, x, c) for y in range(8)] for x in range(4) for c in range(2)]
    squares = [[place(y, x, c) for x in range(4) for c in range(2)] for y in range(8)]
    x_lines = [[place(y, x, c) for x in range(4)] for y in range(8) for c in range(2)]

    half = (rows, feats // 2)
    mine, theirs = call(
        split_kernel, [(half, BF), (half, BF)], [SMEM, HBM], [VMEM, VMEM], pos, tokens,
        scratch=[pltpu.SemaphoreType.DMA((feats // 256,))],
    )
    swapped = lax.ppermute(theirs, "row", swap)
    (low_part,) = call(
        low_kernel, [((16, feats // 2), BF)], [VMEM, VMEM], [VMEM], tokens, down_proj.T
    )
    pair = jnp.concatenate([mine, swapped, low_part], axis=0)

    w_both = jnp.concatenate([w_key, w_value], axis=1)
    wide = w_both.shape[1]
    w_line = lax.all_to_all(
        jnp.broadcast_to(w_both, (4,) + w_both.shape), "row", 0, 0, axis_index_groups=x_lines
    )
    w_own = w_line.reshape(feats // 2, wide)
    w_own = jnp.pad(w_own, ((0, pair.size // wide - w_own.shape[0]), (0, 0)))
    t_parts, w_parts = rings_of(
        (pair, w_own), (("row", "col"), "row"), (z_fore, y_fore), (z_aft, y_aft),
        (rows, w_own.shape[0] // 2),
    )

    deep = feats // 2
    total, low_sum, t_left, w_left = call(
        project_kernel,
        [((2 * rows, wide), F32), ((16, deep), F32), ((2 * rows, deep), BF), (w_own.shape, BF)],
        [SMEM] + [HBM] * 14,
        [VMEM] * 2 + [HBM] * 2,
        pos, *t_parts[:7], *w_parts[:7],
        scratch=[
            pltpu.VMEM((8,) + pair.shape, BF),
            pltpu.VMEM((8,) + w_own.shape, BF),
            pltpu.SemaphoreType.DMA((2, 8)),
        ],
        mib=52,
        cost=(2 * 16 * rows * deep * wide, 14 * (pair.size + w_own.size)),
    )
    own, other, low_half = call(
        finish_kernel,
        [((rows, wide), F32), ((rows, wide), F32), ((rows, 64), BF)],
        [SMEM] + [HBM] * 8,
        [VMEM] * 3,
        pos, *t_parts[7:], *w_parts[7:], total, low_sum, t_left, w_left,
        scratch=[
            pltpu.VMEM(pair.shape, BF),
            pltpu.VMEM(w_own.shape, BF),
            pltpu.VMEM(total.shape, F32),
            pltpu.VMEM(low_sum.shape, F32),
            pltpu.VMEM(t_left.shape, BF),
            pltpu.VMEM(w_left.shape, BF),
            pltpu.SemaphoreType.DMA((8,)),
        ],
        mib=52,
    )
    got = lax.ppermute(other, "row", swap)
    pack, gk, gv = call(
        attend_kernel,
        [((8, 80, 128), BF), ((rows, HD), F32), ((rows, HD), F32)],
        [SMEM] + [VMEM] * 5 + [HBM] * 2,
        [VMEM] * 3,
        lengths, own, got, low_half, up_key, up_value, queries, probes,
        scratch=[
            pltpu.VMEM((rows, feats), BF),
            pltpu.VMEM((rows, feats), BF),
            pltpu.SemaphoreType.DMA((8,)),
        ],
    )
    packs = lax.all_to_all(pack, "col", 0, 0)
    slot = (8, 64 + 8, 2 * HD)
    (terms,) = call(
        weigh_kernel, [(slot, BF)], [SMEM] + [VMEM] * 5, [VMEM],
        lengths, packs, low_half, gk, gv, tokens,
    )
    term_parts = lax.all_to_all(terms, "row", 0, 0, axis_index_groups=squares)
    (square,) = call(sum_kernel, [(slot, BF)], [VMEM], [VMEM], term_parts)
    square_parts = lax.all_to_all(square, "row", 0, 0, axis_index_groups=y_lines)
    (summed,) = call(sum_kernel, [(slot, BF)], [VMEM], [VMEM], square_parts)
    pieces = lax.all_to_all(summed, "row", 0, 0, axis_index_groups=squares)
    grad_down, grad_up_key, grad_up_value = call(
        place_kernel,
        [((64, feats), F32), ((64, HD), F32), ((64, HD), F32)],
        [VMEM], [VMEM] * 3, pieces,
    )
    return grad_down.T, grad_up_key, grad_up_value


def solution(mesh):
    in_specs = (
        P("row", "col"),
        P("row", "col"),
        P("row", "col"),
        P("row", "col"),
        P("row", "col"),
        P("col", None),
        P(None, "col"),
        P(None, "col"),
        P("row", None),
    )
    out_specs = (P("col", None), P(None, "col"), P(None, "col"))
    return jax.shard_map(
        on_device, mesh=mesh, in_specs=in_specs, out_specs=out_specs, check_vma=False
    )
```

```python
import functools
import jax
import jax.numpy as jnp
from jax import lax
from jax.experimental import pallas as pl
from jax.experimental.pallas import tpu as pltpu
from jax.sharding import PartitionSpec as P

HD = 128
QPK = 16
BF = jnp.bfloat16
F32 = jnp.float32
npo_beta = 0.5
LOG2E = 1.4426950408889634

VMEM = pl.BlockSpec(memory_space=pltpu.VMEM)
SMEM = pl.BlockSpec(memory_space=pltpu.SMEM)
HBM = pl.BlockSpec(memory_space=pltpu.HBM)

NT = (((1,), (1,)), ((), ()))
TN = (((0,), (0,)), ((), ()))
NN = (((1,), (0,)), ((), ()))


def mm(a, b, dims):
    return lax.dot_general(a, b, dims, preferred_element_type=F32)


def fold(a, rows):
    return jnp.concatenate([a[i:i + rows] for i in range(0, a.shape[0], rows)], axis=1)


def unfold(a, wide):
    return jnp.concatenate([a[:, i:i + wide] for i in range(0, a.shape[1], wide)], axis=0)


def doc_ids(lengths_ref, axis, count, docs):
    places = lax.broadcasted_iota(jnp.int32, (count, count), axis)
    ids = jnp.zeros((count, count), jnp.int32)
    end = 0
    for j in range(docs):
        end = end + lengths_ref[0, j]
        ids = ids + jnp.where(places >= end, 1, 0)
    return ids


def split_kernel(pos_ref, t_ref, mine_ref, theirs_ref, sem):
    copies = []
    for i in range(t_ref.shape[1] // 512):
        to = pl.ds(i * 256, 256)
        for k, ref in enumerate((mine_ref, theirs_ref)):
            core = lax.rem(pos_ref[0] + k, 2)
            at = pl.ds(pl.multiple_of(i * 512 + core * 256, 256), 256)
            copies.append(pltpu.make_async_copy(t_ref.at[:, at], ref.at[:, to], sem.at[2 * i + k]))
    for c in copies:
        c.start()
    for c in copies:
        c.wait()


def low_kernel(t_ref, down_ref, out_ref):
    low = mm(t_ref[...], down_ref[...], NT)
    rows, wide = out_ref.shape
    low = fold(low, rows // 2)
    high = low.astype(BF).astype(F32)
    out_ref[...] = jnp.concatenate([high, low - high], axis=0).astype(BF)


STEPS = (0, 1, 2, 3, -1, -2, -3, 4)


def ring_of(own, axis, fore, aft, cut):
    fore_going, aft_going = [own], [own]
    for _ in range(3):
        fore_going.append(lax.ppermute(fore_going[-1], axis, fore))
        aft_going.append(lax.ppermute(aft_going[-1], axis, aft))
    return fore_going + aft_going[1:] + [
        lax.ppermute(fore_going[3][:cut], axis, fore),
        lax.ppermute(aft_going[3][cut:], axis, aft),
    ]


def block_at(pos_ref, axis, step, n):
    return lax.rem(pos_ref[1 + axis] + step * (2 * pos_ref[0] - 1) + n, n)


def project_kernel(pos_ref, *refs):
    t_refs, w_refs, refs = refs[:7], refs[7:14], refs[14:]
    total_ref, low_ref, t_left_ref, w_left_ref, t_scr, w_scr, sem = refs
    n = t_scr.shape[0]
    copies = []
    for axis, (parts, scr) in enumerate(((t_refs, t_scr), (w_refs, w_scr))):
        for j, part in enumerate(parts):
            k = block_at(pos_ref, axis, STEPS[j], n)
            copies.append(pltpu.make_async_copy(part, scr.at[k], sem.at[axis, j]))
    for c in copies:
        c.start()
    t_far, w_far = (block_at(pos_ref, axis, STEPS[7], n) for axis in range(2))
    t_scr[t_far] = jnp.zeros(t_scr.shape[1:], BF)
    w_scr[w_far] = jnp.zeros(w_scr.shape[1:], BF)
    for c in copies:
        c.wait()
    rows = total_ref.shape[0]
    total = jnp.zeros(total_ref.shape, F32)
    low = jnp.zeros(low_ref.shape, F32)
    for k in range(n):
        total = total + mm(t_scr[k, pl.ds(0, rows)], w_scr[k], NN)
        low = low + t_scr[k, pl.ds(rows, low.shape[0])].astype(F32)
    total_ref[...] = total
    low_ref[...] = low
    t_left_ref[...] = t_scr[w_far, pl.ds(0, rows)]
    w_left_ref[...] = w_scr[t_far]


def finish_kernel(
    pos_ref, t1_ref, t2_ref, w1_ref, w2_ref, total_ref, low_ref, t_left_ref, w_left_ref,
    own_ref, other_ref, low_half_ref,
    t_scr, w_scr, total_scr, low_scr, t_left_scr, w_left_scr, sem,
):
    pairs = [
        (t1_ref, t_scr.at[pl.ds(0, t1_ref.shape[0])]),
        (t2_ref, t_scr.at[pl.ds(t1_ref.shape[0], t2_ref.shape[0])]),
        (w1_ref, w_scr.at[pl.ds(0, w1_ref.shape[0])]),
        (w2_ref, w_scr.at[pl.ds(w1_ref.shape[0], w2_ref.shape[0])]),
        (total_ref, total_scr),
        (low_ref, low_scr),
        (t_left_ref, t_left_scr),
        (w_left_ref, w_left_scr),
    ]
    copies = [pltpu.make_async_copy(a, b, sem.at[i]) for i, (a, b) in enumerate(pairs)]
    for c in copies:
        c.start()
    for c in copies:
        c.wait()
    rows = own_ref.shape[0]
    same = pos_ref[1] == pos_ref[2]
    w_late = w_scr[...]
    w_match = jnp.where(same, w_late, w_left_scr[...])
    total = total_scr[...] + mm(t_scr[pl.ds(0, 2 * rows)], w_match, NN)
    total = total + mm(t_left_scr[...], w_late, NN)
    own_ref[...] = total[:rows]
    other_ref[...] = total[rows:]
    low = low_scr[...] + t_scr[pl.ds(2 * rows, low_scr.shape[0])].astype(F32)
    low = low[:low.shape[0] // 2] + low[low.shape[0] // 2:]
    low_half_ref[...] = unfold(low, low_half_ref.shape[1]).astype(BF)


def attend_kernel(
    lengths_ref, own_ref, got_ref, low_ref, upk_ref, upv_ref, q_ref, p_ref,
    pack_ref, gk_ref, gv_ref, q_scr, p_scr, sem,
):
    rows = own_ref.shape[0]
    heads = q_ref.shape[1] // HD
    batch = 4
    copies = []
    for i in range(heads // batch):
        at = pl.ds(i * batch * HD, batch * HD)
        for k, (ref, scr) in enumerate(((q_ref, q_scr), (p_ref, p_scr))):
            copies.append(pltpu.make_async_copy(ref.at[:, at], scr.at[:, at], sem.at[2 * i + k]))
    for c in copies:
        c.start()
    score_scale = HD ** (-0.5)
    probe_scale = (q_ref.shape[1] * pack_ref.shape[0]) ** (-0.5)
    low_half = low_ref[...]
    full = own_ref[...] + got_ref[...]
    key_full, value_full = full[:, :HD], full[:, HD:]
    key_pol = (key_full + mm(low_half, upk_ref[...], NN)).astype(BF)
    value_pol = (value_full + mm(low_half, upv_ref[...], NN)).astype(BF)
    keys = jnp.concatenate([key_pol, key_full.astype(BF)], axis=0)
    values = jnp.concatenate([value_pol, value_full.astype(BF)], axis=0)
    doc_s = doc_ids(lengths_ref, 0, rows, lengths_ref.shape[1])
    doc_t = doc_ids(lengths_ref, 1, rows, lengths_ref.shape[1])
    s_at = lax.broadcasted_iota(jnp.int32, (rows, rows), 0)
    t_at = lax.broadcasted_iota(jnp.int32, (rows, rows), 1)
    allowed = (doc_s == doc_t) & (t_at >= s_at)
    banned = jnp.where(allowed, 0.0, -1e30)
    banned = jnp.concatenate([banned, banned], axis=1)

    def raised(scores):
        scores = jnp.where(banned < 0.0, -1e30, scores)
        peak = jnp.max(scores, axis=0, keepdims=True)
        e = jnp.exp2((scores - peak) * (score_scale * LOG2E))
        return e, 1.0 / jnp.sum(e, axis=0, keepdims=True)

    gk = jnp.zeros((rows, HD), F32)
    gv = jnp.zeros((rows, HD), F32)
    gap = jnp.zeros((1, 2 * rows), F32)
    for h in range(0, heads, 2):
        if h % batch == 0:
            for c in copies[2 * h // batch:2 * h // batch + 2]:
                c.wait()
        q, probe = (
            jnp.concatenate([scr[:, pl.ds((h + i) * HD, HD)] for i in range(2)], axis=0)
            for scr in (q_scr, p_scr)
        )
        scores = mm(keys, q, NT)
        grads = mm(values, probe, NT)
        pol, share = raised(scores[:rows])
        pol = pol * share
        ref, share = raised(scores[rows:])
        grad_pol = grads[:rows]
        mean_pol = jnp.sum(pol * grad_pol, axis=0, keepdims=True)
        mean_ref = jnp.sum(ref * grads[rows:], axis=0, keepdims=True) * share
        gap = gap + (mean_pol - mean_ref)
        grad_scores = (pol * (grad_pol - mean_pol)).astype(BF)
        gk = gk + mm(grad_scores, q, NN)
        gv = gv + mm(pol.astype(BF), probe, NN)
    gap = gap[:, :rows] + gap[:, rows:]
    gk = gk * (score_scale * probe_scale)
    gv = gv * probe_scale
    gap = gap * probe_scale
    gk_ref[...] = gk
    gv_ref[...] = gv
    back = mm(gk.astype(BF), upk_ref[...], NT) + mm(gv.astype(BF), upv_ref[...], NT)
    back = fold(back, 64).astype(BF)
    first = gap.astype(BF).astype(F32)
    second = (gap - first).astype(BF).astype(F32)
    third = gap - first - second
    line = lax.broadcasted_iota(jnp.int32, (16, rows), 0)
    tail = jnp.where(line == 0, first, jnp.where(line == 1, second, jnp.where(line == 2, third, 0.0)))
    tail = tail.astype(BF)
    for i in range(pack_ref.shape[0]):
        pack_ref[i, pl.ds(0, 64)] = back
        pack_ref[i, pl.ds(64, 16)] = tail


def weigh_kernel(
    pos_ref, lengths_ref, pack_ref, low_half_ref, gk_ref, gv_ref, t_ref, keep_ref, give_ref, up_ref
):
    rows = gk_ref.shape[0]
    total = pack_ref[0].astype(F32)
    for i in range(1, pack_ref.shape[0]):
        total = total + pack_ref[i].astype(F32)
    gap = total[64:65] + total[65:66] + total[66:67]
    docs = lengths_ref.shape[1]
    same = doc_ids(lengths_ref, 0, rows, docs) == doc_ids(lengths_ref, 1, rows, docs)
    token_gap = jnp.sum(jnp.where(same, gap, 0.0), axis=1, keepdims=True)
    weight = 2.0 * jax.nn.sigmoid(npo_beta * token_gap)
    back_half = (unfold(total[:64], 64) * weight).astype(BF)
    down = mm(back_half, t_ref[...], TN).astype(BF)
    both = jnp.concatenate([gk_ref[...] * weight, gv_ref[...] * weight], axis=1).astype(BF)
    up_ref[...] = mm(low_half_ref[...], both, TN)
    half = keep_ref.shape[1]
    for core in range(2):

        @pl.when(pos_ref[0] == core)
        def _():
            keep_ref[...] = down[:, core * half:(core + 1) * half]
            give_ref[...] = down[:, (1 - core) * half:(2 - core) * half]


def tiles():
    for s in range(32):
        yield s, s // 4 * 128, s % 4 * 16, s // 16 * 128, s // 4 % 4 * 16 + s % 4 * 4


def slot_kernel(keep_ref, got_ref, up_ref, out_ref):
    down = (keep_ref[...].astype(F32) + got_ref[...].astype(F32)).astype(BF)
    up = up_ref[...]
    blank = jnp.zeros((4, 128), F32)
    for s, lane, row, up_lane, up_row in tiles():
        out_ref[s, pl.ds(0, 16)] = down[row:row + 16, lane:lane + 128]
        piece = jnp.concatenate([up[up_row:up_row + 4, up_lane:up_lane + 128], blank], axis=0)
        out_ref[s, pl.ds(16, 8)] = piece.astype(BF)


def sum_kernel(in_ref, out_ref):
    total = in_ref[0].astype(F32)
    for i in range(1, in_ref.shape[0]):
        total = total + in_ref[i].astype(F32)
    total = total.astype(BF)
    for i in range(out_ref.shape[0]):
        out_ref[i] = total


def place_kernel(pos_ref, mine_ref, theirs_ref, down_ref, upk_ref, upv_ref):
    half = down_ref.shape[1] // 2
    for core in range(2):

        @pl.when(pos_ref[0] == core)
        def _():
            for s, lane, row, _, _ in tiles():
                for k, ref in ((core, mine_ref), (1 - core, theirs_ref)):
                    to = pl.ds(k * half + lane, 128)
                    down_ref[pl.ds(row, 16), to] = ref[s, pl.ds(0, 16)].astype(F32)

    for s, _, _, up_lane, up_row in tiles():
        up = mine_ref[s, pl.ds(16, 8)].astype(F32) + theirs_ref[s, pl.ds(16, 8)].astype(F32)
        to = upk_ref if up_lane == 0 else upv_ref
        to[pl.ds(up_row, 4)] = up[:4]


def call(kernel, outs, in_specs, out_specs, *args, scratch=(), mib=8, cost=None):
    return pl.pallas_call(
        kernel,
        out_shape=[jax.ShapeDtypeStruct(s, d) for s, d in outs],
        in_specs=in_specs,
        out_specs=out_specs,
        scratch_shapes=list(scratch),
        cost_estimate=cost and pl.CostEstimate(
            flops=cost[0], bytes_accessed=cost[1], transcendentals=0
        ),
        compiler_params=pltpu.CompilerParams(vmem_limit_bytes=mib * 1024 * 1024),
    )(*args)


def on_device(tokens, queries, probes, w_key, w_value, down_proj, up_key, up_value, lengths):
    rows, feats = tokens.shape
    row_at = lax.axis_index("row")
    pos = jnp.stack([row_at % 2, lax.axis_index("col"), row_at // 8]).astype(jnp.int32)

    def place(y, x, core):
        return ((y % 8) * 4 + x % 4) * 2 + core % 2

    sites = [(y, x, core) for y in range(8) for x in range(4) for core in range(2)]
    swap = [(place(y, x, c), place(y, x, 1 - c)) for y, x, c in sites]
    y_fore = [(place(y, x, c), place(y + 1 - 2 * c, x, c)) for y, x, c in sites]
    y_aft = [(b, a) for a, b in y_fore]
    z_fore = [
        (place(y, x, c) * 8 + z, place(y, x, c) * 8 + (z + 1 - 2 * c) % 8)
        for y, x, c in sites
        for z in range(8)
    ]
    z_aft = [(b, a) for a, b in z_fore]
    kinds = [[place(y, x, c) for y in range(8) for x in range(4)] for c in range(2)]
    x_lines = [[place(y, x, c) for x in range(4)] for y in range(8) for c in range(2)]

    half = (rows, feats // 2)
    mine, theirs = call(
        split_kernel, [(half, BF), (half, BF)], [SMEM, HBM], [VMEM, VMEM], pos, tokens,
        scratch=[pltpu.SemaphoreType.DMA((feats // 256,))],
    )
    swapped = lax.ppermute(theirs, "row", swap)
    (low_part,) = call(
        low_kernel, [((16, feats // 2), BF)], [VMEM, VMEM], [VMEM], tokens, down_proj.T
    )
    pair = jnp.concatenate([mine, swapped, low_part], axis=0)

    w_both = jnp.concatenate([w_key, w_value], axis=1)
    wide = w_both.shape[1]
    w_line = lax.all_to_all(
        jnp.broadcast_to(w_both, (4,) + w_both.shape), "row", 0, 0, axis_index_groups=x_lines
    )
    w_own = w_line.reshape(feats // 2, wide)
    t_parts = ring_of(pair, ("row", "col"), z_fore, z_aft, rows)
    w_parts = ring_of(w_own, "row", y_fore, y_aft, feats // 4)

    deep = feats // 2
    total, low_sum, t_left, w_left = call(
        project_kernel,
        [((2 * rows, wide), F32), ((16, deep), F32), ((2 * rows, deep), BF), (w_own.shape, BF)],
        [SMEM] + [HBM] * 14,
        [VMEM] * 4,
        pos, *t_parts[:7], *w_parts[:7],
        scratch=[
            pltpu.VMEM((8,) + pair.shape, BF),
            pltpu.VMEM((8,) + w_own.shape, BF),
            pltpu.SemaphoreType.DMA((2, 7)),
        ],
        mib=52,
        cost=(2 * 16 * rows * deep * wide, 14 * (pair.size + w_own.size)),
    )
    own, other, low_half = call(
        finish_kernel,
        [((rows, wide), F32), ((rows, wide), F32), ((rows, 64), BF)],
        [SMEM] + [HBM] * 8,
        [VMEM] * 3,
        pos, *t_parts[7:], *w_parts[7:], total, low_sum, t_left, w_left,
        scratch=[
            pltpu.VMEM(pair.shape, BF),
            pltpu.VMEM(w_own.shape, BF),
            pltpu.VMEM(total.shape, F32),
            pltpu.VMEM(low_sum.shape, F32),
            pltpu.VMEM(t_left.shape, BF),
            pltpu.VMEM(w_left.shape, BF),
            pltpu.SemaphoreType.DMA((8,)),
        ],
        mib=52,
    )
    got = lax.ppermute(other, "row", swap)
    pack, gk, gv = call(
        attend_kernel,
        [((8, 80, 128), BF), ((rows, HD), F32), ((rows, HD), F32)],
        [SMEM] + [VMEM] * 5 + [HBM] * 2,
        [VMEM] * 3,
        lengths, own, got, low_half, up_key, up_value, queries, probes,
        scratch=[
            pltpu.VMEM((rows, feats), BF),
            pltpu.VMEM((rows, feats), BF),
            pltpu.SemaphoreType.DMA((8,)),
        ],
    )
    packs = lax.all_to_all(pack, "col", 0, 0)
    keep, give, up = call(
        weigh_kernel,
        [((64, feats // 2), BF), ((64, feats // 2), BF), ((64, 2 * HD), F32)],
        [SMEM] * 2 + [VMEM] * 5, [VMEM] * 3,
        pos, lengths, packs, low_half, gk, gv, tokens,
    )
    slots = (32, 24, 128)
    (terms,) = call(
        slot_kernel, [(slots, BF)], [VMEM] * 3, [VMEM], keep, lax.ppermute(give, "row", swap), up
    )
    term_parts = lax.all_to_all(terms, "row", 0, 0, axis_index_groups=kinds)
    (summed,) = call(sum_kernel, [(slots, BF)], [VMEM], [VMEM], term_parts)
    pieces = lax.all_to_all(summed, "row", 0, 0, axis_index_groups=kinds)
    grad_down, grad_up_key, grad_up_value = call(
        place_kernel,
        [((64, feats), F32), ((64, HD), F32), ((64, HD), F32)],
        [SMEM] + [VMEM] * 2, [VMEM] * 3, pos, pieces, lax.ppermute(pieces, "row", swap),
    )
    return grad_down.T, grad_up_key, grad_up_value


def solution(mesh):
    in_specs = (
        P("row", "col"),
        P("row", "col"),
        P("row", "col"),
        P("row", "col"),
        P("row", "col"),
        P("col", None),
        P(None, "col"),
        P(None, "col"),
        P("row", None),
    )
    out_specs = (P("col", None), P(None, "col"), P(None, "col"))
    return jax.shard_map(
        on_device, mesh=mesh, in_specs=in_specs, out_specs=out_specs, check_vma=False
    )
```

```python
import functools
import jax
import jax.numpy as jnp
from jax import lax
from jax.experimental import pallas as pl
from jax.experimental.pallas import tpu as pltpu
from jax.sharding import PartitionSpec as P

HD = 128
QPK = 16
BF = jnp.bfloat16
F32 = jnp.float32
npo_beta = 0.5
LOG2E = 1.4426950408889634

VMEM = pl.BlockSpec(memory_space=pltpu.VMEM)
SMEM = pl.BlockSpec(memory_space=pltpu.SMEM)
HBM = pl.BlockSpec(memory_space=pltpu.HBM)

NT = (((1,), (1,)), ((), ()))
TN = (((0,), (0,)), ((), ()))
NN = (((1,), (0,)), ((), ()))


def mm(a, b, dims):
    return lax.dot_general(a, b, dims, preferred_element_type=F32)


def fold(a, rows):
    return jnp.concatenate([a[i:i + rows] for i in range(0, a.shape[0], rows)], axis=1)


def unfold(a, wide):
    return jnp.concatenate([a[:, i:i + wide] for i in range(0, a.shape[1], wide)], axis=0)


def doc_ids(lengths_ref, axis, count, docs):
    places = lax.broadcasted_iota(jnp.int32, (count, count), axis)
    ids = jnp.zeros((count, count), jnp.int32)
    end = 0
    for j in range(docs):
        end = end + lengths_ref[0, j]
        ids = ids + jnp.where(places >= end, 1, 0)
    return ids


def split_kernel(pos_ref, t_ref, mine_ref, theirs_ref, sem):
    copies = []
    for i in range(t_ref.shape[1] // 512):
        to = pl.ds(i * 256, 256)
        for k, ref in enumerate((mine_ref, theirs_ref)):
            core = lax.rem(pos_ref[0] + k, 2)
            at = pl.ds(pl.multiple_of(i * 512 + core * 256, 256), 256)
            copies.append(pltpu.make_async_copy(t_ref.at[:, at], ref.at[:, to], sem.at[2 * i + k]))
    for c in copies:
        c.start()
    for c in copies:
        c.wait()


def low_kernel(t_ref, down_ref, out_ref):
    low = mm(t_ref[...], down_ref[...], NT)
    rows, wide = out_ref.shape
    low = fold(low, rows // 2)
    high = low.astype(BF).astype(F32)
    out_ref[...] = jnp.concatenate([high, low - high], axis=0).astype(BF)


STEPS = (0, 1, 2, 3, -1, -2, -3, 4)


def ring_of(own, axis, fore, aft, cut):
    fore_going, aft_going = [own], [own]
    for _ in range(3):
        fore_going.append(lax.ppermute(fore_going[-1], axis, fore))
        aft_going.append(lax.ppermute(aft_going[-1], axis, aft))
    return fore_going + aft_going[1:] + [
        lax.ppermute(fore_going[3][:cut], axis, fore),
        lax.ppermute(aft_going[3][cut:], axis, aft),
    ]


def block_at(pos_ref, axis, step, n):
    return lax.rem(pos_ref[1 + axis] + step * (2 * pos_ref[0] - 1) + n, n)


def project_kernel(pos_ref, *refs):
    t_refs, w_refs, refs = refs[:7], refs[7:14], refs[14:]
    total_ref, low_ref, t_left_ref, w_left_ref, w_scr, sem = refs
    n = w_scr.shape[0]
    copies = [
        pltpu.make_async_copy(part, w_scr.at[block_at(pos_ref, 1, STEPS[j], n)], sem.at[j])
        for j, part in enumerate(w_refs)
    ]
    for c in copies:
        c.start()
    t_far, w_far = (block_at(pos_ref, axis, STEPS[7], n) for axis in range(2))
    w_scr[w_far] = jnp.zeros(w_scr.shape[1:], BF)
    t_left_ref[...] = jnp.zeros(t_left_ref.shape, BF)
    rows = total_ref.shape[0]
    low = jnp.zeros(low_ref.shape, F32)
    for t_ref in t_refs:
        low = low + t_ref[pl.ds(rows, low.shape[0])].astype(F32)
    low_ref[...] = low
    for c in copies:
        c.wait()
    total = jnp.zeros(total_ref.shape, F32)
    for j, t_ref in enumerate(t_refs):
        k = block_at(pos_ref, 0, STEPS[j], n)
        total = total + mm(t_ref[pl.ds(0, rows)], w_scr[k], NN)

        @pl.when(k == w_far)
        def _():
            t_left_ref[...] = t_ref[pl.ds(0, rows)]

    total_ref[...] = total
    w_left_ref[...] = w_scr[t_far]


def finish_kernel(
    pos_ref, t1_ref, t2_ref, w1_ref, w2_ref, total_ref, low_ref, t_left_ref, w_left_ref,
    own_ref, other_ref, low_half_ref,
    t_scr, w_scr, total_scr, low_scr, t_left_scr, w_left_scr, sem,
):
    pairs = [
        (t1_ref, t_scr.at[pl.ds(0, t1_ref.shape[0])]),
        (t2_ref, t_scr.at[pl.ds(t1_ref.shape[0], t2_ref.shape[0])]),
        (w1_ref, w_scr.at[pl.ds(0, w1_ref.shape[0])]),
        (w2_ref, w_scr.at[pl.ds(w1_ref.shape[0], w2_ref.shape[0])]),
        (total_ref, total_scr),
        (low_ref, low_scr),
        (t_left_ref, t_left_scr),
        (w_left_ref, w_left_scr),
    ]
    copies = [pltpu.make_async_copy(a, b, sem.at[i]) for i, (a, b) in enumerate(pairs)]
    for c in copies:
        c.start()
    for c in copies:
        c.wait()
    rows = own_ref.shape[0]
    same = pos_ref[1] == pos_ref[2]
    w_late = w_scr[...]
    w_match = jnp.where(same, w_late, w_left_scr[...])
    total = total_scr[...] + mm(t_scr[pl.ds(0, 2 * rows)], w_match, NN)
    total = total + mm(t_left_scr[...], w_late, NN)
    own_ref[...] = total[:rows]
    other_ref[...] = total[rows:]
    low = low_scr[...] + t_scr[pl.ds(2 * rows, low_scr.shape[0])].astype(F32)
    low = low[:low.shape[0] // 2] + low[low.shape[0] // 2:]
    low_half_ref[...] = unfold(low, low_half_ref.shape[1]).astype(BF)


def attend_kernel(
    lengths_ref, own_ref, got_ref, low_ref, upk_ref, upv_ref, q_ref, p_ref,
    pack_ref, gk_ref, gv_ref, q_scr, p_scr, sem,
):
    rows = own_ref.shape[0]
    heads = q_ref.shape[1] // HD
    batch = 4
    copies = []
    for i in range(heads // batch):
        at = pl.ds(i * batch * HD, batch * HD)
        for k, (ref, scr) in enumerate(((q_ref, q_scr), (p_ref, p_scr))):
            copies.append(pltpu.make_async_copy(ref.at[:, at], scr.at[:, at], sem.at[2 * i + k]))
    for c in copies:
        c.start()
    score_scale = HD ** (-0.5)
    probe_scale = (q_ref.shape[1] * pack_ref.shape[0]) ** (-0.5)
    low_half = low_ref[...]
    full = own_ref[...] + got_ref[...]
    key_full, value_full = full[:, :HD], full[:, HD:]
    key_pol = (key_full + mm(low_half, upk_ref[...], NN)).astype(BF)
    value_pol = (value_full + mm(low_half, upv_ref[...], NN)).astype(BF)
    keys = jnp.concatenate([key_pol, key_full.astype(BF)], axis=0)
    values = jnp.concatenate([value_pol, value_full.astype(BF)], axis=0)
    doc_s = doc_ids(lengths_ref, 0, rows, lengths_ref.shape[1])
    doc_t = doc_ids(lengths_ref, 1, rows, lengths_ref.shape[1])
    s_at = lax.broadcasted_iota(jnp.int32, (rows, rows), 0)
    t_at = lax.broadcasted_iota(jnp.int32, (rows, rows), 1)
    allowed = (doc_s == doc_t) & (t_at >= s_at)
    banned = jnp.where(allowed, 0.0, -1e30)
    banned = jnp.concatenate([banned, banned], axis=1)

    def raised(scores):
        scores = jnp.where(banned < 0.0, -1e30, scores)
        peak = jnp.max(scores, axis=0, keepdims=True)
        e = jnp.exp2((scores - peak) * (score_scale * LOG2E))
        return e, 1.0 / jnp.sum(e, axis=0, keepdims=True)

    gk = jnp.zeros((rows, HD), F32)
    gv = jnp.zeros((rows, HD), F32)
    gap = jnp.zeros((1, 2 * rows), F32)
    for h in range(0, heads, 2):
        if h % batch == 0:
            for c in copies[2 * h // batch:2 * h // batch + 2]:
                c.wait()
        q, probe = (
            jnp.concatenate([scr[:, pl.ds((h + i) * HD, HD)] for i in range(2)], axis=0)
            for scr in (q_scr, p_scr)
        )
        scores = mm(keys, q, NT)
        grads = mm(values, probe, NT)
        pol, share = raised(scores[:rows])
        pol = pol * share
        ref, share = raised(scores[rows:])
        grad_pol = grads[:rows]
        mean_pol = jnp.sum(pol * grad_pol, axis=0, keepdims=True)
        mean_ref = jnp.sum(ref * grads[rows:], axis=0, keepdims=True) * share
        gap = gap + (mean_pol - mean_ref)
        grad_scores = (pol * (grad_pol - mean_pol)).astype(BF)
        gk = gk + mm(grad_scores, q, NN)
        gv = gv + mm(pol.astype(BF), probe, NN)
    gap = gap[:, :rows] + gap[:, rows:]
    gk = gk * (score_scale * probe_scale)
    gv = gv * probe_scale
    gap = gap * probe_scale
    gk_ref[...] = gk
    gv_ref[...] = gv
    back = mm(gk.astype(BF), upk_ref[...], NT) + mm(gv.astype(BF), upv_ref[...], NT)
    back = fold(back, 64).astype(BF)
    first = gap.astype(BF).astype(F32)
    second = (gap - first).astype(BF).astype(F32)
    third = gap - first - second
    line = lax.broadcasted_iota(jnp.int32, (16, rows), 0)
    tail = jnp.where(line == 0, first, jnp.where(line == 1, second, jnp.where(line == 2, third, 0.0)))
    tail = tail.astype(BF)
    for i in range(pack_ref.shape[0]):
        pack_ref[i, pl.ds(0, 64)] = back
        pack_ref[i, pl.ds(64, 16)] = tail


def weigh_kernel(lengths_ref, pack_ref, low_half_ref, gk_ref, gv_ref, t_ref, out_ref):
    rows = gk_ref.shape[0]
    total = pack_ref[0].astype(F32)
    for i in range(1, pack_ref.shape[0]):
        total = total + pack_ref[i].astype(F32)
    gap = total[64:65] + total[65:66] + total[66:67]
    docs = lengths_ref.shape[1]
    same = doc_ids(lengths_ref, 0, rows, docs) == doc_ids(lengths_ref, 1, rows, docs)
    token_gap = jnp.sum(jnp.where(same, gap, 0.0), axis=1, keepdims=True)
    weight = 2.0 * jax.nn.sigmoid(npo_beta * token_gap)
    back_half = (unfold(total[:64], 64) * weight).astype(BF)
    down = mm(back_half, t_ref[...], TN).astype(BF)
    both = jnp.concatenate([gk_ref[...] * weight, gv_ref[...] * weight], axis=1).astype(BF)
    up = mm(low_half_ref[...], both, TN).astype(BF)
    slots = out_ref.shape[0]
    wide, deep = t_ref.shape[1] // slots, up.shape[0] // slots
    for j in range(slots):
        out_ref[j, pl.ds(0, 64)] = down[:, j * wide:(j + 1) * wide]
        out_ref[j, pl.ds(64, deep)] = up[j * deep:(j + 1) * deep]


def sum_kernel(in_ref, out_ref):
    total = in_ref[0].astype(F32)
    for i in range(1, in_ref.shape[0]):
        total = total + in_ref[i].astype(F32)
    total = total.astype(BF)
    for i in range(out_ref.shape[0]):
        out_ref[i] = total


def place_kernel(in_ref, down_ref, upk_ref, upv_ref):
    slots, _, wide = in_ref.shape
    deep = upk_ref.shape[0] // slots
    for j in range(slots):
        down_ref[:, pl.ds(j * wide, wide)] = in_ref[j, pl.ds(0, 64)].astype(F32)
        up = in_ref[j, pl.ds(64, deep)].astype(F32)
        upk_ref[pl.ds(j * deep, deep)] = up[:, :HD]
        upv_ref[pl.ds(j * deep, deep)] = up[:, HD:]


def call(kernel, outs, in_specs, out_specs, *args, scratch=(), mib=8, cost=None):
    return pl.pallas_call(
        kernel,
        out_shape=[jax.ShapeDtypeStruct(s, d) for s, d in outs],
        in_specs=in_specs,
        out_specs=out_specs,
        scratch_shapes=list(scratch),
        cost_estimate=cost and pl.CostEstimate(
            flops=cost[0], bytes_accessed=cost[1], transcendentals=0
        ),
        compiler_params=pltpu.CompilerParams(vmem_limit_bytes=mib * 1024 * 1024),
    )(*args)


def on_device(tokens, queries, probes, w_key, w_value, down_proj, up_key, up_value, lengths):
    rows, feats = tokens.shape
    row_at = lax.axis_index("row")
    pos = jnp.stack([row_at % 2, lax.axis_index("col"), row_at // 8]).astype(jnp.int32)

    def place(y, x, core):
        return ((y % 8) * 4 + x % 4) * 2 + core % 2

    sites = [(y, x, core) for y in range(8) for x in range(4) for core in range(2)]
    swap = [(place(y, x, c), place(y, x, 1 - c)) for y, x, c in sites]
    y_fore = [(place(y, x, c), place(y + 1 - 2 * c, x, c)) for y, x, c in sites]
    y_aft = [(b, a) for a, b in y_fore]
    z_fore = [
        (place(y, x, c) * 8 + z, place(y, x, c) * 8 + (z + 1 - 2 * c) % 8)
        for y, x, c in sites
        for z in range(8)
    ]
    z_aft = [(b, a) for a, b in z_fore]
    y_lines = [[place(y, x, c) for y in range(8)] for x in range(4) for c in range(2)]
    squares = [[place(y, x, c) for x in range(4) for c in range(2)] for y in range(8)]
    x_lines = [[place(y, x, c) for x in range(4)] for y in range(8) for c in range(2)]

    half = (rows, feats // 2)
    mine, theirs = call(
        split_kernel, [(half, BF), (half, BF)], [SMEM, HBM], [VMEM, VMEM], pos, tokens,
        scratch=[pltpu.SemaphoreType.DMA((feats // 256,))],
    )
    swapped = lax.ppermute(theirs, "row", swap)
    (low_part,) = call(
        low_kernel, [((16, feats // 2), BF)], [VMEM, VMEM], [VMEM], tokens, down_proj.T
    )
    pair = jnp.concatenate([mine, swapped, low_part], axis=0)

    w_both = jnp.concatenate([w_key, w_value], axis=1)
    wide = w_both.shape[1]
    w_line = lax.all_to_all(
        jnp.broadcast_to(w_both, (4,) + w_both.shape), "row", 0, 0, axis_index_groups=x_lines
    )
    w_own = w_line.reshape(feats // 2, wide)
    t_parts = ring_of(pair, ("row", "col"), z_fore, z_aft, rows)
    w_parts = ring_of(w_own, "row", y_fore, y_aft, feats // 4)

    deep = feats // 2
    total, low_sum, t_left, w_left = call(
        project_kernel,
        [((2 * rows, wide), F32), ((16, deep), F32), ((2 * rows, deep), BF), (w_own.shape, BF)],
        [SMEM] + [VMEM] * 7 + [HBM] * 7,
        [VMEM] * 4,
        pos, *t_parts[:7], *w_parts[:7],
        scratch=[
            pltpu.VMEM((8,) + w_own.shape, BF),
            pltpu.SemaphoreType.DMA((7,)),
        ],
        mib=40,
        cost=(2 * 16 * rows * deep * wide, 14 * (pair.size + w_own.size)),
    )
    own, other, low_half = call(
        finish_kernel,
        [((rows, wide), F32), ((rows, wide), F32), ((rows, 64), BF)],
        [SMEM] + [HBM] * 8,
        [VMEM] * 3,
        pos, *t_parts[7:], *w_parts[7:], total, low_sum, t_left, w_left,
        scratch=[
            pltpu.VMEM(pair.shape, BF),
            pltpu.VMEM(w_own.shape, BF),
            pltpu.VMEM(total.shape, F32),
            pltpu.VMEM(low_sum.shape, F32),
            pltpu.VMEM(t_left.shape, BF),
            pltpu.VMEM(w_left.shape, BF),
            pltpu.SemaphoreType.DMA((8,)),
        ],
        mib=16,
    )
    got = lax.ppermute(other, "row", swap)
    pack, gk, gv = call(
        attend_kernel,
        [((8, 80, 128), BF), ((rows, HD), F32), ((rows, HD), F32)],
        [SMEM] + [VMEM] * 5 + [HBM] * 2,
        [VMEM] * 3,
        lengths, own, got, low_half, up_key, up_value, queries, probes,
        scratch=[
            pltpu.VMEM((rows, feats), BF),
            pltpu.VMEM((rows, feats), BF),
            pltpu.SemaphoreType.DMA((8,)),
        ],
    )
    packs = lax.all_to_all(pack, "col", 0, 0)
    slot = (8, 64 + 8, 2 * HD)
    (terms,) = call(
        weigh_kernel, [(slot, BF)], [SMEM] + [VMEM] * 5, [VMEM],
        lengths, packs, low_half, gk, gv, tokens,
    )
    term_parts = lax.all_to_all(terms, "row", 0, 0, axis_index_groups=squares)
    (square,) = call(sum_kernel, [(slot, BF)], [VMEM], [VMEM], term_parts)
    square_parts = lax.all_to_all(square, "row", 0, 0, axis_index_groups=y_lines)
    (summed,) = call(sum_kernel, [(slot, BF)], [VMEM], [VMEM], square_parts)
    pieces = lax.all_to_all(summed, "row", 0, 0, axis_index_groups=squares)
    grad_down, grad_up_key, grad_up_value = call(
        place_kernel,
        [((64, feats), F32), ((64, HD), F32), ((64, HD), F32)],
        [VMEM], [VMEM] * 3, pieces,
    )
    return grad_down.T, grad_up_key, grad_up_value


def solution(mesh):
    in_specs = (
        P("row", "col"),
        P("row", "col"),
        P("row", "col"),
        P("row", "col"),
        P("row", "col"),
        P("col", None),
        P(None, "col"),
        P(None, "col"),
        P("row", None),
    )
    out_specs = (P("col", None), P(None, "col"), P(None, "col"))
    return jax.shard_map(
        on_device, mesh=mesh, in_specs=in_specs, out_specs=out_specs, check_vma=False
    )
```

```python
import functools
import jax
import jax.numpy as jnp
from jax import lax
from jax.experimental import pallas as pl
from jax.experimental.pallas import tpu as pltpu
from jax.sharding import PartitionSpec as P

HD = 128
QPK = 16
BF = jnp.bfloat16
F32 = jnp.float32
npo_beta = 0.5
LOG2E = 1.4426950408889634

VMEM = pl.BlockSpec(memory_space=pltpu.VMEM)
SMEM = pl.BlockSpec(memory_space=pltpu.SMEM)
HBM = pl.BlockSpec(memory_space=pltpu.HBM)

NT = (((1,), (1,)), ((), ()))
TN = (((0,), (0,)), ((), ()))
NN = (((1,), (0,)), ((), ()))


def mm(a, b, dims):
    return lax.dot_general(a, b, dims, preferred_element_type=F32)


def fold(a, rows):
    return jnp.concatenate([a[i:i + rows] for i in range(0, a.shape[0], rows)], axis=1)


def unfold(a, wide):
    return jnp.concatenate([a[:, i:i + wide] for i in range(0, a.shape[1], wide)], axis=0)


def doc_ids(lengths_ref, axis, count, docs):
    places = lax.broadcasted_iota(jnp.int32, (count, count), axis)
    ids = jnp.zeros((count, count), jnp.int32)
    end = 0
    for j in range(docs):
        end = end + lengths_ref[0, j]
        ids = ids + jnp.where(places >= end, 1, 0)
    return ids


def split_kernel(pos_ref, t_ref, mine_ref, theirs_ref, sem):
    copies = []
    for i in range(t_ref.shape[1] // 512):
        to = pl.ds(i * 256, 256)
        for k, ref in enumerate((mine_ref, theirs_ref)):
            core = lax.rem(pos_ref[0] + k, 2)
            at = pl.ds(pl.multiple_of(i * 512 + core * 256, 256), 256)
            copies.append(pltpu.make_async_copy(t_ref.at[:, at], ref.at[:, to], sem.at[2 * i + k]))
    for c in copies:
        c.start()
    for c in copies:
        c.wait()


def low_kernel(t_ref, down_ref, out_ref):
    low = mm(t_ref[...], down_ref[...], NT)
    rows, wide = out_ref.shape
    low = fold(low, rows // 2)
    high = low.astype(BF).astype(F32)
    out_ref[...] = jnp.concatenate([high, low - high], axis=0).astype(BF)


STEPS = (0, 1, 2, 3, -1, -2, -3, 4)


def rings_of(owns, axes, fores, afts, halves):
    both = range(2)
    going = [list(owns), list(owns)]
    blocks = [[[own] for own in owns] for _ in going]
    for step in range(4):
        for side, ways in enumerate((fores, afts)):
            now = going[side]
            if step == 0 and side == 1:
                now = lax.optimization_barrier(tuple(now))
            if step == 3:
                now = [halves[i](now[i])[side] for i in both]
            going[side] = [lax.ppermute(now[i], axes[i], ways[i]) for i in both]
            for i in both:
                blocks[side][i].append(going[side][i])
    return [blocks[0][i][:4] + blocks[1][i][1:4] + [blocks[0][i][4], blocks[1][i][4]] for i in both]


def block_at(pos_ref, axis, step, n):
    return lax.rem(pos_ref[1 + axis] + step * (2 * pos_ref[0] - 1) + n, n)


def project_kernel(pos_ref, *refs):
    t_refs, w_refs, refs = refs[:7], refs[7:14], refs[14:]
    total_ref, low_ref, t_left_ref, w_left_ref, w_scr, sem = refs
    n = w_scr.shape[0]
    copies = [
        pltpu.make_async_copy(part, w_scr.at[block_at(pos_ref, 1, STEPS[j], n)], sem.at[j])
        for j, part in enumerate(w_refs)
    ]
    for c in copies:
        c.start()
    t_far, w_far = (block_at(pos_ref, axis, STEPS[7], n) for axis in range(2))
    w_scr[w_far] = jnp.zeros(w_scr.shape[1:], BF)
    t_left_ref[...] = jnp.zeros(t_left_ref.shape, BF)
    rows = total_ref.shape[0]
    low = jnp.zeros(low_ref.shape, F32)
    for t_ref in t_refs:
        low = low + t_ref[pl.ds(rows, low.shape[0])].astype(F32)
    low_ref[...] = low
    for c in copies:
        c.wait()
    deep = w_left_ref.shape[0]
    total = jnp.zeros(total_ref.shape, F32)
    for j, t_ref in enumerate(t_refs):
        k = block_at(pos_ref, 0, STEPS[j], n)
        total = total + mm(t_ref[pl.ds(0, rows)], w_scr[k, pl.ds(0, deep)], NN)

        @pl.when(k == w_far)
        def _():
            t_left_ref[...] = t_ref[pl.ds(0, rows)]

    total_ref[...] = total
    w_left_ref[...] = w_scr[t_far, pl.ds(0, deep)]


def finish_kernel(
    pos_ref, t1_ref, t2_ref, w1_ref, w2_ref, total_ref, low_ref, t_left_ref, w_left_ref,
    own_ref, other_ref, low_half_ref,
    t_scr, w_scr, total_scr, low_scr, t_left_scr, w_left_scr, sem,
):
    pairs = [
        (t1_ref, t_scr.at[:, pl.ds(0, t1_ref.shape[1])]),
        (t2_ref, t_scr.at[:, pl.ds(t1_ref.shape[1], t2_ref.shape[1])]),
        (w1_ref, w_scr.at[pl.ds(0, w1_ref.shape[0])]),
        (w2_ref, w_scr.at[pl.ds(w1_ref.shape[0], w2_ref.shape[0])]),
        (total_ref, total_scr),
        (low_ref, low_scr),
        (t_left_ref, t_left_scr),
        (w_left_ref, w_left_scr),
    ]
    copies = [pltpu.make_async_copy(a, b, sem.at[i]) for i, (a, b) in enumerate(pairs)]
    for c in copies:
        c.start()
    for c in copies:
        c.wait()
    rows = own_ref.shape[0]
    same = pos_ref[1] == pos_ref[2]
    w_late = w_scr[pl.ds(0, w_left_scr.shape[0])]
    w_match = jnp.where(same, w_late, w_left_scr[...])
    total = total_scr[...] + mm(t_scr[pl.ds(0, 2 * rows)], w_match, NN)
    total = total + mm(t_left_scr[...], w_late, NN)
    own_ref[...] = total[:rows]
    other_ref[...] = total[rows:]
    low = low_scr[...] + t_scr[pl.ds(2 * rows, low_scr.shape[0])].astype(F32)
    low = low[:low.shape[0] // 2] + low[low.shape[0] // 2:]
    low_half_ref[...] = unfold(low, low_half_ref.shape[1]).astype(BF)


def attend_kernel(
    lengths_ref, own_ref, got_ref, low_ref, upk_ref, upv_ref, q_ref, p_ref,
    pack_ref, gk_ref, gv_ref, q_scr, p_scr, sem,
):
    rows = own_ref.shape[0]
    heads = q_ref.shape[1] // HD
    batch = 4
    copies = []
    for i in range(heads // batch):
        at = pl.ds(i * batch * HD, batch * HD)
        for k, (ref, scr) in enumerate(((q_ref, q_scr), (p_ref, p_scr))):
            copies.append(pltpu.make_async_copy(ref.at[:, at], scr.at[:, at], sem.at[2 * i + k]))
    for c in copies:
        c.start()
    score_scale = HD ** (-0.5)
    probe_scale = (q_ref.shape[1] * pack_ref.shape[0]) ** (-0.5)
    low_half = low_ref[...]
    full = own_ref[...] + got_ref[...]
    key_full, value_full = full[:, :HD], full[:, HD:]
    key_pol = (key_full + mm(low_half, upk_ref[...], NN)).astype(BF)
    value_pol = (value_full + mm(low_half, upv_ref[...], NN)).astype(BF)
    keys = jnp.concatenate([key_pol, key_full.astype(BF)], axis=0)
    values = jnp.concatenate([value_pol, value_full.astype(BF)], axis=0)
    doc_s = doc_ids(lengths_ref, 0, rows, lengths_ref.shape[1])
    doc_t = doc_ids(lengths_ref, 1, rows, lengths_ref.shape[1])
    s_at = lax.broadcasted_iota(jnp.int32, (rows, rows), 0)
    t_at = lax.broadcasted_iota(jnp.int32, (rows, rows), 1)
    allowed = (doc_s == doc_t) & (t_at >= s_at)
    banned = jnp.where(allowed, 0.0, -1e30)
    banned = jnp.concatenate([banned, banned], axis=1)

    def raised(scores):
        scores = jnp.where(banned < 0.0, -1e30, scores)
        peak = jnp.max(scores, axis=0, keepdims=True)
        e = jnp.exp2((scores - peak) * (score_scale * LOG2E))
        return e, 1.0 / jnp.sum(e, axis=0, keepdims=True)

    gk = jnp.zeros((rows, HD), F32)
    gv = jnp.zeros((rows, HD), F32)
    gap = jnp.zeros((1, 2 * rows), F32)
    for h in range(0, heads, 2):
        if h % batch == 0:
            for c in copies[2 * h // batch:2 * h // batch + 2]:
                c.wait()
        q, probe = (
            jnp.concatenate([scr[:, pl.ds((h + i) * HD, HD)] for i in range(2)], axis=0)
            for scr in (q_scr, p_scr)
        )
        scores = mm(keys, q, NT)
        grads = mm(values, probe, NT)
        pol, share = raised(scores[:rows])
        pol = pol * share
        ref, share = raised(scores[rows:])
        grad_pol = grads[:rows]
        mean_pol = jnp.sum(pol * grad_pol, axis=0, keepdims=True)
        mean_ref = jnp.sum(ref * grads[rows:], axis=0, keepdims=True) * share
        gap = gap + (mean_pol - mean_ref)
        grad_scores = (pol * (grad_pol - mean_pol)).astype(BF)
        gk = gk + mm(grad_scores, q, NN)
        gv = gv + mm(pol.astype(BF), probe, NN)
    gap = gap[:, :rows] + gap[:, rows:]
    gk = gk * (score_scale * probe_scale)
    gv = gv * probe_scale
    gap = gap * probe_scale
    gk_ref[...] = gk
    gv_ref[...] = gv
    back = mm(gk.astype(BF), upk_ref[...], NT) + mm(gv.astype(BF), upv_ref[...], NT)
    back = fold(back, 64).astype(BF)
    first = gap.astype(BF).astype(F32)
    second = (gap - first).astype(BF).astype(F32)
    third = gap - first - second
    line = lax.broadcasted_iota(jnp.int32, (16, rows), 0)
    tail = jnp.where(line == 0, first, jnp.where(line == 1, second, jnp.where(line == 2, third, 0.0)))
    tail = tail.astype(BF)
    for i in range(pack_ref.shape[0]):
        pack_ref[i, pl.ds(0, 64)] = back
        pack_ref[i, pl.ds(64, 16)] = tail


def weigh_kernel(lengths_ref, pack_ref, low_half_ref, gk_ref, gv_ref, t_ref, out_ref):
    rows = gk_ref.shape[0]
    total = pack_ref[0].astype(F32)
    for i in range(1, pack_ref.shape[0]):
        total = total + pack_ref[i].astype(F32)
    gap = total[64:65] + total[65:66] + total[66:67]
    docs = lengths_ref.shape[1]
    same = doc_ids(lengths_ref, 0, rows, docs) == doc_ids(lengths_ref, 1, rows, docs)
    token_gap = jnp.sum(jnp.where(same, gap, 0.0), axis=1, keepdims=True)
    weight = 2.0 * jax.nn.sigmoid(npo_beta * token_gap)
    back_half = (unfold(total[:64], 64) * weight).astype(BF)
    down = mm(back_half, t_ref[...], TN).astype(BF)
    both = jnp.concatenate([gk_ref[...] * weight, gv_ref[...] * weight], axis=1).astype(BF)
    up = mm(low_half_ref[...], both, TN).astype(BF)
    slots = out_ref.shape[0]
    wide, deep = t_ref.shape[1] // slots, up.shape[0] // slots
    for j in range(slots):
        out_ref[j, pl.ds(0, 64)] = down[:, j * wide:(j + 1) * wide]
        out_ref[j, pl.ds(64, deep)] = up[j * deep:(j + 1) * deep]


def sum_kernel(in_ref, out_ref):
    total = in_ref[0].astype(F32)
    for i in range(1, in_ref.shape[0]):
        total = total + in_ref[i].astype(F32)
    total = total.astype(BF)
    for i in range(out_ref.shape[0]):
        out_ref[i] = total


def place_kernel(in_ref, down_ref, upk_ref, upv_ref):
    slots, _, wide = in_ref.shape
    deep = upk_ref.shape[0] // slots
    for j in range(slots):
        down_ref[:, pl.ds(j * wide, wide)] = in_ref[j, pl.ds(0, 64)].astype(F32)
        up = in_ref[j, pl.ds(64, deep)].astype(F32)
        upk_ref[pl.ds(j * deep, deep)] = up[:, :HD]
        upv_ref[pl.ds(j * deep, deep)] = up[:, HD:]


def call(kernel, outs, in_specs, out_specs, *args, scratch=(), mib=8, cost=None):
    return pl.pallas_call(
        kernel,
        out_shape=[jax.ShapeDtypeStruct(s, d) for s, d in outs],
        in_specs=in_specs,
        out_specs=out_specs,
        scratch_shapes=list(scratch),
        cost_estimate=cost and pl.CostEstimate(
            flops=cost[0], bytes_accessed=cost[1], transcendentals=0
        ),
        compiler_params=pltpu.CompilerParams(vmem_limit_bytes=mib * 1024 * 1024),
    )(*args)


def on_device(tokens, queries, probes, w_key, w_value, down_proj, up_key, up_value, lengths):
    rows, feats = tokens.shape
    row_at = lax.axis_index("row")
    pos = jnp.stack([row_at % 2, lax.axis_index("col"), row_at // 8]).astype(jnp.int32)

    def place(y, x, core):
        return ((y % 8) * 4 + x % 4) * 2 + core % 2

    sites = [(y, x, core) for y in range(8) for x in range(4) for core in range(2)]
    swap = [(place(y, x, c), place(y, x, 1 - c)) for y, x, c in sites]
    y_fore = [(place(y, x, c), place(y + 1 - 2 * c, x, c)) for y, x, c in sites]
    y_aft = [(b, a) for a, b in y_fore]
    z_fore = [
        (place(y, x, c) * 8 + z, place(y, x, c) * 8 + (z + 1 - 2 * c) % 8)
        for y, x, c in sites
        for z in range(8)
    ]
    z_aft = [(b, a) for a, b in z_fore]
    y_lines = [[place(y, x, c) for y in range(8)] for x in range(4) for c in range(2)]
    squares = [[place(y, x, c) for x in range(4) for c in range(2)] for y in range(8)]
    x_lines = [[place(y, x, c) for x in range(4)] for y in range(8) for c in range(2)]

    half = (rows, feats // 2)
    mine, theirs = call(
        split_kernel, [(half, BF), (half, BF)], [SMEM, HBM], [VMEM, VMEM], pos, tokens,
        scratch=[pltpu.SemaphoreType.DMA((feats // 256,))],
    )
    swapped = lax.ppermute(theirs, "row", swap)
    (low_part,) = call(
        low_kernel, [((16, feats // 2), BF)], [VMEM, VMEM], [VMEM], tokens, down_proj.T
    )
    pair = jnp.concatenate([mine, swapped, low_part], axis=0)

    w_both = jnp.concatenate([w_key, w_value], axis=1)
    wide = w_both.shape[1]
    w_line = lax.all_to_all(
        jnp.broadcast_to(w_both, (4,) + w_both.shape), "row", 0, 0, axis_index_groups=x_lines
    )
    w_own = w_line.reshape(feats // 2, wide)
    w_own = jnp.pad(w_own, ((0, pair.size // wide - w_own.shape[0]), (0, 0)))
    t_parts, w_parts = rings_of(
        (pair, w_own), (("row", "col"), "row"), (z_fore, y_fore), (z_aft, y_aft),
        (lambda t: jnp.split(t, 2, axis=1), lambda w: jnp.split(w, 2, axis=0)),
    )

    deep = feats // 2
    total, low_sum, t_left, w_left = call(
        project_kernel,
        [((2 * rows, wide), F32), ((16, deep), F32), ((2 * rows, deep), BF), ((deep, wide), BF)],
        [SMEM] + [VMEM] * 7 + [HBM] * 7,
        [VMEM] * 4,
        pos, *t_parts[:7], *w_parts[:7],
        scratch=[
            pltpu.VMEM((8,) + w_own.shape, BF),
            pltpu.SemaphoreType.DMA((7,)),
        ],
        mib=40,
        cost=(2 * 16 * rows * deep * wide, 14 * (pair.size + w_own.size)),
    )
    own, other, low_half = call(
        finish_kernel,
        [((rows, wide), F32), ((rows, wide), F32), ((rows, 64), BF)],
        [SMEM] + [HBM] * 8,
        [VMEM] * 3,
        pos, *t_parts[7:], *w_parts[7:], total, low_sum, t_left, w_left,
        scratch=[
            pltpu.VMEM(pair.shape, BF),
            pltpu.VMEM(w_own.shape, BF),
            pltpu.VMEM(total.shape, F32),
            pltpu.VMEM(low_sum.shape, F32),
            pltpu.VMEM(t_left.shape, BF),
            pltpu.VMEM(w_left.shape, BF),
            pltpu.SemaphoreType.DMA((8,)),
        ],
        mib=16,
    )
    got = lax.ppermute(other, "row", swap)
    pack, gk, gv = call(
        attend_kernel,
        [((8, 80, 128), BF), ((rows, HD), F32), ((rows, HD), F32)],
        [SMEM] + [VMEM] * 5 + [HBM] * 2,
        [VMEM] * 3,
        lengths, own, got, low_half, up_key, up_value, queries, probes,
        scratch=[
            pltpu.VMEM((rows, feats), BF),
            pltpu.VMEM((rows, feats), BF),
            pltpu.SemaphoreType.DMA((8,)),
        ],
    )
    packs = lax.all_to_all(pack, "col", 0, 0)
    slot = (8, 64 + 8, 2 * HD)
    (terms,) = call(
        weigh_kernel, [(slot, BF)], [SMEM] + [VMEM] * 5, [VMEM],
        lengths, packs, low_half, gk, gv, tokens,
    )
    term_parts = lax.all_to_all(terms, "row", 0, 0, axis_index_groups=squares)
    (square,) = call(sum_kernel, [(slot, BF)], [VMEM], [VMEM], term_parts)
    square_parts = lax.all_to_all(square, "row", 0, 0, axis_index_groups=y_lines)
    (summed,) = call(sum_kernel, [(slot, BF)], [VMEM], [VMEM], square_parts)
    pieces = lax.all_to_all(summed, "row", 0, 0, axis_index_groups=squares)
    grad_down, grad_up_key, grad_up_value = call(
        place_kernel,
        [((64, feats), F32), ((64, HD), F32), ((64, HD), F32)],
        [VMEM], [VMEM] * 3, pieces,
    )
    return grad_down.T, grad_up_key, grad_up_value


def solution(mesh):
    in_specs = (
        P("row", "col"),
        P("row", "col"),
        P("row", "col"),
        P("row", "col"),
        P("row", "col"),
        P("col", None),
        P(None, "col"),
        P(None, "col"),
        P("row", None),
    )
    out_specs = (P("col", None), P(None, "col"), P(None, "col"))
    return jax.shard_map(
        on_device, mesh=mesh, in_specs=in_specs, out_specs=out_specs, check_vma=False
    )
```

```python
import functools
import jax
import jax.numpy as jnp
from jax import lax
from jax.experimental import pallas as pl
from jax.experimental.pallas import tpu as pltpu
from jax.sharding import PartitionSpec as P

HD = 128
QPK = 16
BF = jnp.bfloat16
F32 = jnp.float32
npo_beta = 0.5
LOG2E = 1.4426950408889634

VMEM = pl.BlockSpec(memory_space=pltpu.VMEM)
SMEM = pl.BlockSpec(memory_space=pltpu.SMEM)
HBM = pl.BlockSpec(memory_space=pltpu.HBM)

NT = (((1,), (1,)), ((), ()))
TN = (((0,), (0,)), ((), ()))
NN = (((1,), (0,)), ((), ()))


def mm(a, b, dims):
    return lax.dot_general(a, b, dims, preferred_element_type=F32)


def fold(a, rows):
    return jnp.concatenate([a[i:i + rows] for i in range(0, a.shape[0], rows)], axis=1)


def unfold(a, wide):
    return jnp.concatenate([a[:, i:i + wide] for i in range(0, a.shape[1], wide)], axis=0)


def doc_ids(lengths_ref, axis, count, docs):
    places = lax.broadcasted_iota(jnp.int32, (count, count), axis)
    ids = jnp.zeros((count, count), jnp.int32)
    end = 0
    for j in range(docs):
        end = end + lengths_ref[0, j]
        ids = ids + jnp.where(places >= end, 1, 0)
    return ids


def split_kernel(pos_ref, t_ref, mine_ref, theirs_ref, sem):
    copies = []
    for i in range(t_ref.shape[1] // 512):
        to = pl.ds(i * 256, 256)
        for k, ref in enumerate((mine_ref, theirs_ref)):
            core = lax.rem(pos_ref[0] + k, 2)
            at = pl.ds(pl.multiple_of(i * 512 + core * 256, 256), 256)
            copies.append(pltpu.make_async_copy(t_ref.at[:, at], ref.at[:, to], sem.at[2 * i + k]))
    for c in copies:
        c.start()
    for c in copies:
        c.wait()


def low_kernel(t_ref, down_ref, out_ref):
    low = mm(t_ref[...], down_ref[...], NT)
    rows, wide = out_ref.shape
    low = fold(low, rows // 2)
    high = low.astype(BF).astype(F32)
    out_ref[...] = jnp.concatenate([high, low - high], axis=0).astype(BF)


STEPS = (0, 1, 2, 3, -1, -2, -3, 4)


def rings_of(owns, axes, fores, afts):
    both = range(2)
    going = [list(owns), list(owns)]
    blocks = [[[own] for own in owns] for _ in going]
    for step in range(3):
        for side, ways in enumerate((fores, afts)):
            now = going[side]
            if step == 0 and side == 1:
                now = lax.optimization_barrier(tuple(now))
            going[side] = [lax.ppermute(now[i], axes[i], ways[i]) for i in both]
            for i in both:
                blocks[side][i].append(going[side][i])
    far = [lax.ppermute(going[i][i], axes[i], (fores, afts)[i][i]) for i in both]
    return [blocks[0][i] + blocks[1][i][1:] + [far[i]] for i in both]


def block_at(pos_ref, axis, step, n):
    return lax.rem(pos_ref[1 + axis] + step * (2 * pos_ref[0] - 1) + n, n)


def project_kernel(pos_ref, *refs):
    t_refs, w_refs, refs = refs[:7], refs[7:14], refs[14:]
    total_ref, low_ref, t_left_ref, w_left_ref, w_scr, sem = refs
    n = w_scr.shape[0]
    copies = [
        pltpu.make_async_copy(part, w_scr.at[block_at(pos_ref, 1, STEPS[j], n)], sem.at[j])
        for j, part in enumerate(w_refs)
    ]
    for c in copies:
        c.start()
    t_far, w_far = (block_at(pos_ref, axis, STEPS[7], n) for axis in range(2))
    w_scr[w_far] = jnp.zeros(w_scr.shape[1:], BF)
    t_left_ref[...] = jnp.zeros(t_left_ref.shape, BF)
    rows = total_ref.shape[0]
    low = jnp.zeros(low_ref.shape, F32)
    for t_ref in t_refs:
        low = low + t_ref[pl.ds(rows, low.shape[0])].astype(F32)
    low_ref[...] = low
    for c in copies:
        c.wait()
    deep = w_left_ref.shape[0]
    total = jnp.zeros(total_ref.shape, F32)
    for j, t_ref in enumerate(t_refs):
        k = block_at(pos_ref, 0, STEPS[j], n)
        total = total + mm(t_ref[pl.ds(0, rows)], w_scr[k, pl.ds(0, deep)], NN)

        @pl.when(k == w_far)
        def _():
            t_left_ref[...] = t_ref[pl.ds(0, rows)]

    total_ref[...] = total
    w_left_ref[...] = w_scr[t_far, pl.ds(0, deep)]


def finish_kernel(
    pos_ref, t_ref, w_ref, total_ref, low_ref, t_left_ref, w_left_ref,
    own_ref, other_ref, low_half_ref,
    t_scr, w_scr, total_scr, low_scr, t_left_scr, w_left_scr, sem,
):
    pairs = [
        (t_ref, t_scr),
        (w_ref, w_scr),
        (total_ref, total_scr),
        (low_ref, low_scr),
        (t_left_ref, t_left_scr),
        (w_left_ref, w_left_scr),
    ]
    copies = [pltpu.make_async_copy(a, b, sem.at[i]) for i, (a, b) in enumerate(pairs)]
    for c in copies:
        c.start()
    for c in copies:
        c.wait()
    rows = own_ref.shape[0]
    same = pos_ref[1] == pos_ref[2]
    w_late = w_scr[pl.ds(0, w_left_scr.shape[0])]
    w_match = jnp.where(same, w_late, w_left_scr[...])
    total = total_scr[...] + mm(t_scr[pl.ds(0, 2 * rows)], w_match, NN)
    total = total + mm(t_left_scr[...], w_late, NN)
    own_ref[...] = total[:rows]
    other_ref[...] = total[rows:]
    low = low_scr[...] + t_scr[pl.ds(2 * rows, low_scr.shape[0])].astype(F32)
    low = low[:low.shape[0] // 2] + low[low.shape[0] // 2:]
    low_half_ref[...] = unfold(low, low_half_ref.shape[1]).astype(BF)


def attend_kernel(
    lengths_ref, own_ref, got_ref, low_ref, upk_ref, upv_ref, q_ref, p_ref,
    pack_ref, gk_ref, gv_ref, q_scr, p_scr, sem,
):
    rows = own_ref.shape[0]
    heads = q_ref.shape[1] // HD
    batch = 4
    copies = []
    for i in range(heads // batch):
        at = pl.ds(i * batch * HD, batch * HD)
        for k, (ref, scr) in enumerate(((q_ref, q_scr), (p_ref, p_scr))):
            copies.append(pltpu.make_async_copy(ref.at[:, at], scr.at[:, at], sem.at[2 * i + k]))
    for c in copies:
        c.start()
    score_scale = HD ** (-0.5)
    probe_scale = (q_ref.shape[1] * pack_ref.shape[0]) ** (-0.5)
    low_half = low_ref[...]
    full = own_ref[...] + got_ref[...]
    key_full, value_full = full[:, :HD], full[:, HD:]
    key_pol = (key_full + mm(low_half, upk_ref[...], NN)).astype(BF)
    value_pol = (value_full + mm(low_half, upv_ref[...], NN)).astype(BF)
    keys = jnp.concatenate([key_pol, key_full.astype(BF)], axis=0)
    values = jnp.concatenate([value_pol, value_full.astype(BF)], axis=0)
    doc_s = doc_ids(lengths_ref, 0, rows, lengths_ref.shape[1])
    doc_t = doc_ids(lengths_ref, 1, rows, lengths_ref.shape[1])
    s_at = lax.broadcasted_iota(jnp.int32, (rows, rows), 0)
    t_at = lax.broadcasted_iota(jnp.int32, (rows, rows), 1)
    allowed = (doc_s == doc_t) & (t_at >= s_at)
    banned = jnp.where(allowed, 0.0, -1e30)
    banned = jnp.concatenate([banned, banned], axis=1)

    def raised(scores):
        scores = jnp.where(banned < 0.0, -1e30, scores)
        peak = jnp.max(scores, axis=0, keepdims=True)
        e = jnp.exp2((scores - peak) * (score_scale * LOG2E))
        return e, 1.0 / jnp.sum(e, axis=0, keepdims=True)

    gk = jnp.zeros((rows, HD), F32)
    gv = jnp.zeros((rows, HD), F32)
    gap = jnp.zeros((1, 2 * rows), F32)
    for h in range(0, heads, 2):
        if h % batch == 0:
            for c in copies[2 * h // batch:2 * h // batch + 2]:
                c.wait()
        q, probe = (
            jnp.concatenate([scr[:, pl.ds((h + i) * HD, HD)] for i in range(2)], axis=0)
            for scr in (q_scr, p_scr)
        )
        scores = mm(keys, q, NT)
        grads = mm(values, probe, NT)
        pol, share = raised(scores[:rows])
        pol = pol * share
        ref, share = raised(scores[rows:])
        grad_pol = grads[:rows]
        mean_pol = jnp.sum(pol * grad_pol, axis=0, keepdims=True)
        mean_ref = jnp.sum(ref * grads[rows:], axis=0, keepdims=True) * share
        gap = gap + (mean_pol - mean_ref)
        grad_scores = (pol * (grad_pol - mean_pol)).astype(BF)
        gk = gk + mm(grad_scores, q, NN)
        gv = gv + mm(pol.astype(BF), probe, NN)
    gap = gap[:, :rows] + gap[:, rows:]
    gk = gk * (score_scale * probe_scale)
    gv = gv * probe_scale
    gap = gap * probe_scale
    gk_ref[...] = gk
    gv_ref[...] = gv
    back = mm(gk.astype(BF), upk_ref[...], NT) + mm(gv.astype(BF), upv_ref[...], NT)
    back = fold(back, 64).astype(BF)
    first = gap.astype(BF).astype(F32)
    second = (gap - first).astype(BF).astype(F32)
    third = gap - first - second
    line = lax.broadcasted_iota(jnp.int32, (16, rows), 0)
    tail = jnp.where(line == 0, first, jnp.where(line == 1, second, jnp.where(line == 2, third, 0.0)))
    tail = tail.astype(BF)
    for i in range(pack_ref.shape[0]):
        pack_ref[i, pl.ds(0, 64)] = back
        pack_ref[i, pl.ds(64, 16)] = tail


def weigh_kernel(lengths_ref, pack_ref, low_half_ref, gk_ref, gv_ref, t_ref, out_ref):
    rows = gk_ref.shape[0]
    total = pack_ref[0].astype(F32)
    for i in range(1, pack_ref.shape[0]):
        total = total + pack_ref[i].astype(F32)
    gap = total[64:65] + total[65:66] + total[66:67]
    docs = lengths_ref.shape[1]
    same = doc_ids(lengths_ref, 0, rows, docs) == doc_ids(lengths_ref, 1, rows, docs)
    token_gap = jnp.sum(jnp.where(same, gap, 0.0), axis=1, keepdims=True)
    weight = 2.0 * jax.nn.sigmoid(npo_beta * token_gap)
    back_half = (unfold(total[:64], 64) * weight).astype(BF)
    down = mm(back_half, t_ref[...], TN).astype(BF)
    both = jnp.concatenate([gk_ref[...] * weight, gv_ref[...] * weight], axis=1).astype(BF)
    up = mm(low_half_ref[...], both, TN).astype(BF)
    slots = out_ref.shape[0]
    wide, deep = t_ref.shape[1] // slots, up.shape[0] // slots
    for j in range(slots):
        out_ref[j, pl.ds(0, 64)] = down[:, j * wide:(j + 1) * wide]
        out_ref[j, pl.ds(64, deep)] = up[j * deep:(j + 1) * deep]


def sum_kernel(in_ref, out_ref):
    total = in_ref[0].astype(F32)
    for i in range(1, in_ref.shape[0]):
        total = total + in_ref[i].astype(F32)
    total = total.astype(BF)
    for i in range(out_ref.shape[0]):
        out_ref[i] = total


def place_kernel(in_ref, down_ref, upk_ref, upv_ref):
    slots, _, wide = in_ref.shape
    deep = upk_ref.shape[0] // slots
    for j in range(slots):
        down_ref[:, pl.ds(j * wide, wide)] = in_ref[j, pl.ds(0, 64)].astype(F32)
        up = in_ref[j, pl.ds(64, deep)].astype(F32)
        upk_ref[pl.ds(j * deep, deep)] = up[:, :HD]
        upv_ref[pl.ds(j * deep, deep)] = up[:, HD:]


def call(kernel, outs, in_specs, out_specs, *args, scratch=(), mib=8, cost=None):
    return pl.pallas_call(
        kernel,
        out_shape=[jax.ShapeDtypeStruct(s, d) for s, d in outs],
        in_specs=in_specs,
        out_specs=out_specs,
        scratch_shapes=list(scratch),
        cost_estimate=cost and pl.CostEstimate(
            flops=cost[0], bytes_accessed=cost[1], transcendentals=0
        ),
        compiler_params=pltpu.CompilerParams(vmem_limit_bytes=mib * 1024 * 1024),
    )(*args)


def on_device(tokens, queries, probes, w_key, w_value, down_proj, up_key, up_value, lengths):
    rows, feats = tokens.shape
    row_at = lax.axis_index("row")
    pos = jnp.stack([row_at % 2, lax.axis_index("col"), row_at // 8]).astype(jnp.int32)

    def place(y, x, core):
        return ((y % 8) * 4 + x % 4) * 2 + core % 2

    sites = [(y, x, core) for y in range(8) for x in range(4) for core in range(2)]
    swap = [(place(y, x, c), place(y, x, 1 - c)) for y, x, c in sites]
    y_fore = [(place(y, x, c), place(y + 1 - 2 * c, x, c)) for y, x, c in sites]
    y_aft = [(b, a) for a, b in y_fore]
    z_fore = [
        (place(y, x, c) * 8 + z, place(y, x, c) * 8 + (z + 1 - 2 * c) % 8)
        for y, x, c in sites
        for z in range(8)
    ]
    z_aft = [(b, a) for a, b in z_fore]
    y_lines = [[place(y, x, c) for y in range(8)] for x in range(4) for c in range(2)]
    squares = [[place(y, x, c) for x in range(4) for c in range(2)] for y in range(8)]
    x_lines = [[place(y, x, c) for x in range(4)] for y in range(8) for c in range(2)]

    half = (rows, feats // 2)
    mine, theirs = call(
        split_kernel, [(half, BF), (half, BF)], [SMEM, HBM], [VMEM, VMEM], pos, tokens,
        scratch=[pltpu.SemaphoreType.DMA((feats // 256,))],
    )
    swapped = lax.ppermute(theirs, "row", swap)
    (low_part,) = call(
        low_kernel, [((16, feats // 2), BF)], [VMEM, VMEM], [VMEM], tokens, down_proj.T
    )
    pair = jnp.concatenate([mine, swapped, low_part], axis=0)

    w_both = jnp.concatenate([w_key, w_value], axis=1)
    wide = w_both.shape[1]
    w_line = lax.all_to_all(
        jnp.broadcast_to(w_both, (4,) + w_both.shape), "row", 0, 0, axis_index_groups=x_lines
    )
    w_own = w_line.reshape(feats // 2, wide)
    w_own = jnp.pad(w_own, ((0, pair.size // wide - w_own.shape[0]), (0, 0)))
    t_parts, w_parts = rings_of(
        (pair, w_own), (("row", "col"), "row"), (z_fore, y_fore), (z_aft, y_aft),
    )

    deep = feats // 2
    total, low_sum, t_left, w_left = call(
        project_kernel,
        [((2 * rows, wide), F32), ((16, deep), F32), ((2 * rows, deep), BF), ((deep, wide), BF)],
        [SMEM] + [VMEM] * 7 + [HBM] * 7,
        [VMEM] * 4,
        pos, *t_parts[:7], *w_parts[:7],
        scratch=[
            pltpu.VMEM((8,) + w_own.shape, BF),
            pltpu.SemaphoreType.DMA((7,)),
        ],
        mib=40,
        cost=(2 * 16 * rows * deep * wide, 14 * (pair.size + w_own.size)),
    )
    own, other, low_half = call(
        finish_kernel,
        [((rows, wide), F32), ((rows, wide), F32), ((rows, 64), BF)],
        [SMEM] + [HBM] * 6,
        [VMEM] * 3,
        pos, t_parts[7], w_parts[7], total, low_sum, t_left, w_left,
        scratch=[
            pltpu.VMEM(pair.shape, BF),
            pltpu.VMEM(w_own.shape, BF),
            pltpu.VMEM(total.shape, F32),
            pltpu.VMEM(low_sum.shape, F32),
            pltpu.VMEM(t_left.shape, BF),
            pltpu.VMEM(w_left.shape, BF),
            pltpu.SemaphoreType.DMA((6,)),
        ],
        mib=16,
    )
    got = lax.ppermute(other, "row", swap)
    pack, gk, gv = call(
        attend_kernel,
        [((8, 80, 128), BF), ((rows, HD), F32), ((rows, HD), F32)],
        [SMEM] + [VMEM] * 5 + [HBM] * 2,
        [VMEM] * 3,
        lengths, own, got, low_half, up_key, up_value, queries, probes,
        scratch=[
            pltpu.VMEM((rows, feats), BF),
            pltpu.VMEM((rows, feats), BF),
            pltpu.SemaphoreType.DMA((8,)),
        ],
    )
    packs = lax.all_to_all(pack, "col", 0, 0)
    slot = (8, 64 + 8, 2 * HD)
    (terms,) = call(
        weigh_kernel, [(slot, BF)], [SMEM] + [VMEM] * 5, [VMEM],
        lengths, packs, low_half, gk, gv, tokens,
    )
    term_parts = lax.all_to_all(terms, "row", 0, 0, axis_index_groups=squares)
    (square,) = call(sum_kernel, [(slot, BF)], [VMEM], [VMEM], term_parts)
    square_parts = lax.all_to_all(square, "row", 0, 0, axis_index_groups=y_lines)
    (summed,) = call(sum_kernel, [(slot, BF)], [VMEM], [VMEM], square_parts)
    pieces = lax.all_to_all(summed, "row", 0, 0, axis_index_groups=squares)
    grad_down, grad_up_key, grad_up_value = call(
        place_kernel,
        [((64, feats), F32), ((64, HD), F32), ((64, HD), F32)],
        [VMEM], [VMEM] * 3, pieces,
    )
    return grad_down.T, grad_up_key, grad_up_value


def solution(mesh):
    in_specs = (
        P("row", "col"),
        P("row", "col"),
        P("row", "col"),
        P("row", "col"),
        P("row", "col"),
        P("col", None),
        P(None, "col"),
        P(None, "col"),
        P("row", None),
    )
    out_specs = (P("col", None), P(None, "col"), P(None, "col"))
    return jax.shard_map(
        on_device, mesh=mesh, in_specs=in_specs, out_specs=out_specs, check_vma=False
    )
```

```python
import functools
import jax
import jax.numpy as jnp
from jax import lax
from jax.experimental import pallas as pl
from jax.experimental.pallas import tpu as pltpu
from jax.sharding import PartitionSpec as P

HD = 128
QPK = 16
BF = jnp.bfloat16
F32 = jnp.float32
npo_beta = 0.5
LOG2E = 1.4426950408889634

VMEM = pl.BlockSpec(memory_space=pltpu.VMEM)
SMEM = pl.BlockSpec(memory_space=pltpu.SMEM)
HBM = pl.BlockSpec(memory_space=pltpu.HBM)

NT = (((1,), (1,)), ((), ()))
TN = (((0,), (0,)), ((), ()))
NN = (((1,), (0,)), ((), ()))


def mm(a, b, dims):
    return lax.dot_general(a, b, dims, preferred_element_type=F32)


def fold(a, rows):
    return jnp.concatenate([a[i:i + rows] for i in range(0, a.shape[0], rows)], axis=1)


def unfold(a, wide):
    return jnp.concatenate([a[:, i:i + wide] for i in range(0, a.shape[1], wide)], axis=0)


def doc_ids(lengths_ref, axis, count, docs):
    places = lax.broadcasted_iota(jnp.int32, (count, count), axis)
    ids = jnp.zeros((count, count), jnp.int32)
    end = 0
    for j in range(docs):
        end = end + lengths_ref[0, j]
        ids = ids + jnp.where(places >= end, 1, 0)
    return ids


def split_kernel(pos_ref, t_ref, mine_ref, theirs_ref, sem):
    copies = []
    for i in range(t_ref.shape[1] // 512):
        to = pl.ds(i * 256, 256)
        for k, ref in enumerate((mine_ref, theirs_ref)):
            core = lax.rem(pos_ref[0] + k, 2)
            at = pl.ds(pl.multiple_of(i * 512 + core * 256, 256), 256)
            copies.append(pltpu.make_async_copy(t_ref.at[:, at], ref.at[:, to], sem.at[2 * i + k]))
    for c in copies:
        c.start()
    for c in copies:
        c.wait()


def low_kernel(t_ref, down_ref, out_ref):
    low = mm(t_ref[...], down_ref[...], NT)
    rows, wide = out_ref.shape
    low = fold(low, rows // 2)
    high = low.astype(BF).astype(F32)
    out_ref[...] = jnp.concatenate([high, low - high], axis=0).astype(BF)


STEPS = (0, 1, 2, 3, -1, -2, -3, 4)
W_LATE = (4, 3)


def rings_of(owns, axes, fores, afts):
    both = range(2)
    going = [list(owns), list(owns)]
    blocks = [[[own] for own in owns] for _ in going]
    for step in range(3):
        for side, ways in enumerate((fores, afts)):
            now = going[side]
            if step == 0 and side == 1:
                now = lax.optimization_barrier(tuple(now))
            going[side] = [lax.ppermute(now[i], axes[i], ways[i]) for i in both]
            for i in both:
                blocks[side][i].append(going[side][i])
    far = [lax.ppermute(going[i][i], axes[i], (fores, afts)[i][i]) for i in both]
    return [blocks[0][i] + blocks[1][i][1:] + [far[i]] for i in both]


def block_at(pos_ref, axis, step, n):
    return lax.rem(pos_ref[1 + axis] + step * (2 * pos_ref[0] - 1) + n, n)


def project_kernel(pos_ref, *refs):
    t_refs, w_refs, refs = refs[:7], refs[7:13], refs[13:]
    total_ref, low_ref, t_left_ref, w_left_ref, w_scr, sem = refs
    n = w_scr.shape[0]
    copies = [
        pltpu.make_async_copy(part, w_scr.at[block_at(pos_ref, 1, step, n)], sem.at[j])
        for j, (part, step) in enumerate(zip(w_refs, STEPS[:3] + STEPS[4:7]))
    ]
    for c in copies:
        c.start()
    t_far = block_at(pos_ref, 0, STEPS[7], n)
    w_late = [block_at(pos_ref, 1, step, n) for step in W_LATE]
    for k in w_late:
        w_scr[k] = jnp.zeros(w_scr.shape[1:], BF)
    t_left_ref[...] = jnp.zeros(t_left_ref.shape, BF)
    rows = total_ref.shape[0]
    low = jnp.zeros(low_ref.shape, F32)
    for t_ref in t_refs:
        low = low + t_ref[pl.ds(rows, low.shape[0])].astype(F32)
    low_ref[...] = low
    for c in copies:
        c.wait()
    deep = w_left_ref.shape[0]
    total = jnp.zeros(total_ref.shape, F32)
    for j, t_ref in enumerate(t_refs):
        k = block_at(pos_ref, 0, STEPS[j], n)
        total = total + mm(t_ref[pl.ds(0, rows)], w_scr[k, pl.ds(0, deep)], NN)

        for i in range(2):

            @pl.when(k == w_late[i])
            def _():
                t_left_ref[i] = t_ref[pl.ds(0, rows)]

    total_ref[...] = total
    w_left_ref[...] = w_scr[t_far, pl.ds(0, deep)]


def finish_kernel(
    pos_ref, t_ref, w_ref, w3_ref, total_ref, low_ref, t_left_ref, w_left_ref,
    own_ref, other_ref, low_half_ref,
    t_scr, w_scr, w3_scr, total_scr, low_scr, t_left_scr, w_left_scr, sem,
):
    pairs = [
        (t_ref, t_scr),
        (w_ref, w_scr),
        (w3_ref, w3_scr),
        (total_ref, total_scr),
        (low_ref, low_scr),
        (t_left_ref, t_left_scr),
        (w_left_ref, w_left_scr),
    ]
    copies = [pltpu.make_async_copy(a, b, sem.at[i]) for i, (a, b) in enumerate(pairs)]
    for c in copies:
        c.start()
    for c in copies:
        c.wait()
    rows = own_ref.shape[0]
    t_far = block_at(pos_ref, 0, STEPS[7], 8)
    late = [scr[pl.ds(0, w_left_scr.shape[0])] for scr in (w_scr, w3_scr)]
    w_match = w_left_scr[...]
    for step, w in zip(W_LATE, late):
        w_match = jnp.where(t_far == block_at(pos_ref, 1, step, 8), w, w_match)
    total = total_scr[...] + mm(t_scr[pl.ds(0, 2 * rows)], w_match, NN)
    for i in range(2):
        total = total + mm(t_left_scr[i], late[i], NN)
    own_ref[...] = total[:rows]
    other_ref[...] = total[rows:]
    low = low_scr[...] + t_scr[pl.ds(2 * rows, low_scr.shape[0])].astype(F32)
    low = low[:low.shape[0] // 2] + low[low.shape[0] // 2:]
    low_half_ref[...] = unfold(low, low_half_ref.shape[1]).astype(BF)


def attend_kernel(
    lengths_ref, own_ref, got_ref, low_ref, upk_ref, upv_ref, q_ref, p_ref,
    pack_ref, gk_ref, gv_ref, q_scr, p_scr, sem,
):
    rows = own_ref.shape[0]
    heads = q_ref.shape[1] // HD
    batch = 4
    copies = []
    for i in range(heads // batch):
        at = pl.ds(i * batch * HD, batch * HD)
        for k, (ref, scr) in enumerate(((q_ref, q_scr), (p_ref, p_scr))):
            copies.append(pltpu.make_async_copy(ref.at[:, at], scr.at[:, at], sem.at[2 * i + k]))
    for c in copies:
        c.start()
    score_scale = HD ** (-0.5)
    probe_scale = (q_ref.shape[1] * pack_ref.shape[0]) ** (-0.5)
    low_half = low_ref[...]
    full = own_ref[...] + got_ref[...]
    key_full, value_full = full[:, :HD], full[:, HD:]
    key_pol = (key_full + mm(low_half, upk_ref[...], NN)).astype(BF)
    value_pol = (value_full + mm(low_half, upv_ref[...], NN)).astype(BF)
    keys = jnp.concatenate([key_pol, key_full.astype(BF)], axis=0)
    values = jnp.concatenate([value_pol, value_full.astype(BF)], axis=0)
    doc_s = doc_ids(lengths_ref, 0, rows, lengths_ref.shape[1])
    doc_t = doc_ids(lengths_ref, 1, rows, lengths_ref.shape[1])
    s_at = lax.broadcasted_iota(jnp.int32, (rows, rows), 0)
    t_at = lax.broadcasted_iota(jnp.int32, (rows, rows), 1)
    allowed = (doc_s == doc_t) & (t_at >= s_at)
    banned = jnp.where(allowed, 0.0, -1e30)
    banned = jnp.concatenate([banned, banned], axis=1)

    def raised(scores):
        scores = jnp.where(banned < 0.0, -1e30, scores)
        peak = jnp.max(scores, axis=0, keepdims=True)
        e = jnp.exp2((scores - peak) * (score_scale * LOG2E))
        return e, 1.0 / jnp.sum(e, axis=0, keepdims=True)

    gk = jnp.zeros((rows, HD), F32)
    gv = jnp.zeros((rows, HD), F32)
    gap = jnp.zeros((1, 2 * rows), F32)
    for h in range(0, heads, 2):
        if h % batch == 0:
            for c in copies[2 * h // batch:2 * h // batch + 2]:
                c.wait()
        q, probe = (
            jnp.concatenate([scr[:, pl.ds((h + i) * HD, HD)] for i in range(2)], axis=0)
            for scr in (q_scr, p_scr)
        )
        scores = mm(keys, q, NT)
        grads = mm(values, probe, NT)
        pol, share = raised(scores[:rows])
        pol = pol * share
        ref, share = raised(scores[rows:])
        grad_pol = grads[:rows]
        mean_pol = jnp.sum(pol * grad_pol, axis=0, keepdims=True)
        mean_ref = jnp.sum(ref * grads[rows:], axis=0, keepdims=True) * share
        gap = gap + (mean_pol - mean_ref)
        grad_scores = (pol * (grad_pol - mean_pol)).astype(BF)
        gk = gk + mm(grad_scores, q, NN)
        gv = gv + mm(pol.astype(BF), probe, NN)
    gap = gap[:, :rows] + gap[:, rows:]
    gk = gk * (score_scale * probe_scale)
    gv = gv * probe_scale
    gap = gap * probe_scale
    gk_ref[...] = gk
    gv_ref[...] = gv
    back = mm(gk.astype(BF), upk_ref[...], NT) + mm(gv.astype(BF), upv_ref[...], NT)
    back = fold(back, 64).astype(BF)
    first = gap.astype(BF).astype(F32)
    second = (gap - first).astype(BF).astype(F32)
    third = gap - first - second
    line = lax.broadcasted_iota(jnp.int32, (16, rows), 0)
    tail = jnp.where(line == 0, first, jnp.where(line == 1, second, jnp.where(line == 2, third, 0.0)))
    tail = tail.astype(BF)
    for i in range(pack_ref.shape[0]):
        pack_ref[i, pl.ds(0, 64)] = back
        pack_ref[i, pl.ds(64, 16)] = tail


def weigh_kernel(lengths_ref, pack_ref, low_half_ref, gk_ref, gv_ref, t_ref, out_ref):
    rows = gk_ref.shape[0]
    total = pack_ref[0].astype(F32)
    for i in range(1, pack_ref.shape[0]):
        total = total + pack_ref[i].astype(F32)
    gap = total[64:65] + total[65:66] + total[66:67]
    docs = lengths_ref.shape[1]
    same = doc_ids(lengths_ref, 0, rows, docs) == doc_ids(lengths_ref, 1, rows, docs)
    token_gap = jnp.sum(jnp.where(same, gap, 0.0), axis=1, keepdims=True)
    weight = 2.0 * jax.nn.sigmoid(npo_beta * token_gap)
    back_half = (unfold(total[:64], 64) * weight).astype(BF)
    down = mm(back_half, t_ref[...], TN).astype(BF)
    both = jnp.concatenate([gk_ref[...] * weight, gv_ref[...] * weight], axis=1).astype(BF)
    up = mm(low_half_ref[...], both, TN).astype(BF)
    slots = out_ref.shape[0]
    wide, deep = t_ref.shape[1] // slots, up.shape[0] // slots
    for j in range(slots):
        out_ref[j, pl.ds(0, 64)] = down[:, j * wide:(j + 1) * wide]
        out_ref[j, pl.ds(64, deep)] = up[j * deep:(j + 1) * deep]


def sum_kernel(in_ref, out_ref):
    total = in_ref[0].astype(F32)
    for i in range(1, in_ref.shape[0]):
        total = total + in_ref[i].astype(F32)
    total = total.astype(BF)
    for i in range(out_ref.shape[0]):
        out_ref[i] = total


def place_kernel(in_ref, down_ref, upk_ref, upv_ref):
    slots, _, wide = in_ref.shape
    deep = upk_ref.shape[0] // slots
    for j in range(slots):
        down_ref[:, pl.ds(j * wide, wide)] = in_ref[j, pl.ds(0, 64)].astype(F32)
        up = in_ref[j, pl.ds(64, deep)].astype(F32)
        upk_ref[pl.ds(j * deep, deep)] = up[:, :HD]
        upv_ref[pl.ds(j * deep, deep)] = up[:, HD:]


def call(kernel, outs, in_specs, out_specs, *args, scratch=(), mib=8, cost=None):
    return pl.pallas_call(
        kernel,
        out_shape=[jax.ShapeDtypeStruct(s, d) for s, d in outs],
        in_specs=in_specs,
        out_specs=out_specs,
        scratch_shapes=list(scratch),
        cost_estimate=cost and pl.CostEstimate(
            flops=cost[0], bytes_accessed=cost[1], transcendentals=0
        ),
        compiler_params=pltpu.CompilerParams(vmem_limit_bytes=mib * 1024 * 1024),
    )(*args)


def on_device(tokens, queries, probes, w_key, w_value, down_proj, up_key, up_value, lengths):
    rows, feats = tokens.shape
    row_at = lax.axis_index("row")
    pos = jnp.stack([row_at % 2, lax.axis_index("col"), row_at // 8]).astype(jnp.int32)

    def place(y, x, core):
        return ((y % 8) * 4 + x % 4) * 2 + core % 2

    sites = [(y, x, core) for y in range(8) for x in range(4) for core in range(2)]
    swap = [(place(y, x, c), place(y, x, 1 - c)) for y, x, c in sites]
    y_fore = [(place(y, x, c), place(y + 1 - 2 * c, x, c)) for y, x, c in sites]
    y_aft = [(b, a) for a, b in y_fore]
    z_fore = [
        (place(y, x, c) * 8 + z, place(y, x, c) * 8 + (z + 1 - 2 * c) % 8)
        for y, x, c in sites
        for z in range(8)
    ]
    z_aft = [(b, a) for a, b in z_fore]
    y_lines = [[place(y, x, c) for y in range(8)] for x in range(4) for c in range(2)]
    squares = [[place(y, x, c) for x in range(4) for c in range(2)] for y in range(8)]
    x_lines = [[place(y, x, c) for x in range(4)] for y in range(8) for c in range(2)]

    half = (rows, feats // 2)
    mine, theirs = call(
        split_kernel, [(half, BF), (half, BF)], [SMEM, HBM], [VMEM, VMEM], pos, tokens,
        scratch=[pltpu.SemaphoreType.DMA((feats // 256,))],
    )
    swapped = lax.ppermute(theirs, "row", swap)
    (low_part,) = call(
        low_kernel, [((16, feats // 2), BF)], [VMEM, VMEM], [VMEM], tokens, down_proj.T
    )
    pair = jnp.concatenate([mine, swapped, low_part], axis=0)

    w_both = jnp.concatenate([w_key, w_value], axis=1)
    wide = w_both.shape[1]
    w_line = lax.all_to_all(
        jnp.broadcast_to(w_both, (4,) + w_both.shape), "row", 0, 0, axis_index_groups=x_lines
    )
    w_own = w_line.reshape(feats // 2, wide)
    w_own = jnp.pad(w_own, ((0, pair.size // wide - w_own.shape[0]), (0, 0)))
    t_parts, w_parts = rings_of(
        (pair, w_own), (("row", "col"), "row"), (z_fore, y_fore), (z_aft, y_aft),
    )

    deep = feats // 2
    total, low_sum, t_left, w_left = call(
        project_kernel,
        [((2 * rows, wide), F32), ((16, deep), F32), ((2, 2 * rows, deep), BF), ((deep, wide), BF)],
        [SMEM] + [VMEM] * 7 + [HBM] * 6,
        [VMEM] * 4,
        pos, *t_parts[:7], *w_parts[:3], *w_parts[4:7],
        scratch=[
            pltpu.VMEM((8,) + w_own.shape, BF),
            pltpu.SemaphoreType.DMA((6,)),
        ],
        mib=40,
        cost=(2 * 16 * rows * deep * wide, 14 * (pair.size + w_own.size)),
    )
    own, other, low_half = call(
        finish_kernel,
        [((rows, wide), F32), ((rows, wide), F32), ((rows, 64), BF)],
        [SMEM] + [HBM] * 7,
        [VMEM] * 3,
        pos, t_parts[7], w_parts[7], w_parts[3], total, low_sum, t_left, w_left,
        scratch=[
            pltpu.VMEM(pair.shape, BF),
            pltpu.VMEM(w_own.shape, BF),
            pltpu.VMEM(w_own.shape, BF),
            pltpu.VMEM(total.shape, F32),
            pltpu.VMEM(low_sum.shape, F32),
            pltpu.VMEM(t_left.shape, BF),
            pltpu.VMEM(w_left.shape, BF),
            pltpu.SemaphoreType.DMA((7,)),
        ],
        mib=16,
    )
    got = lax.ppermute(other, "row", swap)
    pack, gk, gv = call(
        attend_kernel,
        [((8, 80, 128), BF), ((rows, HD), F32), ((rows, HD), F32)],
        [SMEM] + [VMEM] * 5 + [HBM] * 2,
        [VMEM] * 3,
        lengths, own, got, low_half, up_key, up_value, queries, probes,
        scratch=[
            pltpu.VMEM((rows, feats), BF),
            pltpu.VMEM((rows, feats), BF),
            pltpu.SemaphoreType.DMA((8,)),
        ],
    )
    packs = lax.all_to_all(pack, "col", 0, 0)
    slot = (8, 64 + 8, 2 * HD)
    (terms,) = call(
        weigh_kernel, [(slot, BF)], [SMEM] + [VMEM] * 5, [VMEM],
        lengths, packs, low_half, gk, gv, tokens,
    )
    term_parts = lax.all_to_all(terms, "row", 0, 0, axis_index_groups=squares)
    (square,) = call(sum_kernel, [(slot, BF)], [VMEM], [VMEM], term_parts)
    square_parts = lax.all_to_all(square, "row", 0, 0, axis_index_groups=y_lines)
    (summed,) = call(sum_kernel, [(slot, BF)], [VMEM], [VMEM], square_parts)
    pieces = lax.all_to_all(summed, "row", 0, 0, axis_index_groups=squares)
    grad_down, grad_up_key, grad_up_value = call(
        place_kernel,
        [((64, feats), F32), ((64, HD), F32), ((64, HD), F32)],
        [VMEM], [VMEM] * 3, pieces,
    )
    return grad_down.T, grad_up_key, grad_up_value


def solution(mesh):
    in_specs = (
        P("row", "col"),
        P("row", "col"),
        P("row", "col"),
        P("row", "col"),
        P("row", "col"),
        P("col", None),
        P(None, "col"),
        P(None, "col"),
        P("row", None),
    )
    out_specs = (P("col", None), P(None, "col"), P(None, "col"))
    return jax.shard_map(
        on_device, mesh=mesh, in_specs=in_specs, out_specs=out_specs, check_vma=False
    )
```

```python
import functools
import jax
import jax.numpy as jnp
from jax import lax
from jax.experimental import pallas as pl
from jax.experimental.pallas import tpu as pltpu
from jax.sharding import PartitionSpec as P

HD = 128
QPK = 16
BF = jnp.bfloat16
F32 = jnp.float32
npo_beta = 0.5
LOG2E = 1.4426950408889634

VMEM = pl.BlockSpec(memory_space=pltpu.VMEM)
SMEM = pl.BlockSpec(memory_space=pltpu.SMEM)
HBM = pl.BlockSpec(memory_space=pltpu.HBM)

NT = (((1,), (1,)), ((), ()))
TN = (((0,), (0,)), ((), ()))
NN = (((1,), (0,)), ((), ()))


def mm(a, b, dims):
    return lax.dot_general(a, b, dims, preferred_element_type=F32)


def fold(a, rows):
    return jnp.concatenate([a[i:i + rows] for i in range(0, a.shape[0], rows)], axis=1)


def unfold(a, wide):
    return jnp.concatenate([a[:, i:i + wide] for i in range(0, a.shape[1], wide)], axis=0)


def doc_ids(lengths_ref, axis, count, docs):
    places = lax.broadcasted_iota(jnp.int32, (count, count), axis)
    ids = jnp.zeros((count, count), jnp.int32)
    end = 0
    for j in range(docs):
        end = end + lengths_ref[0, j]
        ids = ids + jnp.where(places >= end, 1, 0)
    return ids


def split_kernel(pos_ref, t_ref, mine_ref, theirs_ref, sem):
    copies = []
    for i in range(t_ref.shape[1] // 512):
        to = pl.ds(i * 256, 256)
        for k, ref in enumerate((mine_ref, theirs_ref)):
            core = lax.rem(pos_ref[0] + k, 2)
            at = pl.ds(pl.multiple_of(i * 512 + core * 256, 256), 256)
            copies.append(pltpu.make_async_copy(t_ref.at[:, at], ref.at[:, to], sem.at[2 * i + k]))
    for c in copies:
        c.start()
    for c in copies:
        c.wait()


def low_kernel(t_ref, down_ref, out_ref):
    low = mm(t_ref[...], down_ref[...], NT)
    rows, wide = out_ref.shape
    low = fold(low, rows // 2)
    high = low.astype(BF).astype(F32)
    out_ref[...] = jnp.concatenate([high, low - high], axis=0).astype(BF)


STEPS = (0, 1, 2, 3, -1, -2, -3, 4)


def rings_of(owns, axes, fores, afts):
    both = range(2)
    going = [list(owns), list(owns)]
    blocks = [[[own] for own in owns] for _ in going]
    for step in range(3):
        for side, ways in enumerate((fores, afts)):
            now = going[side]
            if step == 0 and side == 1:
                now = lax.optimization_barrier(tuple(now))
            going[side] = [lax.ppermute(now[i], axes[i], ways[i]) for i in both]
            for i in both:
                blocks[side][i].append(going[side][i])
    far = [lax.ppermute(going[i][i], axes[i], (fores, afts)[i][i]) for i in both]
    return [blocks[0][i] + blocks[1][i][1:] + [far[i]] for i in both]


def block_at(pos_ref, axis, step, n):
    return lax.rem(pos_ref[1 + axis] + step * (2 * pos_ref[0] - 1) + n, n)


def project_kernel(pos_ref, *refs):
    t_refs, w_refs, refs = refs[:7], refs[7:14], refs[14:]
    total_ref, low_ref, t_left_ref, w_left_ref, w_scr, sem = refs
    n = w_scr.shape[0]
    copies = [
        pltpu.make_async_copy(part, w_scr.at[block_at(pos_ref, 1, STEPS[j], n)], sem.at[j])
        for j, part in enumerate(w_refs)
    ]
    for c in copies:
        c.start()
    t_far, w_far = (block_at(pos_ref, axis, STEPS[7], n) for axis in range(2))
    w_scr[w_far] = jnp.zeros(w_scr.shape[1:], BF)
    t_left_ref[...] = jnp.zeros(t_left_ref.shape, BF)
    rows = total_ref.shape[0]
    low = jnp.zeros(low_ref.shape, F32)
    for t_ref in t_refs:
        low = low + t_ref[pl.ds(rows, low.shape[0])].astype(F32)
    low_ref[...] = low
    for c in copies:
        c.wait()
    deep = w_left_ref.shape[0]
    total = jnp.zeros(total_ref.shape, F32)
    for j, t_ref in enumerate(t_refs):
        k = block_at(pos_ref, 0, STEPS[j], n)
        total = total + mm(t_ref[pl.ds(0, rows)], w_scr[k, pl.ds(0, deep)], NN)

        @pl.when(k == w_far)
        def _():
            t_left_ref[...] = t_ref[pl.ds(0, rows)]

    total_ref[...] = total
    w_left_ref[...] = w_scr[t_far, pl.ds(0, deep)]


def finish_kernel(
    pos_ref, t_ref, w_ref, total_ref, low_ref, t_left_ref, w_left_ref,
    own_ref, other_ref, low_half_ref,
    t_scr, w_scr, total_scr, low_scr, t_left_scr, w_left_scr, sem,
):
    pairs = [
        (t_ref, t_scr),
        (w_ref, w_scr),
        (total_ref, total_scr),
        (low_ref, low_scr),
        (t_left_ref, t_left_scr),
        (w_left_ref, w_left_scr),
    ]
    copies = [pltpu.make_async_copy(a, b, sem.at[i]) for i, (a, b) in enumerate(pairs)]
    for c in copies:
        c.start()
    for c in copies:
        c.wait()
    rows = own_ref.shape[0]
    same = pos_ref[1] == pos_ref[2]
    w_late = w_scr[pl.ds(0, w_left_scr.shape[0])]
    w_match = jnp.where(same, w_late, w_left_scr[...])
    total = total_scr[...] + mm(t_scr[pl.ds(0, 2 * rows)], w_match, NN)
    total = total + mm(t_left_scr[...], w_late, NN)
    own_ref[...] = total[:rows]
    other_ref[...] = total[rows:]
    low = low_scr[...] + t_scr[pl.ds(2 * rows, low_scr.shape[0])].astype(F32)
    low = low[:low.shape[0] // 2] + low[low.shape[0] // 2:]
    low_half_ref[...] = unfold(low, low_half_ref.shape[1]).astype(BF)


def attend_kernel(
    lengths_ref, own_ref, got_ref, low_ref, upk_ref, upv_ref, q_ref, p_ref,
    pack_ref, gk_ref, gv_ref, q_scr, p_scr, sem,
):
    rows = own_ref.shape[0]
    heads = q_ref.shape[1] // HD
    batch = 4
    copies = []
    for i in range(heads // batch):
        at = pl.ds(i * batch * HD, batch * HD)
        for k, (ref, scr) in enumerate(((q_ref, q_scr), (p_ref, p_scr))):
            copies.append(pltpu.make_async_copy(ref.at[:, at], scr.at[:, at], sem.at[2 * i + k]))
    for c in copies:
        c.start()
    score_scale = HD ** (-0.5)
    probe_scale = (q_ref.shape[1] * pack_ref.shape[0]) ** (-0.5)
    low_half = low_ref[...]
    full = own_ref[...] + got_ref[...]
    key_full, value_full = full[:, :HD], full[:, HD:]
    key_pol = (key_full + mm(low_half, upk_ref[...], NN)).astype(BF)
    value_pol = (value_full + mm(low_half, upv_ref[...], NN)).astype(BF)
    keys = jnp.concatenate([key_pol, key_full.astype(BF)], axis=0)
    values = jnp.concatenate([value_pol, value_full.astype(BF)], axis=0)
    doc_s = doc_ids(lengths_ref, 0, rows, lengths_ref.shape[1])
    doc_t = doc_ids(lengths_ref, 1, rows, lengths_ref.shape[1])
    s_at = lax.broadcasted_iota(jnp.int32, (rows, rows), 0)
    t_at = lax.broadcasted_iota(jnp.int32, (rows, rows), 1)
    allowed = (doc_s == doc_t) & (t_at >= s_at)
    banned = jnp.where(allowed, 0.0, -1e30)
    banned = jnp.concatenate([banned, banned], axis=1)

    def raised(scores):
        scores = jnp.where(banned < 0.0, -1e30, scores)
        peak = jnp.max(scores, axis=0, keepdims=True)
        e = jnp.exp2((scores - peak) * (score_scale * LOG2E))
        return e, 1.0 / jnp.sum(e, axis=0, keepdims=True)

    gk = jnp.zeros((rows, HD), F32)
    gv = jnp.zeros((rows, HD), F32)
    gap = jnp.zeros((1, 2 * rows), F32)
    for h in range(0, heads, 2):
        if h % batch == 0:
            for c in copies[2 * h // batch:2 * h // batch + 2]:
                c.wait()
        q, probe = (
            jnp.concatenate([scr[:, pl.ds((h + i) * HD, HD)] for i in range(2)], axis=0)
            for scr in (q_scr, p_scr)
        )
        scores = mm(keys, q, NT)
        grads = mm(values, probe, NT)
        pol, share = raised(scores[:rows])
        pol = pol * share
        ref, share = raised(scores[rows:])
        grad_pol = grads[:rows]
        mean_pol = jnp.sum(pol * grad_pol, axis=0, keepdims=True)
        mean_ref = jnp.sum(ref * grads[rows:], axis=0, keepdims=True) * share
        gap = gap + (mean_pol - mean_ref)
        grad_scores = (pol * (grad_pol - mean_pol)).astype(BF)
        gk = gk + mm(grad_scores, q, NN)
        gv = gv + mm(pol.astype(BF), probe, NN)
    gap = gap[:, :rows] + gap[:, rows:]
    gk = gk * (score_scale * probe_scale)
    gv = gv * probe_scale
    gap = gap * probe_scale
    gk_ref[...] = gk
    gv_ref[...] = gv
    back = mm(gk.astype(BF), upk_ref[...], NT) + mm(gv.astype(BF), upv_ref[...], NT)
    back = fold(back, 64).astype(BF)
    first = gap.astype(BF).astype(F32)
    second = (gap - first).astype(BF).astype(F32)
    third = gap - first - second
    line = lax.broadcasted_iota(jnp.int32, (8, rows), 0)
    tail = jnp.where(line == 0, first, jnp.where(line == 1, second, jnp.where(line == 2, third, 0.0)))
    tail = tail.astype(BF)
    for i in range(pack_ref.shape[0]):
        pack_ref[i, pl.ds(0, 64)] = back
        pack_ref[i, pl.ds(64, 8)] = tail


def weigh_kernel(lengths_ref, pack_ref, low_half_ref, gk_ref, gv_ref, t_ref, out_ref):
    rows = gk_ref.shape[0]
    total = pack_ref[0].astype(F32)
    for i in range(1, pack_ref.shape[0]):
        total = total + pack_ref[i].astype(F32)
    gap = total[64:65] + total[65:66] + total[66:67]
    docs = lengths_ref.shape[1]
    same = doc_ids(lengths_ref, 0, rows, docs) == doc_ids(lengths_ref, 1, rows, docs)
    token_gap = jnp.sum(jnp.where(same, gap, 0.0), axis=1, keepdims=True)
    weight = 2.0 * jax.nn.sigmoid(npo_beta * token_gap)
    back_half = (unfold(total[:64], 64) * weight).astype(BF)
    down = mm(back_half, t_ref[...], TN).astype(BF)
    both = jnp.concatenate([gk_ref[...] * weight, gv_ref[...] * weight], axis=1).astype(BF)
    up = mm(low_half_ref[...], both, TN).astype(BF)
    slots = out_ref.shape[0]
    wide, deep = t_ref.shape[1] // slots, up.shape[0] // slots
    for j in range(slots):
        out_ref[j, pl.ds(0, 64)] = down[:, j * wide:(j + 1) * wide]
        out_ref[j, pl.ds(64, deep)] = up[j * deep:(j + 1) * deep]


def sum_kernel(in_ref, out_ref):
    total = in_ref[0].astype(F32)
    for i in range(1, in_ref.shape[0]):
        total = total + in_ref[i].astype(F32)
    total = total.astype(BF)
    for i in range(out_ref.shape[0]):
        out_ref[i] = total


def place_kernel(in_ref, down_ref, upk_ref, upv_ref):
    slots, _, wide = in_ref.shape
    deep = upk_ref.shape[0] // slots
    for j in range(slots):
        down_ref[:, pl.ds(j * wide, wide)] = in_ref[j, pl.ds(0, 64)].astype(F32)
        up = in_ref[j, pl.ds(64, deep)].astype(F32)
        upk_ref[pl.ds(j * deep, deep)] = up[:, :HD]
        upv_ref[pl.ds(j * deep, deep)] = up[:, HD:]


def call(kernel, outs, in_specs, out_specs, *args, scratch=(), mib=8, cost=None):
    return pl.pallas_call(
        kernel,
        out_shape=[jax.ShapeDtypeStruct(s, d) for s, d in outs],
        in_specs=in_specs,
        out_specs=out_specs,
        scratch_shapes=list(scratch),
        cost_estimate=cost and pl.CostEstimate(
            flops=cost[0], bytes_accessed=cost[1], transcendentals=0
        ),
        compiler_params=pltpu.CompilerParams(vmem_limit_bytes=mib * 1024 * 1024),
    )(*args)


def on_device(tokens, queries, probes, w_key, w_value, down_proj, up_key, up_value, lengths):
    rows, feats = tokens.shape
    row_at = lax.axis_index("row")
    pos = jnp.stack([row_at % 2, lax.axis_index("col"), row_at // 8]).astype(jnp.int32)

    def place(y, x, core):
        return ((y % 8) * 4 + x % 4) * 2 + core % 2

    sites = [(y, x, core) for y in range(8) for x in range(4) for core in range(2)]
    swap = [(place(y, x, c), place(y, x, 1 - c)) for y, x, c in sites]
    y_fore = [(place(y, x, c), place(y + 1 - 2 * c, x, c)) for y, x, c in sites]
    y_aft = [(b, a) for a, b in y_fore]
    z_fore = [
        (place(y, x, c) * 8 + z, place(y, x, c) * 8 + (z + 1 - 2 * c) % 8)
        for y, x, c in sites
        for z in range(8)
    ]
    z_aft = [(b, a) for a, b in z_fore]
    y_lines = [[place(y, x, c) for y in range(8)] for x in range(4) for c in range(2)]
    squares = [[place(y, x, c) for x in range(4) for c in range(2)] for y in range(8)]
    x_lines = [[place(y, x, c) for x in range(4)] for y in range(8) for c in range(2)]

    half = (rows, feats // 2)
    mine, theirs = call(
        split_kernel, [(half, BF), (half, BF)], [SMEM, HBM], [VMEM, VMEM], pos, tokens,
        scratch=[pltpu.SemaphoreType.DMA((feats // 256,))],
    )
    swapped = lax.ppermute(theirs, "row", swap)
    (low_part,) = call(
        low_kernel, [((16, feats // 2), BF)], [VMEM, VMEM], [VMEM], tokens, down_proj.T
    )
    pair = jnp.concatenate([mine, swapped, low_part], axis=0)

    w_both = jnp.concatenate([w_key, w_value], axis=1)
    wide = w_both.shape[1]
    w_line = lax.all_to_all(
        jnp.broadcast_to(w_both, (4,) + w_both.shape), "row", 0, 0, axis_index_groups=x_lines
    )
    w_own = w_line.reshape(feats // 2, wide)
    w_own = jnp.pad(w_own, ((0, pair.size // wide - w_own.shape[0]), (0, 0)))
    t_parts, w_parts = rings_of(
        (pair, w_own), (("row", "col"), "row"), (z_fore, y_fore), (z_aft, y_aft),
    )

    deep = feats // 2
    total, low_sum, t_left, w_left = call(
        project_kernel,
        [((2 * rows, wide), F32), ((16, deep), F32), ((2 * rows, deep), BF), ((deep, wide), BF)],
        [SMEM] + [VMEM] * 7 + [HBM] * 7,
        [VMEM] * 4,
        pos, *t_parts[:7], *w_parts[:7],
        scratch=[
            pltpu.VMEM((8,) + w_own.shape, BF),
            pltpu.SemaphoreType.DMA((7,)),
        ],
        mib=40,
        cost=(2 * 16 * rows * deep * wide, 14 * (pair.size + w_own.size)),
    )
    own, other, low_half = call(
        finish_kernel,
        [((rows, wide), F32), ((rows, wide), F32), ((rows, 64), BF)],
        [SMEM] + [HBM] * 6,
        [VMEM] * 3,
        pos, t_parts[7], w_parts[7], total, low_sum, t_left, w_left,
        scratch=[
            pltpu.VMEM(pair.shape, BF),
            pltpu.VMEM(w_own.shape, BF),
            pltpu.VMEM(total.shape, F32),
            pltpu.VMEM(low_sum.shape, F32),
            pltpu.VMEM(t_left.shape, BF),
            pltpu.VMEM(w_left.shape, BF),
            pltpu.SemaphoreType.DMA((6,)),
        ],
        mib=16,
    )
    got = lax.ppermute(other, "row", swap)
    pack, gk, gv = call(
        attend_kernel,
        [((8, 72, 128), BF), ((rows, HD), F32), ((rows, HD), F32)],
        [SMEM] + [VMEM] * 5 + [HBM] * 2,
        [VMEM] * 3,
        lengths, own, got, low_half, up_key, up_value, queries, probes,
        scratch=[
            pltpu.VMEM((rows, feats), BF),
            pltpu.VMEM((rows, feats), BF),
            pltpu.SemaphoreType.DMA((8,)),
        ],
    )
    packs = lax.all_to_all(pack, "col", 0, 0)
    slot = (8, 64 + 8, 2 * HD)
    (terms,) = call(
        weigh_kernel, [(slot, BF)], [SMEM] + [VMEM] * 5, [VMEM],
        lengths, packs, low_half, gk, gv, tokens,
    )
    term_parts = lax.all_to_all(terms, "row", 0, 0, axis_index_groups=squares)
    (square,) = call(sum_kernel, [(slot, BF)], [VMEM], [VMEM], term_parts)
    square_parts = lax.all_to_all(square, "row", 0, 0, axis_index_groups=y_lines)
    (summed,) = call(sum_kernel, [(slot, BF)], [VMEM], [VMEM], square_parts)
    pieces = lax.all_to_all(summed, "row", 0, 0, axis_index_groups=squares)
    grad_down, grad_up_key, grad_up_value = call(
        place_kernel,
        [((64, feats), F32), ((64, HD), F32), ((64, HD), F32)],
        [VMEM], [VMEM] * 3, pieces,
    )
    return grad_down.T, grad_up_key, grad_up_value


def solution(mesh):
    in_specs = (
        P("row", "col"),
        P("row", "col"),
        P("row", "col"),
        P("row", "col"),
        P("row", "col"),
        P("col", None),
        P(None, "col"),
        P(None, "col"),
        P("row", None),
    )
    out_specs = (P("col", None), P(None, "col"), P(None, "col"))
    return jax.shard_map(
        on_device, mesh=mesh, in_specs=in_specs, out_specs=out_specs, check_vma=False
    )
```
